128 devices in a mesh: row: 4 (over z), col: 32 (over y, x, core).
Axes of the slice: x: 4, y: 4, z: 4, core: 2. Of those that a mesh axis runs over, the one named last changes fastest.
Arguments:
- features: bfloat16 [524288, 128], P(('row', 'col')), may hold values from -6 to 6
- neighbors: int32 [524288, 10], P(('row', 'col')), may hold values from 0 to 10239, as said below
- counts: int32 [524288], P(('row', 'col')), may hold values from 1 to 10
- hub_rows: int32 [16384], P(('row', 'col')), may hold values from 0 to 4095, as said below
- w_self: bfloat16 [128, 256], replicated, may hold values from -0.5 to 0.5
- w_neigh: bfloat16 [128, 256], replicated, may hold values from -0.5 to 0.5
- out_bias: float32 [256], replicated, may hold values from -3 to 3
- cotangent: bfloat16 [524288, 256], P(('row', 'col')), may hold values from -6 to 6
Outputs:
- activations: bfloat16 [524288, 256], P(('row', 'col'))
- grad_features: bfloat16 [524288, 128], P(('row', 'col'))
- grad_w_self: float32 [128, 256], replicated
- grad_w_neigh: float32 [128, 256], replicated
- grad_bias: float32 [256], replicated
The draws below stay inside these ranges and needn't reach their ends.
Inputs may be any that keep to these rules, and one draw needn't show every extreme that they name: `neighbors`: rows below 1024 are never used by a partition of row 0, rows 5120 to 6143 never by one of the last row; slots at or past a node's count hold valid rows and are ignored. `hub_rows`: the 128 rows of one partition are distinct.
All inputs are finite; a program needn't handle non-finite values.
Results may differ from the reference program's by a relative error of at most 0.0075.
Values may be sent and summed in bfloat16 or wider, within the bound.
No kernel may reach another device: no remote copies, remote signals or barrier semaphores. Data moves between devices by JAX's collectives and lax.ppermute only.
A program may use at most 256 MiB of HBM per device.

```python
import jax
import jax.numpy as jnp
from jax import lax

F = 128
H = 256
NODE_DEV = 4096
HUB_DEV = 128
FANOUT = 10
HALO = 1024
NODES = 524288
N_ROW = 4
N_COL = 32
DEVICES = 128


def draw_neighbors(key, part):
    key = jax.random.fold_in(key, 11)
    keys = jax.random.split(key, 5)
    total = NODE_DEV * DEVICES
    shape = (total, FANOUT)
    hub_count = HUB_DEV * N_COL
    extent = 2 * HALO + NODE_DEV + hub_count
    node = jnp.arange(total, dtype=jnp.int32)
    local_pos = node % NODE_DEV
    row_of = (node // NODE_DEV // N_COL)[:, None]
    category = jax.random.randint(keys[0], shape, 0, 20)
    inside = HALO + jax.random.randint(keys[1], shape, 0, NODE_DEV)
    border = jax.random.randint(keys[2], shape, 0, 2 * HALO)
    border = jnp.where((row_of == 0) & (border < HALO), border + HALO, border)
    border = jnp.where((row_of == N_ROW - 1) & (border >= HALO), border - HALO, border)
    border = jnp.where(border < HALO, border, border + NODE_DEV)
    first_hub = jax.random.randint(keys[3], shape, 0, hub_count)
    second_hub = jax.random.randint(keys[4], shape, 0, hub_count)
    hubward = 2 * HALO + NODE_DEV + jnp.minimum(first_hub, second_hub)
    picked = jnp.where(category < 14, inside, jnp.where(category < 17, border, hubward))
    leading = picked[:, 0]
    leading = jnp.where(local_pos == 0, extent - 1, jnp.where(local_pos == 1, HALO, jnp.where((local_pos == 2) & (row_of[:, 0] > 0), 0, leading)))
    return picked.at[:, 0].set(leading).astype(jnp.int32)


def draw_counts(key, part):
    key = jax.random.fold_in(key, 12)
    total = NODE_DEV * DEVICES
    node = jnp.arange(total, dtype=jnp.int32)
    drawn = jax.random.randint(key, (total,), 1, FANOUT + 1)
    drawn = jnp.where(node % 128 == 0, FANOUT, jnp.where(node % 128 == 1, 1, drawn))
    return drawn.astype(jnp.int32)


def draw_hub_rows(key, part):
    key = jax.random.fold_in(key, 13)
    total = DEVICES * HUB_DEV
    stride = NODE_DEV // HUB_DEV
    position = jnp.arange(total, dtype=jnp.int32) % HUB_DEV
    offsets = jax.random.randint(key, (total,), 0, stride)
    picked = position * stride + offsets
    picked = picked.at[0].set(0).at[HUB_DEV - 1].set(NODE_DEV - 1)
    return picked.astype(jnp.int32)


def block_levels(own_key, shape, cuts, least, largest):
    gain = 1.0
    for dim, shards_of in cuts:
        steps = jax.random.uniform(jax.random.fold_in(jax.random.fold_in(own_key, 6), dim), (shards_of,), jnp.float32, least / len(cuts), largest / len(cuts))
        gain = gain * jnp.repeat(jnp.exp(steps), shape[dim] // shards_of).reshape((-1,) + (1,) * (len(shape) - 1 - dim))
    return gain


def centred(own_key, shape, scale, bound, pieces=(), kind=jnp.bfloat16):
    values = jax.random.normal(own_key, shape, jnp.float32) * scale
    if len(pieces) > 0:
        values = block_levels(own_key, shape, pieces, -0.22, 0.18) * values
    return jnp.clip(values, min=-bound, max=bound).astype(kind)


def setup_inputs(seed: int = 0) -> dict:
    key_of = jax.random.split(jax.random.key(seed), 9)
    return {
        "features": centred(key_of[0], (NODES, F), 1.0, 6.0, ((0, 128),)),
        "neighbors": draw_neighbors(jax.random.fold_in(key_of[8], 71), 0),
        "counts": draw_counts(jax.random.fold_in(key_of[8], 71), 0),
        "hub_rows": draw_hub_rows(jax.random.fold_in(key_of[8], 71), 0),
        "w_self": centred(key_of[4], (F, H), F ** -0.5, 0.5),
        "w_neigh": centred(key_of[5], (F, H), F ** -0.5, 0.5),
        "out_bias": centred(key_of[6], (H,), 0.5, 3.0, (), jnp.float32),
        "cotangent": centred(key_of[7], (NODES, H), 1.0, 6.0, ((0, 128),)),
    }


def gelu_tanh(value):
    return jax.nn.gelu(value, approximate=True)

def reference(features, neighbors, counts, hub_rows, w_self, w_neigh, out_bias, cotangent):
    node_count = NODE_DEV
    extent = 2 * HALO + node_count + HUB_DEV * N_COL
    cube = features.reshape(N_ROW, N_COL, node_count, F)
    hub_index = hub_rows.reshape(N_ROW, N_COL, HUB_DEV)
    hub_table = jax.vmap(jax.vmap(lambda block, picks: jnp.take(block, picks, axis=0)))(cube, hub_index)
    hub_table = hub_table.reshape(N_ROW, N_COL * HUB_DEV, F)
    slot_ids = neighbors.reshape(DEVICES, node_count, FANOUT)
    live_counts = counts.reshape(DEVICES, node_count)
    cot_parts = cotangent.reshape(DEVICES, node_count, H)
    zero_rim = jnp.zeros((HALO, F), jnp.bfloat16)

    def per_partition(carry, inputs):
        index_part, slots, count_part, cot_part = inputs
        row_pos = index_part // N_COL
        col_pos = index_part % N_COL
        mine = cube[row_pos, col_pos]
        lower = jnp.where(row_pos > 0, cube[jnp.maximum(row_pos - 1, 0), col_pos, node_count - HALO:], zero_rim)
        upper = jnp.where(row_pos < N_ROW - 1, cube[jnp.minimum(row_pos + 1, N_ROW - 1), col_pos, :HALO], zero_rim)
        table = jnp.concatenate([lower, mine, upper, hub_table[row_pos]], axis=0)
        active = jnp.arange(FANOUT)[None, :] < count_part[:, None]
        divisor = count_part.astype(jnp.float32)[:, None]
        picked = table[slots].astype(jnp.float32)
        agg = (lax.optimization_barrier(jnp.sum(jnp.where(active[:, :, None], picked, 0.0), axis=1)) / divisor).astype(jnp.bfloat16)
        pre = jnp.dot(mine, w_self, preferred_element_type=jnp.float32) + jnp.dot(agg, w_neigh, preferred_element_type=jnp.float32) + out_bias.astype(jnp.float32)
        act, backward = jax.vjp(gelu_tanh, pre)
        dz = backward(cot_part.astype(jnp.float32))[0].astype(jnp.bfloat16)
        dims = (((0,), (0,)), ((), ()))
        grad_self = carry[0] + lax.dot_general(mine, dz, dims, preferred_element_type=jnp.float32)
        grad_neigh = carry[1] + lax.dot_general(agg, dz, dims, preferred_element_type=jnp.float32)
        grad_b = carry[2] + lax.optimization_barrier(jnp.sum(dz.astype(jnp.float32), axis=0))
        back_dims = (((1,), (1,)), ((), ()))
        d_agg = lax.dot_general(dz, w_neigh, back_dims, preferred_element_type=jnp.float32) / divisor
        values = jnp.where(active[:, :, None], d_agg[:, None, :], 0.0)
        d_table = jnp.zeros((extent, F), jnp.float32).at[slots.reshape(-1)].add(values.reshape(-1, F))
        base = lax.dot_general(dz, w_self, back_dims, preferred_element_type=jnp.float32) + d_table[HALO:HALO + node_count]
        outputs = (act.astype(jnp.bfloat16), base, d_table[:HALO], d_table[HALO + node_count:2 * HALO + node_count], d_table[2 * HALO + node_count:])
        return ((grad_self, grad_neigh, grad_b), outputs)
    init = (jnp.zeros((F, H), jnp.float32), jnp.zeros((F, H), jnp.float32), jnp.zeros((H,), jnp.float32))
    part_ids = jnp.arange(DEVICES, dtype=jnp.int32)
    sums, outputs = lax.scan(per_partition, init, (part_ids, slot_ids, live_counts, cot_parts))
    acts, base, lower_grads, upper_grads, hub_grads = outputs
    base = base.reshape(N_ROW, N_COL, node_count, F)
    lower_grads = lower_grads.reshape(N_ROW, N_COL, HALO, F)
    upper_grads = upper_grads.reshape(N_ROW, N_COL, HALO, F)
    zero_row = jnp.zeros((1, N_COL, HALO, F), jnp.float32)
    from_above = jnp.concatenate([zero_row, upper_grads[:-1]], axis=0)
    from_below = jnp.concatenate([lower_grads[1:], zero_row], axis=0)
    base = base.at[:, :, :HALO].add(from_above)
    base = base.at[:, :, node_count - HALO:].add(from_below)
    hub_total = lax.optimization_barrier(jnp.sum(hub_grads.reshape(N_ROW, N_COL, N_COL, HUB_DEV, F), axis=1))
    base = jax.vmap(jax.vmap(lambda block, picks, extra: block.at[picks].add(extra)))(base, hub_index, hub_total)
    grad_features = base.reshape(DEVICES * node_count, F).astype(jnp.bfloat16)
    activations = acts.reshape(DEVICES * node_count, H)
    return (activations, grad_features, sums[0], sums[1], sums[2])
```

```python
import functools

import jax
import jax.numpy as jnp
from jax import lax
from jax.experimental import pallas as pl
from jax.experimental.pallas import tpu as pltpu
from jax.sharding import Mesh, PartitionSpec as P

F = 128
H = 256
NODES = 4096
HALO = 1024
HUB = 128
FANOUT = 10
COLS = 32
HUBS = HUB * COLS
OWN = HALO
UPPER = HALO + NODES
HUB_AT = 2 * HALO + NODES
EXTENT = HUB_AT + HUBS
LANES = 128
CHAINS = 8
VMEM_BYTES = 60 * 2**20
AXES = ("z", "y", "x", "core")

smem = pl.BlockSpec(memory_space=pltpu.SMEM)
vmem = pl.BlockSpec(memory_space=pltpu.VMEM)
params = pltpu.CompilerParams(vmem_limit_bytes=VMEM_BYTES)


def group_of(count):
    return 16 if count <= 3 else 8


def hub_kernel(hub_rows, features, out, wide, rows):
    @pl.loop(0, NODES // 512)
    def _(i):
        cut = pl.ds(i * 512, 512)
        wide[cut, :] = features[cut, :].astype(jnp.float32)

    @pl.loop(0, HUB // 16)
    def _(i):
        for u in range(16):
            rows[pl.ds(i * 16 + u, 1), :] = wide[pl.ds(hub_rows[i * 16 + u], 1), :]

    out[...] = rows[...].astype(jnp.bfloat16)


def pick_hubs(hub_rows, features):
    return pl.pallas_call(
        hub_kernel,
        out_shape=jax.ShapeDtypeStruct((HUB, F), jnp.bfloat16),
        in_specs=[smem, vmem],
        out_specs=vmem,
        scratch_shapes=[pltpu.VMEM((NODES, F), jnp.float32), pltpu.VMEM((HUB, F), jnp.float32)],
        compiler_params=params,
        name="pick_hubs",
    )(hub_rows, features)


def order_kernel(counts, perm, ends):
    rows = NODES // LANES
    count = counts[...]
    lane_r = lax.broadcasted_iota(jnp.int32, (LANES, LANES), 0)
    lane_c = lax.broadcasted_iota(jnp.int32, (LANES, LANES), 1)
    before = (lane_r < lane_c).astype(jnp.float32)
    row_r = lax.broadcasted_iota(jnp.int32, (rows, rows), 0)
    row_c = lax.broadcasted_iota(jnp.int32, (rows, rows), 1)
    above = (row_c < row_r).astype(jnp.float32)
    place = jnp.zeros((rows, LANES), jnp.float32)
    start = jnp.zeros((1, 1), jnp.float32)
    lane = lax.broadcasted_iota(jnp.int32, (1, LANES), 1)
    end_row = jnp.zeros((1, LANES), jnp.float32)
    for c in range(1, FANOUT + 1):
        hit = (count == c).astype(jnp.float32)
        in_row = jnp.dot(hit, before, preferred_element_type=jnp.float32)
        per_row = jnp.sum(hit, axis=1, keepdims=True)
        earlier = jnp.dot(
            above, jnp.broadcast_to(per_row, (rows, LANES)), preferred_element_type=jnp.float32
        )
        place = place + hit * (in_row + earlier + start)
        start = start + jnp.sum(per_row, axis=0, keepdims=True)
        end_row = end_row + jnp.where(lane == c, start, 0.0)
    ends[...] = end_row.astype(jnp.int32)
    place = place.astype(jnp.int32)
    high = place >> 7
    low = place - high * LANES
    slot_row = lax.broadcasted_iota(jnp.int32, (rows, LANES), 0)
    slot_lane = lax.broadcasted_iota(jnp.int32, (LANES, LANES), 0)
    own_lane = lax.broadcasted_iota(jnp.int32, (rows, LANES), 1).astype(jnp.float32)
    total = jnp.zeros((rows, LANES), jnp.float32)
    for r in range(rows):
        to_row = (high[r : r + 1, :] == slot_row).astype(jnp.float32)
        to_lane = (low[r : r + 1, :] == slot_lane).astype(jnp.bfloat16)
        both = jnp.concatenate([to_row * own_lane, to_row * float(r)], axis=0)
        found = lax.dot_general(
            both.astype(jnp.bfloat16),
            to_lane,
            (((1,), (1,)), ((), ())),
            preferred_element_type=jnp.float32,
        )
        total = total + found[:rows] + found[rows:] * float(LANES)
    perm[...] = total.astype(jnp.int32)


def order_nodes(counts):
    rows = NODES // LANES
    perm, ends = pl.pallas_call(
        order_kernel,
        out_shape=(
            jax.ShapeDtypeStruct((rows, LANES), jnp.int32),
            jax.ShapeDtypeStruct((1, LANES), jnp.int32),
        ),
        in_specs=[vmem],
        out_specs=(vmem, vmem),
        compiler_params=params,
        name="order_nodes",
    )(counts.reshape(rows, LANES))
    return perm.reshape(NODES), ends.reshape(LANES)


def over_nodes(ends, perm, visit):
    for count in range(1, FANOUT + 1):
        size = group_of(count)
        first = ends[count - 1]
        groups = (ends[count] - first) // size
        rest = first + groups * size

        @pl.loop(0, groups)
        def _(g, count=count, size=size, first=first):
            at = first + g * size
            visit([perm[at + u] for u in range(size)], count)

        @pl.loop(rest, ends[count])
        def _(at, count=count):
            visit([perm[at]], count)


def forward_kernel(
    ends, perm, slots, features, lower, upper, h0, h1, h2, h3, h4, h5,
    counts, w_self, w_neigh, bias, cotangent,
    act, src, base, grads, table, sums,
):
    def widen(source, at, rows):
        step = min(rows, 256)

        @pl.loop(0, rows // step)
        def _(i):
            table[pl.ds(at + i * step, step), :] = source[pl.ds(i * step, step), :].astype(
                jnp.float32
            )

    widen(features, OWN, NODES)
    widen(lower, 0, HALO)
    widen(upper, UPPER, HALO)
    y, x, core = lax.axis_index("y"), lax.axis_index("x"), lax.axis_index("core")
    position = 0
    for piece in (h0, h1, h2, h3, h4, h5):
        for i in range(piece.shape[0] // HUB):
            b = [(position >> k) & 1 for k in range(5)]
            owner_y = y ^ (b[0] * 1) ^ (b[1] * 3)
            owner_x = x ^ (b[2] * 1) ^ (b[3] * 3)
            owner = owner_y * 8 + owner_x * 2 + (core ^ b[4])
            table[pl.ds(HUB_AT + owner * HUB, HUB), :] = piece[
                i * HUB : (i + 1) * HUB, :
            ].astype(jnp.float32)
            position += 1

    def gather(nodes, count):
        for n in nodes:
            total = table[pl.ds(slots[0, n], 1), :]
            for s in range(1, count):
                total = total + table[pl.ds(slots[s, n], 1), :]
            sums[pl.ds(n, 1), :] = total

    over_nodes(ends, perm, gather)

    grads[...] = jnp.zeros_like(grads)
    contract_rows = (((0,), (0,)), ((), ()))
    contract_cols = (((1,), (1,)), ((), ()))
    block = 256

    @pl.loop(0, NODES // block)
    def _(i):
        cut = pl.ds(i * block, block)
        parts = []
        for k in range(block // LANES):
            row = counts[pl.ds(i * (block // LANES) + k, 1), :].astype(jnp.float32)
            parts.append(jnp.broadcast_to(row, (LANES, LANES)).T)
        divisor = jnp.concatenate(parts, axis=0)
        own = features[cut, :]
        agg = (sums[cut, :] / divisor).astype(jnp.bfloat16)
        z = (
            jnp.dot(own, w_self[...], preferred_element_type=jnp.float32)
            + jnp.dot(agg, w_neigh[...], preferred_element_type=jnp.float32)
            + bias[...]
        )
        scale = 0.7978845608028654
        squared = z * z
        t = jnp.tanh(scale * (z + 0.044715 * (squared * z)))
        half = 0.5 * (1.0 + t)
        act[cut, :] = (z * half).astype(jnp.bfloat16)
        slope = half + 0.5 * z * (1.0 - t * t) * (scale * (1.0 + 3 * 0.044715 * squared))
        dz_wide = cotangent[cut, :].astype(jnp.float32) * slope
        dz = dz_wide.astype(jnp.bfloat16)
        grads[0:F, :] += lax.dot_general(
            own, dz, contract_rows, preferred_element_type=jnp.float32
        )
        grads[F : 2 * F, :] += lax.dot_general(
            agg, dz, contract_rows, preferred_element_type=jnp.float32
        )
        partial = jnp.sum(
            dz.astype(jnp.float32).reshape(block // 8, 8, H), axis=0
        )
        grads[2 * F : 2 * F + 8, :] += partial
        src[cut, :] = (
            lax.dot_general(dz, w_neigh[...], contract_cols, preferred_element_type=jnp.float32)
            / divisor
        )
        base[cut, :] = lax.dot_general(
            dz, w_self[...], contract_cols, preferred_element_type=jnp.float32
        )


def forward(ends, perm, slots, features, lower, upper, hubs, counts, w_self, w_neigh, bias, cot):
    return pl.pallas_call(
        forward_kernel,
        out_shape=(
            jax.ShapeDtypeStruct((NODES, H), jnp.bfloat16),
            jax.ShapeDtypeStruct((NODES, F), jnp.float32),
            jax.ShapeDtypeStruct((NODES, F), jnp.float32),
            jax.ShapeDtypeStruct((2 * F + 16, H), jnp.float32),
        ),
        in_specs=[smem] * 3 + [vmem] * (3 + len(hubs) + 5),
        out_specs=(vmem,) * 4,
        scratch_shapes=[
            pltpu.VMEM((EXTENT, F), jnp.float32),
            pltpu.VMEM((NODES, F), jnp.float32),
        ],
        compiler_params=params,
        name="forward",
    )(ends, perm, slots, features, lower, upper, *hubs, counts, w_self, w_neigh, bias, cot)


def scatter_kernel(ends, perm, slots, src, base, lower, upper, hub, own, *chains):
    for k, chain in enumerate(chains):
        if k == 0:
            parts = ((0, HALO), (UPPER, EXTENT - UPPER))
            step = 512

            @pl.loop(0, NODES // step)
            def _(i):
                chains[0][pl.ds(OWN + i * step, step), :] = base[pl.ds(i * step, step), :]
        else:
            parts = ((0, EXTENT),)
        for at, rows in parts:
            step = 512

            @pl.loop(0, rows // step)
            def _(i, chain=chain, at=at):
                chain[pl.ds(at + i * step, step), :] = jnp.zeros((step, F), jnp.float32)

    turn = [0]

    def scatter(nodes, count):
        turn[0] = 0
        for n in nodes:
            row = src[pl.ds(n, 1), :]
            for s in range(count):
                chain = chains[turn[0] % CHAINS]
                turn[0] += 1
                at = pl.ds(slots[s, n], 1)
                chain[at, :] = chain[at, :] + row

    over_nodes(ends, perm, scatter)

    def total(cut):
        out = chains[0][cut, :]
        for chain in chains[1:]:
            out = out + chain[cut, :]
        return out

    @pl.loop(0, HALO // HUB)
    def _(i):
        lower[pl.ds(i * HUB, HUB), :] = total(pl.ds(i * HUB, HUB)).astype(jnp.bfloat16)
        upper[pl.ds(i * HUB, HUB), :] = total(pl.ds(UPPER + i * HUB, HUB)).astype(jnp.bfloat16)

    @pl.loop(0, COLS)
    def _(owner):
        y, x, core = owner // 8, (owner // 2) % 4, owner % 2
        at = (core * 16 + x * 4 + y) * HUB
        hub[pl.ds(at, HUB), :] = total(pl.ds(HUB_AT + owner * HUB, HUB)).astype(jnp.bfloat16)

    @pl.loop(0, NODES // HUB)
    def _(i):
        own[pl.ds(i * HUB, HUB), :] = total(pl.ds(OWN + i * HUB, HUB))


def scatter(ends, perm, slots, src, base):
    return pl.pallas_call(
        scatter_kernel,
        out_shape=(
            jax.ShapeDtypeStruct((HALO, F), jnp.bfloat16),
            jax.ShapeDtypeStruct((HALO, F), jnp.bfloat16),
            jax.ShapeDtypeStruct((HUBS, F), jnp.bfloat16),
            jax.ShapeDtypeStruct((NODES, F), jnp.float32),
        ),
        in_specs=[smem] * 3 + [vmem] * 2,
        out_specs=(vmem,) * 4,
        scratch_shapes=[pltpu.VMEM((EXTENT, F), jnp.float32)] * CHAINS,
        compiler_params=params,
        name="scatter",
    )(ends, perm, slots, src, base)


def finish_kernel(hub_rows, own, from_above, from_below, share, out, total):
    step = 256

    @pl.loop(0, NODES // step)
    def _(i):
        cut = pl.ds(i * step, step)
        total[cut, :] = own[cut, :]

    @pl.loop(0, HALO // step)
    def _(i):
        cut = pl.ds(i * step, step)
        total[cut, :] = total[cut, :] + from_above[cut, :].astype(jnp.float32)

    @pl.loop(0, HALO // step)
    def _(i):
        cut = pl.ds(NODES - HALO + i * step, step)
        total[cut, :] = total[cut, :] + from_below[pl.ds(i * step, step), :].astype(jnp.float32)

    @pl.loop(0, HUB // 8)
    def _(i):
        for u in range(8):
            at = pl.ds(hub_rows[i * 8 + u], 1)
            total[at, :] = total[at, :] + share[pl.ds(i * 8 + u, 1), :]

    @pl.loop(0, NODES // step)
    def _(i):
        cut = pl.ds(i * step, step)
        out[cut, :] = total[cut, :].astype(jnp.bfloat16)


def finish(hub_rows, own, from_above, from_below, share):
    return pl.pallas_call(
        finish_kernel,
        out_shape=jax.ShapeDtypeStruct((NODES, F), jnp.bfloat16),
        in_specs=[smem] + [vmem] * 4,
        out_specs=vmem,
        scratch_shapes=[pltpu.VMEM((NODES, F), jnp.float32)],
        compiler_params=params,
        name="finish",
    )(hub_rows, own, from_above, from_below, share)


def swap(value, axis, flip):
    count = lax.axis_size(axis)
    return lax.ppermute(value, axis, [(i, i ^ flip) for i in range(count)])


def shifted(value, axis, by):
    count = lax.axis_size(axis)
    pairs = [(i, i + by) for i in range(count) if 0 <= i + by < count]
    return lax.ppermute(value, axis, pairs)


def gather_hubs(mine):
    pieces = [mine]
    held = mine
    steps = (("y", 1), ("y", 3), ("x", 1), ("x", 3), ("core", 1))
    for k, (axis, flip) in enumerate(steps):
        other = swap(held, axis, flip)
        pieces.append(other)
        if k < len(steps) - 1:
            held = jnp.concatenate([held, other], axis=0)
    return pieces


def halve(value, axis, flip, bit):
    rows = value.shape[0] // 2
    keep = lax.dynamic_slice_in_dim(value, bit * rows, rows, axis=0)
    give = lax.dynamic_slice_in_dim(value, (1 - bit) * rows, rows, axis=0)
    got = swap(give.astype(jnp.bfloat16), axis, flip)
    return keep.astype(jnp.float32) + got.astype(jnp.float32)


def reduce_hubs(hub):
    x, y, core = lax.axis_index("x"), lax.axis_index("y"), lax.axis_index("core")
    value = halve(hub, "core", 1, core)
    value = halve(value, "x", 3, x // 2)
    value = halve(value, "x", 1, x % 2)
    value = halve(value, "y", 3, y // 2)
    return halve(value, "y", 1, y % 2)


def reduce_everywhere(grads):
    core = lax.axis_index("core")
    rows = grads.shape[0] // 2
    keep = lax.dynamic_slice_in_dim(grads, core * rows, rows, axis=0)
    give = lax.dynamic_slice_in_dim(grads, (1 - core) * rows, rows, axis=0)
    value = keep + swap(give, "core", 1)
    for axis in ("z", "x", "y"):
        for flip in (1, 3):
            value = value + swap(value, axis, flip)
    other = swap(value, "core", 1)
    first = jnp.where(core == 0, value, other)
    second = jnp.where(core == 0, other, value)
    return jnp.concatenate([first, second], axis=0)


def on_device(features, neighbors, counts, hub_rows, w_self, w_neigh, out_bias, cotangent):
    hubs = gather_hubs(pick_hubs(hub_rows, features))
    lower = shifted(features[NODES - HALO :], "z", 1)
    upper = shifted(features[:HALO], "z", -1)
    perm, ends = order_nodes(counts)
    slots = neighbors.T
    act, src, base, grads = forward(
        ends, perm, slots, features, lower, upper, hubs,
        counts.reshape(NODES // LANES, LANES), w_self, w_neigh,
        out_bias.reshape(1, H), cotangent,
    )
    to_above, to_below, hub, own = scatter(ends, perm, slots, src, base)
    from_below = shifted(to_above, "z", -1)
    from_above = shifted(to_below, "z", 1)
    share = reduce_hubs(hub)
    grads = reduce_everywhere(grads)
    grad_features = finish(hub_rows, own, from_above, from_below, share)
    grad_bias = jnp.sum(grads[2 * F :], axis=0)
    return act, grad_features, grads[:F], grads[F : 2 * F], grad_bias


def solution(mesh):
    mesh = Mesh(mesh.devices.reshape(4, 4, 4, 2), AXES)
    rows = P(AXES, None)
    placed = (rows, rows, P(AXES), P(AXES), P(), P(), P(), rows)
    return jax.shard_map(
        on_device,
        mesh=mesh,
        in_specs=placed,
        out_specs=(rows, rows, P(), P(), P()),
        check_vma=False,
    )
```

```python
import functools

import jax
import jax.numpy as jnp
from jax import lax
from jax.experimental import pallas as pl
from jax.experimental.pallas import tpu as pltpu
from jax.sharding import Mesh, PartitionSpec as P

F = 128
H = 256
NODES = 4096
HALO = 1024
HUB = 128
FANOUT = 10
COLS = 32
HUBS = HUB * COLS
OWN = HALO
UPPER = HALO + NODES
HUB_AT = 2 * HALO + NODES
EXTENT = HUB_AT + HUBS
LANES = 128
CHAINS = 8
VMEM_BYTES = 60 * 2**20
AXES = ("z", "y", "x", "core")

smem = pl.BlockSpec(memory_space=pltpu.SMEM)
vmem = pl.BlockSpec(memory_space=pltpu.VMEM)
params = pltpu.CompilerParams(vmem_limit_bytes=VMEM_BYTES)


def group_of(count):
    return 16 if count <= 3 else 8


def cost(us):
    return pl.CostEstimate(flops=int(us * 1e9), bytes_accessed=0, transcendentals=0)


def hub_kernel(hub_rows, features, out, wide, rows):
    @pl.loop(0, NODES // 512)
    def _(i):
        cut = pl.ds(i * 512, 512)
        wide[cut, :] = features[cut, :].astype(jnp.float32)

    @pl.loop(0, HUB // 16)
    def _(i):
        for u in range(16):
            rows[pl.ds(i * 16 + u, 1), :] = wide[pl.ds(hub_rows[i * 16 + u], 1), :]

    out[...] = rows[...].astype(jnp.bfloat16)


def pick_hubs(hub_rows, features):
    return pl.pallas_call(
        hub_kernel,
        out_shape=jax.ShapeDtypeStruct((HUB, F), jnp.bfloat16),
        in_specs=[smem, vmem],
        out_specs=vmem,
        scratch_shapes=[pltpu.VMEM((NODES, F), jnp.float32), pltpu.VMEM((HUB, F), jnp.float32)],
        compiler_params=params,
        cost_estimate=cost(2),
        name="pick_hubs",
    )(hub_rows, features)


ROWS = NODES // LANES


def order_by(count):
    lane_r = lax.broadcasted_iota(jnp.int32, (LANES, LANES), 0)
    lane_c = lax.broadcasted_iota(jnp.int32, (LANES, LANES), 1)
    before = (lane_r < lane_c).astype(jnp.bfloat16)
    row_r = lax.broadcasted_iota(jnp.int32, (ROWS, ROWS), 0)
    row_c = lax.broadcasted_iota(jnp.int32, (ROWS, ROWS), 1)
    above = (row_c < row_r).astype(jnp.bfloat16)
    lane = lax.broadcasted_iota(jnp.int32, (1, LANES), 1)
    hits = [(count == c).astype(jnp.float32) for c in range(FANOUT + 1)]
    stacked = jnp.concatenate(hits, axis=0).astype(jnp.bfloat16)
    in_rows = jnp.dot(stacked, before, preferred_element_type=jnp.float32)
    place = jnp.zeros((ROWS, LANES), jnp.float32)
    start = jnp.zeros((1, 1), jnp.float32)
    end_row = jnp.zeros((1, LANES), jnp.float32)
    for c in range(FANOUT + 1):
        hit = hits[c]
        per_row = jnp.sum(hit, axis=1, keepdims=True)
        earlier = jnp.dot(
            above,
            jnp.broadcast_to(per_row, (ROWS, LANES)).astype(jnp.bfloat16),
            preferred_element_type=jnp.float32,
        )
        in_row = in_rows[c * ROWS : (c + 1) * ROWS]
        place = place + hit * (in_row + earlier + start)
        start = start + jnp.sum(per_row, axis=0, keepdims=True)
        end_row = end_row + jnp.where(lane == c, start, 0.0)
    place = place.astype(jnp.int32)
    high = place >> 7
    low = place & (LANES - 1)
    slot_row = lax.broadcasted_iota(jnp.int32, (ROWS, LANES), 0)
    slot_lane = lax.broadcasted_iota(jnp.int32, (LANES, LANES), 0)
    own_lane = lax.broadcasted_iota(jnp.int32, (ROWS, LANES), 1).astype(jnp.float32)
    total = jnp.zeros((ROWS, LANES), jnp.float32)
    for r in range(ROWS):
        to_row = (high[r : r + 1, :] == slot_row).astype(jnp.float32)
        to_lane = (low[r : r + 1, :] == slot_lane).astype(jnp.bfloat16)
        both = jnp.concatenate([to_row * own_lane, to_row * float(r)], axis=0)
        found = lax.dot_general(
            both.astype(jnp.bfloat16),
            to_lane,
            (((1,), (1,)), ((), ())),
            preferred_element_type=jnp.float32,
        )
        total = total + found[:ROWS] + found[ROWS:] * float(LANES)
    return total.astype(jnp.int32), end_row.astype(jnp.int32)


def spread(neighbors, flat):
    for s in range(FANOUT):
        for r in range(ROWS):
            flat[s, r : r + 1, :] = neighbors[s : s + 1, r * LANES : (r + 1) * LANES]


def split(flat, count, out, is_front, is_back, front_value, back_value):
    fronts = jnp.zeros((ROWS, LANES), jnp.int32)
    backs = jnp.zeros((ROWS, LANES), jnp.int32)
    placed = [jnp.zeros((ROWS, LANES), jnp.int32) for _ in range(FANOUT)]
    for s in range(FANOUT):
        row = flat[s]
        live = count > s
        front = jnp.logical_and(live, is_front(row))
        back = jnp.logical_and(live, is_back(row))
        at_front = jnp.where(front, fronts, -1)
        at_back = jnp.where(back, backs, -1)
        for k in range(s + 1):
            placed[k] = jnp.where(at_front == k, front_value(row), placed[k])
            last = FANOUT - 1 - k
            placed[last] = jnp.where(at_back == k, back_value(row), placed[last])
        fronts = fronts + front.astype(jnp.int32)
        backs = backs + back.astype(jnp.int32)
    for s in range(FANOUT):
        out[s][...] = placed[s]
    return fronts, backs


def is_hub(row):
    return row >= HUB_AT


def is_own(row):
    return jnp.logical_and(row >= OWN, row < UPPER)


def near_kernel(neighbors, counts, *refs):
    out, (perm, ends, hub_counts, flat) = refs[:FANOUT], refs[FANOUT:]
    spread(neighbors, flat)
    near, hub = split(
        flat, counts[...], out,
        lambda row: jnp.logical_not(is_hub(row)), is_hub,
        lambda row: row, lambda row: row - HUB_AT,
    )
    hub_counts[...] = hub
    perm[...], ends[...] = order_by(near)


def hub_order_kernel(hub_counts, perm, ends):
    perm[...], ends[...] = order_by(hub_counts[...])


def back_kernel(neighbors, counts, *refs):
    out, (perm, ends, rim_perm, rim_ends, flat) = refs[:FANOUT], refs[FANOUT:]
    spread(neighbors, flat)
    own, rim = split(
        flat, counts[...], out,
        is_own, lambda row: jnp.logical_and(jnp.logical_not(is_own(row)), row < HUB_AT),
        lambda row: row - OWN, lambda row: jnp.where(row < OWN, row, row - NODES),
    )
    perm[...], ends[...] = order_by(own)
    rim_perm[...], rim_ends[...] = order_by(rim)


tile = jax.ShapeDtypeStruct((ROWS, LANES), jnp.int32)
line = jax.ShapeDtypeStruct((1, LANES), jnp.int32)
flat_slots = pltpu.VMEM((FANOUT, ROWS, LANES), jnp.int32)


def flat_order(perm, ends):
    return ends.reshape(LANES), perm.reshape(NODES)


def near_plan(neighbors, counts):
    *slots, perm, ends, hub_counts = pl.pallas_call(
        near_kernel,
        out_shape=(tile,) * FANOUT + (tile, line, tile),
        in_specs=[vmem] * 2,
        out_specs=(vmem,) * (FANOUT + 3),
        scratch_shapes=[flat_slots],
        compiler_params=params,
        cost_estimate=cost(4),
        name="near_plan",
    )(neighbors, counts)
    return [s.reshape(NODES) for s in slots], flat_order(perm, ends), hub_counts


def hub_plan(hub_counts):
    return flat_order(*pl.pallas_call(
        hub_order_kernel,
        out_shape=(tile, line),
        in_specs=[vmem],
        out_specs=(vmem,) * 2,
        compiler_params=params,
        cost_estimate=cost(3),
        name="hub_plan",
    )(hub_counts))


def back_plan(neighbors, counts):
    *slots, perm, ends, rim_perm, rim_ends = pl.pallas_call(
        back_kernel,
        out_shape=(tile,) * FANOUT + (tile, line) * 2,
        in_specs=[vmem] * 2,
        out_specs=(vmem,) * (FANOUT + 4),
        scratch_shapes=[flat_slots],
        compiler_params=params,
        cost_estimate=cost(6),
        name="back_plan",
    )(neighbors, counts)
    return [s.reshape(NODES) for s in slots], flat_order(perm, ends), flat_order(rim_perm, rim_ends)


def over_nodes(ends, perm, visit):
    for count in range(1, FANOUT + 1):
        size = group_of(count)
        first = ends[count - 1]
        groups = (ends[count] - first) // size
        rest = first + groups * size

        @pl.loop(0, groups)
        def _(g, count=count, size=size, first=first):
            at = first + g * size
            visit([perm[at + u] for u in range(size)], count)

        @pl.loop(rest, ends[count])
        def _(at, count=count):
            visit([perm[at]], count)


def gather_rows(ends, perm, slots, table, sums):
    def gather(nodes, count):
        for n in nodes:
            total = table[pl.ds(slots[0][n], 1), :]
            for s in range(1, count):
                total = total + table[pl.ds(slots[s][n], 1), :]
            sums[pl.ds(n, 1), :] = total

    over_nodes(ends, perm, gather)


def clear(ref, at, rows):
    step = 512

    @pl.loop(0, rows // step)
    def _(i):
        ref[pl.ds(at + i * step, step), :] = jnp.zeros((step, F), jnp.float32)


def near_gather_kernel(ends, perm, *refs):
    slots, (features, lower, upper, sums, table) = refs[:FANOUT], refs[FANOUT:]

    def widen(source, at, rows):
        step = 256

        @pl.loop(0, rows // step)
        def _(i):
            table[pl.ds(at + i * step, step), :] = source[pl.ds(i * step, step), :].astype(
                jnp.float32
            )

    widen(features, OWN, NODES)
    widen(lower, 0, HALO)
    widen(upper, UPPER, HALO)
    clear(sums, 0, NODES)
    gather_rows(ends, perm, slots, table, sums)


def near_gather(order, slots, features, lower, upper):
    return pl.pallas_call(
        near_gather_kernel,
        out_shape=jax.ShapeDtypeStruct((NODES, F), jnp.float32),
        in_specs=[smem] * (2 + FANOUT) + [vmem] * 3,
        out_specs=vmem,
        scratch_shapes=[pltpu.VMEM((HUB_AT, F), jnp.float32)],
        compiler_params=params,
        cost_estimate=cost(20),
        name="near_gather",
    )(*order, *slots, features, lower, upper)


def forward_kernel(ends, perm, *refs):
    slots = refs[:FANOUT][::-1]
    (
        h0, h1, h2, h3, h4, h5, near, features, counts, w_self, w_neigh, bias, cotangent,
        act, src, base, grads, table, sums,
    ) = refs[FANOUT:]
    y, x, core = lax.axis_index("y"), lax.axis_index("x"), lax.axis_index("core")
    position = 0
    for piece in (h0, h1, h2, h3, h4, h5):
        for i in range(piece.shape[0] // HUB):
            b = [(position >> k) & 1 for k in range(5)]
            owner_y = y ^ (b[0] * 1) ^ (b[1] * 3)
            owner_x = x ^ (b[2] * 1) ^ (b[3] * 3)
            owner = owner_y * 8 + owner_x * 2 + (core ^ b[4])
            table[pl.ds(owner * HUB, HUB), :] = piece[i * HUB : (i + 1) * HUB, :].astype(
                jnp.float32
            )
            position += 1

    clear(sums, 0, NODES)
    gather_rows(ends, perm, slots, table, sums)

    grads[...] = jnp.zeros_like(grads)
    contract_rows = (((0,), (0,)), ((), ()))
    contract_cols = (((1,), (1,)), ((), ()))
    block = 256

    @pl.loop(0, NODES // block)
    def _(i):
        cut = pl.ds(i * block, block)
        parts = []
        for k in range(block // LANES):
            row = counts[pl.ds(i * (block // LANES) + k, 1), :].astype(jnp.float32)
            parts.append(jnp.broadcast_to(row, (LANES, LANES)).T)
        divisor = jnp.concatenate(parts, axis=0)
        own = features[cut, :]
        agg = ((near[cut, :] + sums[cut, :]) / divisor).astype(jnp.bfloat16)
        z = (
            jnp.dot(own, w_self[...], preferred_element_type=jnp.float32)
            + jnp.dot(agg, w_neigh[...], preferred_element_type=jnp.float32)
            + bias[...]
        )
        scale = 0.7978845608028654
        squared = z * z
        t = jnp.tanh(scale * (z + 0.044715 * (squared * z)))
        half = 0.5 * (1.0 + t)
        act[cut, :] = (z * half).astype(jnp.bfloat16)
        slope = half + 0.5 * z * (1.0 - t * t) * (scale * (1.0 + 3 * 0.044715 * squared))
        dz_wide = cotangent[cut, :].astype(jnp.float32) * slope
        dz = dz_wide.astype(jnp.bfloat16)
        grads[0:F, :] += lax.dot_general(
            own, dz, contract_rows, preferred_element_type=jnp.float32
        )
        grads[F : 2 * F, :] += lax.dot_general(
            agg, dz, contract_rows, preferred_element_type=jnp.float32
        )
        partial = jnp.sum(
            dz.astype(jnp.float32).reshape(block // 8, 8, H), axis=0
        )
        grads[2 * F : 2 * F + 8, :] += partial
        src[cut, :] = (
            lax.dot_general(dz, w_neigh[...], contract_cols, preferred_element_type=jnp.float32)
            / divisor
        )
        base[cut, :] = lax.dot_general(
            dz, w_self[...], contract_cols, preferred_element_type=jnp.float32
        )


def forward(order, slots, hubs, near, features, counts, w_self, w_neigh, bias, cot):
    return pl.pallas_call(
        forward_kernel,
        out_shape=(
            jax.ShapeDtypeStruct((NODES, H), jnp.bfloat16),
            jax.ShapeDtypeStruct((NODES, F), jnp.float32),
            jax.ShapeDtypeStruct((NODES, F), jnp.float32),
            jax.ShapeDtypeStruct((2 * F + 16, H), jnp.float32),
        ),
        in_specs=[smem] * (2 + FANOUT) + [vmem] * (len(hubs) + 7),
        out_specs=(vmem,) * 4,
        scratch_shapes=[
            pltpu.VMEM((HUBS, F), jnp.float32),
            pltpu.VMEM((NODES, F), jnp.float32),
        ],
        compiler_params=params,
        cost_estimate=cost(16),
        name="forward",
    )(*order, *slots, *hubs, near, features, counts, w_self, w_neigh, bias, cot)


def scatter_rows(ends, perm, slots, src, chains):
    def scatter(nodes, count):
        turn = 0
        for n in nodes:
            row = src[pl.ds(n, 1), :]
            for s in range(count):
                chain = chains[turn % CHAINS]
                turn += 1
                at = pl.ds(slots[s][n], 1)
                chain[at, :] = chain[at, :] + row

    over_nodes(ends, perm, scatter)


def chain_sum(chains, cut):
    out = chains[0][cut, :]
    for chain in chains[1:]:
        out = out + chain[cut, :]
    return out


def hub_scatter_kernel(ends, perm, *refs):
    slots, (src, hub), chains = refs[:FANOUT][::-1], refs[FANOUT : FANOUT + 2], refs[FANOUT + 2 :]
    for chain in chains:
        clear(chain, 0, HUBS)
    scatter_rows(ends, perm, slots, src, chains)

    @pl.loop(0, COLS)
    def _(owner):
        y, x, core = owner >> 3, (owner >> 1) & 3, owner & 1
        at = (core * 16 + x * 4 + y) * HUB
        hub[pl.ds(at, HUB), :] = chain_sum(chains, pl.ds(owner * HUB, HUB)).astype(jnp.bfloat16)


def rim_scatter_kernel(ends, perm, *refs):
    slots, (src, rim), chains = refs[:FANOUT][::-1], refs[FANOUT : FANOUT + 2], refs[FANOUT + 2 :]
    for chain in chains:
        clear(chain, 0, 2 * HALO)
    scatter_rows(ends, perm, slots, src, chains)

    @pl.loop(0, 2 * HALO // HUB)
    def _(i):
        cut = pl.ds(i * HUB, HUB)
        rim[cut, :] = chain_sum(chains, cut).astype(jnp.bfloat16)


def own_scatter_kernel(ends, perm, *refs):
    slots, (src, base, own), chains = refs[:FANOUT], refs[FANOUT : FANOUT + 3], refs[FANOUT + 3 :]
    for chain in chains[1:]:
        clear(chain, 0, NODES)
    step = 512

    @pl.loop(0, NODES // step)
    def _(i):
        cut = pl.ds(i * step, step)
        chains[0][cut, :] = base[cut, :]

    scatter_rows(ends, perm, slots, src, chains)

    @pl.loop(0, NODES // HUB)
    def _(i):
        cut = pl.ds(i * HUB, HUB)
        own[cut, :] = chain_sum(chains, cut)


def scatter(kernel, rows, kind, us, order, slots, *inputs):
    return pl.pallas_call(
        kernel,
        out_shape=jax.ShapeDtypeStruct((rows, F), kind),
        in_specs=[smem] * (2 + FANOUT) + [vmem] * len(inputs),
        out_specs=vmem,
        scratch_shapes=[pltpu.VMEM((rows, F), jnp.float32)] * CHAINS,
        compiler_params=params,
        cost_estimate=cost(us),
        name=kernel.__name__,
    )(*order, *slots, *inputs)


def finish_kernel(hub_rows, own, from_above, from_below, share, out, total):
    step = 256

    @pl.loop(0, NODES // step)
    def _(i):
        cut = pl.ds(i * step, step)
        total[cut, :] = own[cut, :]

    @pl.loop(0, HALO // step)
    def _(i):
        cut = pl.ds(i * step, step)
        total[cut, :] = total[cut, :] + from_above[cut, :].astype(jnp.float32)

    @pl.loop(0, HALO // step)
    def _(i):
        cut = pl.ds(NODES - HALO + i * step, step)
        total[cut, :] = total[cut, :] + from_below[pl.ds(i * step, step), :].astype(jnp.float32)

    @pl.loop(0, HUB // 8)
    def _(i):
        for u in range(8):
            at = pl.ds(hub_rows[i * 8 + u], 1)
            total[at, :] = total[at, :] + share[pl.ds(i * 8 + u, 1), :]

    @pl.loop(0, NODES // step)
    def _(i):
        cut = pl.ds(i * step, step)
        out[cut, :] = total[cut, :].astype(jnp.bfloat16)


def finish(hub_rows, own, from_above, from_below, share):
    return pl.pallas_call(
        finish_kernel,
        out_shape=jax.ShapeDtypeStruct((NODES, F), jnp.bfloat16),
        in_specs=[smem] + [vmem] * 4,
        out_specs=vmem,
        scratch_shapes=[pltpu.VMEM((NODES, F), jnp.float32)],
        compiler_params=params,
        cost_estimate=cost(3),
        name="finish",
    )(hub_rows, own, from_above, from_below, share)


def swap(value, axis, flip):
    count = lax.axis_size(axis)
    return lax.ppermute(value, axis, [(i, i ^ flip) for i in range(count)])


def shifted(value, axis, by):
    count = lax.axis_size(axis)
    pairs = [(i, i + by) for i in range(count) if 0 <= i + by < count]
    return lax.ppermute(value, axis, pairs)


def halves(value, bit):
    rows = value.shape[0] // 2
    keep = lax.dynamic_slice_in_dim(value, bit * rows, rows, axis=0)
    give = lax.dynamic_slice_in_dim(value, (1 - bit) * rows, rows, axis=0)
    return keep, give


def halve(value, axis, flip, bit):
    keep, give = halves(value, bit)
    got = swap(give.astype(jnp.bfloat16), axis, flip)
    return keep.astype(jnp.float32) + got.astype(jnp.float32)


def tie(*values):
    return lax.optimization_barrier(values)


def on_device(features, neighbors, counts, hub_rows, w_self, w_neigh, out_bias, cotangent):
    x, y, core = lax.axis_index("x"), lax.axis_index("y"), lax.axis_index("core")
    slots = neighbors.T
    counts = counts.reshape(ROWS, LANES)

    h0 = pick_hubs(hub_rows, features)
    h1 = swap(h0, "y", 1)
    near_slots, near_order, hub_counts = near_plan(slots, counts)
    lower = shifted(features[NODES - HALO :], "z", 1)
    upper = shifted(features[:HALO], "z", -1)
    h1, hub_counts = tie(h1, hub_counts)
    held = jnp.concatenate([h0, h1], axis=0)
    h2 = swap(held, "y", 3)
    hub_order = hub_plan(hub_counts)
    h2, slots, *hub_order = tie(h2, slots, *hub_order)
    held = jnp.concatenate([held, h2], axis=0)
    h3 = swap(held, "x", 1)
    back_slots, own_order, rim_order = back_plan(slots, counts)
    h3, lower, upper, own_order, rim_order = tie(h3, lower, upper, own_order, rim_order)
    held = jnp.concatenate([held, h3], axis=0)
    h4 = swap(held, "x", 3)
    near = near_gather(near_order, near_slots, features, lower, upper)
    h4, near = tie(h4, near)
    held = jnp.concatenate([held, h4], axis=0)
    h5 = swap(held, "core", 1)

    act, src, base, grads = forward(
        hub_order, near_slots, (h0, h1, h2, h3, h4, h5), near, features, counts,
        w_self, w_neigh, out_bias.reshape(1, H), cotangent,
    )

    keep, give = halves(grads, core)
    grads = keep + swap(give, "core", 1)
    src, grads = tie(src, grads)
    other = swap(grads, "z", 1)
    hub = scatter(hub_scatter_kernel, HUBS, jnp.bfloat16, 8, hub_order, near_slots, src)
    hub, src, other = tie(hub, src, other)
    grads = grads + other
    other = swap(grads, "z", 3)
    hub = halve(hub, "core", 1, core)
    rim = scatter(rim_scatter_kernel, 2 * HALO, jnp.bfloat16, 8, rim_order, back_slots, src)
    hub, src, other, rim = tie(hub, src, other, rim)
    grads = grads + other
    other = swap(grads, "x", 3)
    hub = halve(hub, "x", 3, x // 2)
    from_below = shifted(rim[:HALO], "z", -1)
    from_above = shifted(rim[HALO:], "z", 1)
    own = scatter(own_scatter_kernel, NODES, jnp.float32, 20, own_order, back_slots, src, base)
    hub, other, own, from_above, from_below = tie(hub, other, own, from_above, from_below)
    grads = grads + other
    grads = grads + swap(grads, "x", 1)
    hub = halve(hub, "x", 1, x % 2)
    grads = grads + swap(grads, "y", 3)
    hub = halve(hub, "y", 3, y // 2)
    grads = grads + swap(grads, "y", 1)
    share = halve(hub, "y", 1, y % 2)
    other = swap(grads, "core", 1)
    grads = jnp.concatenate(
        [jnp.where(core == 0, grads, other), jnp.where(core == 0, other, grads)], axis=0
    )
    grad_features = finish(hub_rows, own, from_above, from_below, share)
    grad_bias = jnp.sum(grads[2 * F :], axis=0)
    return act, grad_features, grads[:F], grads[F : 2 * F], grad_bias


def solution(mesh):
    mesh = Mesh(mesh.devices.reshape(4, 4, 4, 2), AXES)
    rows = P(AXES, None)
    placed = (rows, rows, P(AXES), P(AXES), P(), P(), P(), rows)
    return jax.shard_map(
        on_device,
        mesh=mesh,
        in_specs=placed,
        out_specs=(rows, rows, P(), P(), P()),
        check_vma=False,
    )
```

```python
import functools

import jax
import jax.numpy as jnp
from jax import lax
from jax.experimental import pallas as pl
from jax.experimental.pallas import tpu as pltpu
from jax.sharding import Mesh, PartitionSpec as P

F = 128
H = 256
NODES = 4096
HALO = 1024
HUB = 128
FANOUT = 10
COLS = 32
HUBS = HUB * COLS
OWN = HALO
UPPER = HALO + NODES
HUB_AT = 2 * HALO + NODES
EXTENT = HUB_AT + HUBS
LANES = 128
CHAINS = 8
VMEM_BYTES = 60 * 2**20
AXES = ("z", "y", "x", "core")

smem = pl.BlockSpec(memory_space=pltpu.SMEM)
vmem = pl.BlockSpec(memory_space=pltpu.VMEM)
hbm = pl.BlockSpec(memory_space=pl.ANY)
params = pltpu.CompilerParams(vmem_limit_bytes=VMEM_BYTES)


def group_of(count):
    return 16 if count <= 3 else 8


def cost(us):
    return pl.CostEstimate(flops=int(us * 1e9), bytes_accessed=0, transcendentals=0)


def hub_kernel(hub_rows, features, out, wide, rows):
    @pl.loop(0, NODES // 512)
    def _(i):
        cut = pl.ds(i * 512, 512)
        wide[cut, :] = features[cut, :].astype(jnp.float32)

    @pl.loop(0, HUB // 16)
    def _(i):
        for u in range(16):
            rows[pl.ds(i * 16 + u, 1), :] = wide[pl.ds(hub_rows[i * 16 + u], 1), :]

    out[...] = rows[...].astype(jnp.bfloat16)


def pick_hubs(hub_rows, features):
    return pl.pallas_call(
        hub_kernel,
        out_shape=jax.ShapeDtypeStruct((HUB, F), jnp.bfloat16),
        in_specs=[smem, vmem],
        out_specs=vmem,
        scratch_shapes=[pltpu.VMEM((NODES, F), jnp.float32), pltpu.VMEM((HUB, F), jnp.float32)],
        compiler_params=params,
        cost_estimate=cost(2),
        name="pick_hubs",
    )(hub_rows, features)


ROWS = NODES // LANES


def order_by(count):
    lane_r = lax.broadcasted_iota(jnp.int32, (LANES, LANES), 0)
    lane_c = lax.broadcasted_iota(jnp.int32, (LANES, LANES), 1)
    before = (lane_r < lane_c).astype(jnp.bfloat16)
    row_r = lax.broadcasted_iota(jnp.int32, (ROWS, ROWS), 0)
    row_c = lax.broadcasted_iota(jnp.int32, (ROWS, ROWS), 1)
    above = (row_c < row_r).astype(jnp.bfloat16)
    lane = lax.broadcasted_iota(jnp.int32, (1, LANES), 1)
    hits = [(count == c).astype(jnp.float32) for c in range(FANOUT + 1)]
    stacked = jnp.concatenate(hits, axis=0).astype(jnp.bfloat16)
    in_rows = jnp.dot(stacked, before, preferred_element_type=jnp.float32)
    place = jnp.zeros((ROWS, LANES), jnp.float32)
    start = jnp.zeros((1, 1), jnp.float32)
    end_row = jnp.zeros((1, LANES), jnp.float32)
    for c in range(FANOUT + 1):
        hit = hits[c]
        per_row = jnp.sum(hit, axis=1, keepdims=True)
        earlier = jnp.dot(
            above,
            jnp.broadcast_to(per_row, (ROWS, LANES)).astype(jnp.bfloat16),
            preferred_element_type=jnp.float32,
        )
        in_row = in_rows[c * ROWS : (c + 1) * ROWS]
        place = place + hit * (in_row + earlier + start)
        start = start + jnp.sum(per_row, axis=0, keepdims=True)
        end_row = end_row + jnp.where(lane == c, start, 0.0)
    place = place.astype(jnp.int32)
    high = place >> 7
    low = place & (LANES - 1)
    slot_row = lax.broadcasted_iota(jnp.int32, (ROWS, LANES), 0)
    slot_lane = lax.broadcasted_iota(jnp.int32, (LANES, LANES), 0)
    own_lane = lax.broadcasted_iota(jnp.int32, (ROWS, LANES), 1).astype(jnp.float32)
    total = jnp.zeros((ROWS, LANES), jnp.float32)
    for r in range(ROWS):
        to_row = (high[r : r + 1, :] == slot_row).astype(jnp.float32)
        to_lane = (low[r : r + 1, :] == slot_lane).astype(jnp.bfloat16)
        both = jnp.concatenate([to_row * own_lane, to_row * float(r)], axis=0)
        found = lax.dot_general(
            both.astype(jnp.bfloat16),
            to_lane,
            (((1,), (1,)), ((), ())),
            preferred_element_type=jnp.float32,
        )
        total = total + found[:ROWS] + found[ROWS:] * float(LANES)
    return total.astype(jnp.int32), end_row.astype(jnp.int32)


def compact(flat, count, is_kind, value, backwards, placed):
    found = jnp.zeros((ROWS, LANES), jnp.int32)
    for s in range(FANOUT):
        row = flat[s * ROWS : (s + 1) * ROWS, :]
        hit = jnp.logical_and(count > s, is_kind(row))
        at = jnp.where(hit, found, -1)
        for k in range(s + 1):
            place = FANOUT - 1 - k if backwards else k
            placed[place] = jnp.where(at == k, value(row), placed[place])
        found = found + hit.astype(jnp.int32)
    return found


def nothing_placed():
    return [jnp.zeros((ROWS, LANES), jnp.int32) for _ in range(FANOUT)]


def is_own(row):
    return jnp.logical_and(row >= OWN, row < UPPER)


def is_rim(row):
    return jnp.logical_or(row < OWN, jnp.logical_and(row >= UPPER, row < HUB_AT))


def all_plan_kernel(neighbors, counts, flat, perm, ends):
    for s in range(FANOUT):
        for r in range(ROWS):
            at = s * ROWS + r
            flat[at : at + 1, :] = neighbors[s : s + 1, r * LANES : (r + 1) * LANES]
    perm[...], ends[...] = order_by(counts[...])


def hub_plan_kernel(flat, counts, slots, perm, ends):
    placed = nothing_placed()
    hubs = compact(
        flat, counts[...], lambda row: row >= HUB_AT, lambda row: row - HUB_AT, False, placed
    )
    for s in range(FANOUT):
        slots[s * ROWS : (s + 1) * ROWS, :] = placed[s]
    perm[...], ends[...] = order_by(hubs)


def rim_plan_kernel(flat, counts, slots, perm, ends, own_counts):
    placed = nothing_placed()
    own_counts[...] = compact(flat, counts[...], is_own, lambda row: row - OWN, False, placed)
    rims = compact(
        flat, counts[...], is_rim, lambda row: jnp.where(row < OWN, row, row - NODES), True, placed
    )
    for s in range(FANOUT):
        slots[s * ROWS : (s + 1) * ROWS, :] = placed[s]
    perm[...], ends[...] = order_by(rims)


def own_plan_kernel(own_counts, perm, ends):
    perm[...], ends[...] = order_by(own_counts[...])


tile = jax.ShapeDtypeStruct((ROWS, LANES), jnp.int32)
line = jax.ShapeDtypeStruct((1, LANES), jnp.int32)
tiles = jax.ShapeDtypeStruct((FANOUT * ROWS, LANES), jnp.int32)


def plan(kernel, outs, us, *inputs):
    return pl.pallas_call(
        kernel,
        out_shape=outs,
        in_specs=[vmem] * len(inputs),
        out_specs=(vmem,) * len(outs),
        compiler_params=params,
        cost_estimate=cost(us),
        name=kernel.__name__,
    )(*inputs)


def lists(perm, ends, slots):
    return ends.reshape(LANES), perm.reshape(NODES), slots.reshape(FANOUT * NODES)


list_specs = [smem, hbm, hbm]
list_scratch = [pltpu.SMEM((NODES,), jnp.int32)] * (1 + FANOUT) + [
    pltpu.SemaphoreType.DMA((1 + FANOUT,))
]


class Lists:
    def __init__(self, ends, perm, slots, perm_at, *rest):
        slots_at, sems = rest[:FANOUT], rest[FANOUT]
        self.ends, self.perm, self.slots = ends, perm_at, slots_at
        self.copies = [pltpu.make_async_copy(perm, perm_at, sems.at[0])]
        for s in range(FANOUT):
            part = slots.at[pl.ds(s * NODES, NODES)]
            self.copies.append(pltpu.make_async_copy(part, slots_at[s], sems.at[1 + s]))
        for copy in self.copies:
            copy.start()

    def visit(self, act, backwards=False):
        slots = self.slots[::-1] if backwards else self.slots
        copies = self.copies[:0:-1] if backwards else self.copies[1:]
        self.copies[0].wait()
        for count in range(1, FANOUT + 1):
            copies[count - 1].wait()
            size = group_of(count)
            first = self.ends[count - 1]
            last = self.ends[count]
            groups = (last - first) // size
            rest = first + groups * size

            @pl.loop(0, groups)
            def _(g, count=count, size=size, first=first):
                at = first + g * size
                act([self.perm[at + u] for u in range(size)], count, slots)

            @pl.loop(rest, last)
            def _(at, count=count):
                act([self.perm[at]], count, slots)


def clear(ref, at, rows):
    step = 512

    @pl.loop(0, rows // step)
    def _(i):
        ref[pl.ds(at + i * step, step), :] = jnp.zeros((step, F), jnp.float32)


BLOCK = 256
HUB_PIECES = (1, 1, 2, 4, 8, 16)


def forward_kernel(ends, perm, slots, features, lower, upper, *refs):
    pieces, refs = refs[:6], refs[6:]
    counts, w_self, w_neigh, bias, cotangent, act, src, base, grads = refs[:9]
    table, sums, features_at, rims_at, hubs_at, cot_at, act_at, src_at, base_at, weights = refs[9:19]
    lists_at, (sem_in, sem_out) = refs[19:-2], refs[-2:]
    copies = [
        pltpu.make_async_copy(features, features_at, sem_in.at[0]),
        pltpu.make_async_copy(lower, rims_at.at[pl.ds(0, HALO)], sem_in.at[1]),
        pltpu.make_async_copy(upper, rims_at.at[pl.ds(HALO, HALO)], sem_in.at[2]),
    ]
    at = 0
    for k, piece in enumerate(pieces):
        rows = HUB_PIECES[k] * HUB
        copies.append(
            pltpu.make_async_copy(piece, hubs_at.at[pl.ds(at, rows)], sem_in.at[3 + k])
        )
        at += rows
    for copy in copies:
        copy.start()
    todo = Lists(ends, perm, slots, *lists_at)
    cot_copy = pltpu.make_async_copy(cotangent, cot_at, sem_in.at[9])
    cot_copy.start()

    weights[0:F, :] = w_self[...]
    weights[F : 2 * F, :] = w_neigh[...]
    grads[...] = jnp.zeros_like(grads)

    def widen(source, start, at, rows):
        step = 256

        @pl.loop(0, rows // step)
        def _(i):
            table[pl.ds(at + i * step, step), :] = source[
                pl.ds(start + i * step, step), :
            ].astype(jnp.float32)

    copies[0].wait()
    widen(features_at, 0, OWN, NODES)
    copies[1].wait()
    widen(rims_at, 0, 0, HALO)
    copies[2].wait()
    widen(rims_at, HALO, UPPER, HALO)
    y, x, core = lax.axis_index("y"), lax.axis_index("x"), lax.axis_index("core")
    position = 0
    for k in range(6):
        copies[3 + k].wait()
        for _ in range(HUB_PIECES[k]):
            b = [(position >> k) & 1 for k in range(5)]
            owner_y = y ^ (b[0] * 1) ^ (b[1] * 3)
            owner_x = x ^ (b[2] * 1) ^ (b[3] * 3)
            owner = owner_y * 8 + owner_x * 2 + (core ^ b[4])
            table[pl.ds(HUB_AT + owner * HUB, HUB), :] = hubs_at[
                position * HUB : (position + 1) * HUB, :
            ].astype(jnp.float32)
            position += 1

    def gather(nodes, count, slots):
        for n in nodes:
            total = table[pl.ds(slots[0][n], 1), :]
            for s in range(1, count):
                total = total + table[pl.ds(slots[s][n], 1), :]
            sums[pl.ds(n, 1), :] = total

    todo.visit(gather)
    cot_copy.wait()

    @pl.loop(0, NODES // BLOCK)
    def _(i):
        cut = pl.ds(i * BLOCK, BLOCK)
        parts = []
        for k in range(BLOCK // LANES):
            row = counts[pl.ds(i * (BLOCK // LANES) + k, 1), :].astype(jnp.float32)
            parts.append(jnp.broadcast_to(row, (LANES, LANES)).T)
        divisor = jnp.concatenate(parts, axis=0)
        agg = (sums[cut, :] / divisor).astype(jnp.bfloat16)
        both = jnp.concatenate([features_at[cut, :], agg], axis=1)
        z = jnp.dot(both, weights[...], preferred_element_type=jnp.float32) + bias[...]
        scale = 0.7978845608028654
        cubic = 0.044715 * scale
        squared = z * z
        t = jnp.tanh(z * (scale + cubic * squared))
        half = 0.5 * z
        rest = half * t
        act_at[cut, :] = (half + rest).astype(jnp.bfloat16)
        slope = (0.5 + 0.5 * t) + (half - rest * t) * (scale + 3 * cubic * squared)
        dz = (cot_at[cut, :].astype(jnp.float32) * slope).astype(jnp.bfloat16)
        grads[0 : 2 * F, :] += lax.dot_general(
            both, dz, (((0,), (0,)), ((), ())), preferred_element_type=jnp.float32
        )
        grads[2 * F : 2 * F + 8, :] += jnp.sum(
            dz.astype(jnp.float32).reshape(BLOCK // 8, 8, H), axis=0
        )
        back = lax.dot_general(
            dz, weights[...], (((1,), (1,)), ((), ())), preferred_element_type=jnp.float32
        )
        base_at[cut, :] = back[:, :F]
        src_at[cut, :] = back[:, F:] / divisor
        for k, (here, there) in enumerate(((act_at, act), (src_at, src), (base_at, base))):
            pltpu.make_async_copy(here.at[cut], there.at[cut], sem_out.at[k]).start()

    for k, (here, there) in enumerate(((act_at, act), (src_at, src), (base_at, base))):
        pltpu.make_async_copy(here, there, sem_out.at[k]).wait()


def forward(lists, features, lower, upper, hubs, counts, w_self, w_neigh, bias, cot):
    return pl.pallas_call(
        forward_kernel,
        out_shape=(
            jax.ShapeDtypeStruct((NODES, H), jnp.bfloat16),
            jax.ShapeDtypeStruct((NODES, F), jnp.float32),
            jax.ShapeDtypeStruct((NODES, F), jnp.float32),
            jax.ShapeDtypeStruct((2 * F + 16, H), jnp.float32),
        ),
        in_specs=list_specs + [hbm] * (3 + len(hubs)) + [vmem] * 4 + [hbm],
        out_specs=(hbm, hbm, hbm, vmem),
        scratch_shapes=[
            pltpu.VMEM((EXTENT, F), jnp.float32),
            pltpu.VMEM((NODES, F), jnp.float32),
            pltpu.VMEM((NODES, F), jnp.bfloat16),
            pltpu.VMEM((2 * HALO, F), jnp.bfloat16),
            pltpu.VMEM((HUBS, F), jnp.bfloat16),
            pltpu.VMEM((NODES, H), jnp.bfloat16),
            pltpu.VMEM((NODES, H), jnp.bfloat16),
            pltpu.VMEM((NODES, F), jnp.float32),
            pltpu.VMEM((NODES, F), jnp.float32),
            pltpu.VMEM((2 * F, H), jnp.bfloat16),
        ]
        + list_scratch
        + [pltpu.SemaphoreType.DMA((10,)), pltpu.SemaphoreType.DMA((3,))],
        compiler_params=params,
        cost_estimate=cost(30),
        name="forward",
    )(*lists, features, lower, upper, *hubs, counts, w_self, w_neigh, bias, cot)


def chain_sum(chains, cut):
    out = chains[0][cut, :]
    for chain in chains[1:]:
        out = out + chain[cut, :]
    return out


def scatter_kernel(place, backwards, based, ends, perm, slots, src, *refs):
    if based:
        base, refs = refs[0], refs[1:]
    out, refs = refs[0], refs[1:]
    chains, refs = refs[:CHAINS], refs[CHAINS:]
    src_at, out_at = refs[:2]
    lists_at, sems = refs[2:-1], refs[-1]
    todo = Lists(ends, perm, slots, *lists_at)
    src_copy = pltpu.make_async_copy(src, src_at, sems.at[0])
    src_copy.start()
    rows = out_at.shape[0]
    if based:
        base_copy = pltpu.make_async_copy(base, chains[0], sems.at[1])
        base_copy.start()
    for chain in chains[1 if based else 0 :]:
        clear(chain, 0, rows)
    if based:
        base_copy.wait()
    src_copy.wait()

    def scatter(nodes, count, slots):
        turn = 0
        for n in nodes:
            row = src_at[pl.ds(n, 1), :]
            for s in range(count):
                chain = chains[turn % CHAINS]
                turn += 1
                at = pl.ds(slots[s][n], 1)
                chain[at, :] = chain[at, :] + row

    todo.visit(scatter, backwards)

    @pl.loop(0, rows // HUB)
    def _(i):
        to = pl.ds(place(i) * HUB, HUB)
        out_at[to, :] = chain_sum(chains, pl.ds(i * HUB, HUB)).astype(out_at.dtype)
        pltpu.make_async_copy(out_at.at[to], out.at[to], sems.at[2]).start()

    pltpu.make_async_copy(out_at, out, sems.at[2]).wait()


def hub_place(owner):
    return (owner & 1) * 16 + ((owner >> 1) & 3) * 4 + (owner >> 3)


def scatter(name, rows, kind, us, place, backwards, lists, *inputs):
    return pl.pallas_call(
        functools.partial(scatter_kernel, place, backwards, len(inputs) > 1),
        out_shape=jax.ShapeDtypeStruct((rows, F), kind),
        in_specs=list_specs + [hbm] * len(inputs),
        out_specs=hbm,
        scratch_shapes=[pltpu.VMEM((rows, F), jnp.float32)] * CHAINS
        + [pltpu.VMEM((NODES, F), jnp.float32), pltpu.VMEM((rows, F), kind)]
        + list_scratch
        + [pltpu.SemaphoreType.DMA((3,))],
        compiler_params=params,
        cost_estimate=cost(us),
        name=name,
    )(*lists, *inputs)


def finish_kernel(hub_rows, own, from_above, from_below, share, out, total):
    step = 256

    @pl.loop(0, NODES // step)
    def _(i):
        cut = pl.ds(i * step, step)
        total[cut, :] = own[cut, :]

    @pl.loop(0, HALO // step)
    def _(i):
        cut = pl.ds(i * step, step)
        total[cut, :] = total[cut, :] + from_above[cut, :].astype(jnp.float32)

    @pl.loop(0, HALO // step)
    def _(i):
        cut = pl.ds(NODES - HALO + i * step, step)
        total[cut, :] = total[cut, :] + from_below[pl.ds(i * step, step), :].astype(jnp.float32)

    @pl.loop(0, HUB // 8)
    def _(i):
        for u in range(8):
            at = pl.ds(hub_rows[i * 8 + u], 1)
            total[at, :] = total[at, :] + share[pl.ds(i * 8 + u, 1), :]

    @pl.loop(0, NODES // step)
    def _(i):
        cut = pl.ds(i * step, step)
        out[cut, :] = total[cut, :].astype(jnp.bfloat16)


def finish(hub_rows, own, from_above, from_below, share):
    return pl.pallas_call(
        finish_kernel,
        out_shape=jax.ShapeDtypeStruct((NODES, F), jnp.bfloat16),
        in_specs=[smem] + [vmem] * 4,
        out_specs=vmem,
        scratch_shapes=[pltpu.VMEM((NODES, F), jnp.float32)],
        compiler_params=params,
        cost_estimate=cost(3),
        name="finish",
    )(hub_rows, own, from_above, from_below, share)


def swap(value, axis, flip):
    count = lax.axis_size(axis)
    return lax.ppermute(value, axis, [(i, i ^ flip) for i in range(count)])


def shifted(value, axis, by):
    count = lax.axis_size(axis)
    pairs = [(i, i + by) for i in range(count) if 0 <= i + by < count]
    return lax.ppermute(value, axis, pairs)


def halves(value, bit):
    rows = value.shape[0] // 2
    keep = lax.dynamic_slice_in_dim(value, bit * rows, rows, axis=0)
    give = lax.dynamic_slice_in_dim(value, (1 - bit) * rows, rows, axis=0)
    return keep, give


def halve(value, axis, flip, bit):
    keep, give = halves(value, bit)
    got = swap(give.astype(jnp.bfloat16), axis, flip)
    return keep.astype(jnp.float32) + got.astype(jnp.float32)


def tie(*values):
    return lax.optimization_barrier(values)


def on_device(features, neighbors, counts, hub_rows, w_self, w_neigh, out_bias, cotangent):
    x, y, core = lax.axis_index("x"), lax.axis_index("y"), lax.axis_index("core")
    counts = counts.reshape(ROWS, LANES)

    h0 = pick_hubs(hub_rows, features)
    h1 = swap(h0, "y", 1)
    lower = shifted(features[NODES - HALO :], "z", 1)
    upper = shifted(features[:HALO], "z", -1)
    flat, perm, ends = plan(all_plan_kernel, (tiles, tile, line), 4, neighbors.T, counts)
    all_lists = lists(perm, ends, flat)
    h1, flat = tie(h1, flat)
    held = jnp.concatenate([h0, h1], axis=0)
    h2 = swap(held, "y", 3)
    slots, perm, ends = plan(hub_plan_kernel, (tiles, tile, line), 4, flat, counts)
    hub_lists = lists(perm, ends, slots)
    h2, flat, *hub_lists = tie(h2, flat, *hub_lists)
    held = jnp.concatenate([held, h2], axis=0)
    h3 = swap(held, "x", 1)
    slots, perm, ends, own_counts = plan(
        rim_plan_kernel, (tiles, tile, line, tile), 4, flat, counts
    )
    rim_lists = lists(perm, ends, slots)
    h3, lower, upper, own_counts, rim_lists = tie(h3, lower, upper, own_counts, rim_lists)
    held = jnp.concatenate([held, h3], axis=0)
    h4 = swap(held, "x", 3)
    perm, ends = plan(own_plan_kernel, (tile, line), 4, own_counts)
    own_lists = lists(perm, ends, slots)
    h4, *own_lists = tie(h4, *own_lists)
    held = jnp.concatenate([held, h4], axis=0)
    h5 = swap(held, "core", 1)

    act, src, base, grads = forward(
        all_lists, features, lower, upper, (h0, h1, h2, h3, h4, h5), counts,
        w_self, w_neigh, out_bias.reshape(1, H), cotangent,
    )

    keep, give = halves(grads, core)
    other = swap(give, "core", 1)
    hub = scatter("hub_scatter", HUBS, jnp.bfloat16, 8, hub_place, False, hub_lists, src)
    hub, src, other = tie(hub, src, other)
    grads = keep + other
    other = swap(grads, "z", 1)
    hub = halve(hub, "core", 1, core)
    rim = scatter(
        "rim_scatter", 2 * HALO, jnp.bfloat16, 8, lambda i: i, True, rim_lists, src
    )
    hub, src, other, rim = tie(hub, src, other, rim)
    grads = grads + other
    other = swap(grads, "z", 3)
    hub = halve(hub, "x", 3, x // 2)
    from_below = shifted(rim[:HALO], "z", -1)
    from_above = shifted(rim[HALO:], "z", 1)
    own = scatter(
        "own_scatter", NODES, jnp.float32, 20, lambda i: i, False, own_lists, src, base
    )
    hub, other, own, from_above, from_below = tie(hub, other, own, from_above, from_below)
    grads = grads + other
    grads = grads + swap(grads, "x", 3)
    hub = halve(hub, "x", 1, x % 2)
    grads = grads + swap(grads, "x", 1)
    hub = halve(hub, "y", 3, y // 2)
    grads = grads + swap(grads, "y", 3)
    share = halve(hub, "y", 1, y % 2)
    grads = grads + swap(grads, "y", 1)
    other = swap(grads, "core", 1)
    grads = jnp.concatenate(
        [jnp.where(core == 0, grads, other), jnp.where(core == 0, other, grads)], axis=0
    )
    grad_features = finish(hub_rows, own, from_above, from_below, share)
    grad_bias = jnp.sum(grads[2 * F :], axis=0)
    return act, grad_features, grads[:F], grads[F : 2 * F], grad_bias


def solution(mesh):
    mesh = Mesh(mesh.devices.reshape(4, 4, 4, 2), AXES)
    rows = P(AXES, None)
    placed = (rows, rows, P(AXES), P(AXES), P(), P(), P(), rows)
    return jax.shard_map(
        on_device,
        mesh=mesh,
        in_specs=placed,
        out_specs=(rows, rows, P(), P(), P()),
        check_vma=False,
    )
```

```python
import functools

import jax
import jax.numpy as jnp
from jax import lax
from jax.experimental import pallas as pl
from jax.experimental.pallas import tpu as pltpu
from jax.sharding import Mesh, PartitionSpec as P

F = 128
H = 256
NODES = 4096
HALO = 1024
HUB = 128
FANOUT = 10
COLS = 32
HUBS = HUB * COLS
OWN = HALO
UPPER = HALO + NODES
HUB_AT = 2 * HALO + NODES
EXTENT = HUB_AT + HUBS
LANES = 128
CHAINS = 8
VMEM_BYTES = 60 * 2**20
HALF = F + 8
AXES = ("z", "y", "x", "core")

smem = pl.BlockSpec(memory_space=pltpu.SMEM)
vmem = pl.BlockSpec(memory_space=pltpu.VMEM)
hbm = pl.BlockSpec(memory_space=pltpu.HBM)
params = pltpu.CompilerParams(vmem_limit_bytes=VMEM_BYTES)


def group_of(count):
    return 16 if count <= 3 else 8


def cost(us):
    return pl.CostEstimate(flops=int(us * 1e9), bytes_accessed=0, transcendentals=0)


def hub_kernel(hub_rows, features, out, wide, rows):
    @pl.loop(0, NODES // 512)
    def _(i):
        cut = pl.ds(i * 512, 512)
        wide[cut, :] = features[cut, :].astype(jnp.float32)

    @pl.loop(0, HUB // 16)
    def _(i):
        for u in range(16):
            rows[pl.ds(i * 16 + u, 1), :] = wide[pl.ds(hub_rows[i * 16 + u], 1), :]

    out[...] = rows[...].astype(jnp.bfloat16)


def pick_hubs(hub_rows, features):
    return pl.pallas_call(
        hub_kernel,
        out_shape=jax.ShapeDtypeStruct((HUB, F), jnp.bfloat16),
        in_specs=[smem, vmem],
        out_specs=vmem,
        scratch_shapes=[pltpu.VMEM((NODES, F), jnp.float32), pltpu.VMEM((HUB, F), jnp.float32)],
        compiler_params=params,
        cost_estimate=cost(2),
        name="pick_hubs",
    )(hub_rows, features)


ROWS = NODES // LANES


def order_by(count):
    lane_r = lax.broadcasted_iota(jnp.int32, (LANES, LANES), 0)
    lane_c = lax.broadcasted_iota(jnp.int32, (LANES, LANES), 1)
    before = (lane_r < lane_c).astype(jnp.bfloat16)
    row_r = lax.broadcasted_iota(jnp.int32, (ROWS, ROWS), 0)
    row_c = lax.broadcasted_iota(jnp.int32, (ROWS, ROWS), 1)
    above = (row_c < row_r).astype(jnp.bfloat16)
    lane = lax.broadcasted_iota(jnp.int32, (1, LANES), 1)
    hits = [(count == c).astype(jnp.float32) for c in range(FANOUT + 1)]
    stacked = jnp.concatenate(hits, axis=0).astype(jnp.bfloat16)
    in_rows = jnp.dot(stacked, before, preferred_element_type=jnp.float32)
    place = jnp.zeros((ROWS, LANES), jnp.float32)
    start = jnp.zeros((1, 1), jnp.float32)
    end_row = jnp.zeros((1, LANES), jnp.float32)
    for c in range(FANOUT + 1):
        hit = hits[c]
        per_row = jnp.sum(hit, axis=1, keepdims=True)
        earlier = jnp.dot(
            above,
            jnp.broadcast_to(per_row, (ROWS, LANES)).astype(jnp.bfloat16),
            preferred_element_type=jnp.float32,
        )
        in_row = in_rows[c * ROWS : (c + 1) * ROWS]
        place = place + hit * (in_row + earlier + start)
        start = start + jnp.sum(per_row, axis=0, keepdims=True)
        end_row = end_row + jnp.where(lane == c, start, 0.0)
    place = place.astype(jnp.int32)
    high = place >> 7
    low = place & (LANES - 1)
    slot_row = lax.broadcasted_iota(jnp.int32, (ROWS, LANES), 0)
    slot_lane = lax.broadcasted_iota(jnp.int32, (LANES, LANES), 0)
    own_lane = lax.broadcasted_iota(jnp.int32, (ROWS, LANES), 1).astype(jnp.float32)
    total = jnp.zeros((ROWS, LANES), jnp.float32)
    for r in range(ROWS):
        to_row = (high[r : r + 1, :] == slot_row).astype(jnp.float32)
        to_lane = (low[r : r + 1, :] == slot_lane).astype(jnp.bfloat16)
        both = jnp.concatenate([to_row * own_lane, to_row * float(r)], axis=0)
        found = lax.dot_general(
            both.astype(jnp.bfloat16),
            to_lane,
            (((1,), (1,)), ((), ())),
            preferred_element_type=jnp.float32,
        )
        total = total + found[:ROWS] + found[ROWS:] * float(LANES)
    return total.astype(jnp.int32), end_row.astype(jnp.int32)


def compact(flat, count, is_kind, value, backwards, placed):
    found = jnp.zeros((ROWS, LANES), jnp.int32)
    for s in range(FANOUT):
        row = flat[s * ROWS : (s + 1) * ROWS, :]
        hit = jnp.logical_and(count > s, is_kind(row))
        at = jnp.where(hit, found, -1)
        for k in range(s + 1):
            place = FANOUT - 1 - k if backwards else k
            placed[place] = jnp.where(at == k, value(row), placed[place])
        found = found + hit.astype(jnp.int32)
    return found


def nothing_placed():
    return [jnp.zeros((ROWS, LANES), jnp.int32) for _ in range(FANOUT)]


def is_own(row):
    return jnp.logical_and(row >= OWN, row < UPPER)


def is_rim(row):
    return jnp.logical_or(row < OWN, jnp.logical_and(row >= UPPER, row < HUB_AT))


def all_plan_kernel(neighbors, counts, flat, perm, ends):
    for s in range(FANOUT):
        for r in range(ROWS):
            at = s * ROWS + r
            flat[at : at + 1, :] = neighbors[s : s + 1, r * LANES : (r + 1) * LANES]
    perm[...], ends[...] = order_by(counts[...])


def hub_plan_kernel(flat, counts, slots, perm, ends):
    placed = nothing_placed()
    hubs = compact(
        flat, counts[...], lambda row: row >= HUB_AT, lambda row: row - HUB_AT, False, placed
    )
    for s in range(FANOUT):
        slots[s * ROWS : (s + 1) * ROWS, :] = placed[s]
    perm[...], ends[...] = order_by(hubs)


def rim_plan_kernel(flat, counts, slots, perm, ends, own_perm, own_ends):
    placed = nothing_placed()
    owns = compact(flat, counts[...], is_own, lambda row: row - OWN, False, placed)
    rims = compact(
        flat, counts[...], is_rim, lambda row: jnp.where(row < OWN, row, row - NODES), True, placed
    )
    for s in range(FANOUT):
        slots[s * ROWS : (s + 1) * ROWS, :] = placed[s]
    perm[...], ends[...] = order_by(rims)
    own_perm[...], own_ends[...] = order_by(owns)


tile = jax.ShapeDtypeStruct((ROWS, LANES), jnp.int32)
line = jax.ShapeDtypeStruct((1, LANES), jnp.int32)
tiles = jax.ShapeDtypeStruct((FANOUT * ROWS, LANES), jnp.int32)


def plan(kernel, outs, us, *inputs):
    return pl.pallas_call(
        kernel,
        out_shape=outs,
        in_specs=[vmem] * len(inputs),
        out_specs=(vmem,) * len(outs),
        compiler_params=params,
        cost_estimate=cost(us),
        name=kernel.__name__,
    )(*inputs)


def lists(perm, ends, slots):
    return ends.reshape(LANES), perm.reshape(NODES), slots.reshape(FANOUT * NODES)


list_specs = [smem, hbm, hbm]
list_scratch = [pltpu.SMEM((NODES,), jnp.int32)] * (1 + FANOUT) + [
    pltpu.SemaphoreType.DMA((1 + FANOUT,))
]


class Lists:
    def __init__(self, backwards, ends, perm, slots, perm_at, *rest):
        slots_at, sems = rest[:FANOUT], rest[FANOUT]
        self.ends, self.perm, self.slots = ends, perm_at, slots_at
        self.copies = [pltpu.make_async_copy(perm, perm_at, sems.at[0])]
        for s in range(FANOUT):
            part = slots.at[pl.ds(s * NODES, NODES)]
            self.copies.append(pltpu.make_async_copy(part, slots_at[s], sems.at[1 + s]))
        if backwards:
            self.slots = self.slots[::-1]
            self.copies[1:] = self.copies[:0:-1]
        for copy in self.copies:
            copy.start()

    def visit(self, act):
        slots, copies = self.slots, self.copies[1:]
        self.copies[0].wait()
        for count in range(1, FANOUT + 1):
            copies[count - 1].wait()
            size = group_of(count)
            first = self.ends[count - 1]
            last = self.ends[count]
            groups = (last - first) // size
            rest = first + groups * size

            @pl.loop(0, groups)
            def _(g, count=count, size=size, first=first):
                at = first + g * size
                act([self.perm[at + u] for u in range(size)], count, slots)

            @pl.loop(rest, last)
            def _(at, count=count):
                act([self.perm[at]], count, slots)


def clear(ref, at, rows):
    step = 512

    @pl.loop(0, rows // step)
    def _(i):
        ref[pl.ds(at + i * step, step), :] = jnp.zeros((step, F), jnp.float32)


BLOCK = 512
HUB_PIECES = (1, 1, 2, 4, 8, 16)


def forward_kernel(ends, perm, slots, features, lower, upper, *refs):
    pieces, refs = refs[:6], refs[6:]
    counts, w_self, w_neigh, bias, cotangent, act, src, base, grads = refs[:9]
    table, sums, features_at, rims_at, hubs_at, cot_at, act_at, src_at, base_at, weights = refs[9:19]
    lists_at, (sem_in, sem_out) = refs[19:-2], refs[-2:]
    copies = [
        pltpu.make_async_copy(features, features_at, sem_in.at[0]),
        pltpu.make_async_copy(lower, rims_at.at[pl.ds(0, HALO)], sem_in.at[1]),
        pltpu.make_async_copy(upper, rims_at.at[pl.ds(HALO, HALO)], sem_in.at[2]),
    ]
    at = 0
    for k, piece in enumerate(pieces):
        rows = HUB_PIECES[k] * HUB
        copies.append(
            pltpu.make_async_copy(piece, hubs_at.at[pl.ds(at, rows)], sem_in.at[3 + k])
        )
        at += rows
    for copy in copies:
        copy.start()
    todo = Lists(False, ends, perm, slots, *lists_at)
    cot_copy = pltpu.make_async_copy(cotangent, cot_at, sem_in.at[9])
    cot_copy.start()

    weights[0:F, :] = w_self[...]
    weights[F : 2 * F, :] = w_neigh[...]
    grads[...] = jnp.zeros_like(grads)

    def widen(source, start, at, rows):
        step = 256

        @pl.loop(0, rows // step)
        def _(i):
            table[pl.ds(at + i * step, step), :] = source[
                pl.ds(start + i * step, step), :
            ].astype(jnp.float32)

    copies[0].wait()
    widen(features_at, 0, OWN, NODES)
    copies[1].wait()
    widen(rims_at, 0, 0, HALO)
    copies[2].wait()
    widen(rims_at, HALO, UPPER, HALO)
    y, x, core = lax.axis_index("y"), lax.axis_index("x"), lax.axis_index("core")
    position = 0
    for k in range(6):
        copies[3 + k].wait()
        for _ in range(HUB_PIECES[k]):
            b = [(position >> k) & 1 for k in range(5)]
            owner_y = y ^ (b[0] * 1) ^ (b[1] * 3)
            owner_x = x ^ (b[2] * 1) ^ (b[3] * 3)
            owner = owner_y * 8 + owner_x * 2 + (core ^ b[4])
            table[pl.ds(HUB_AT + owner * HUB, HUB), :] = hubs_at[
                position * HUB : (position + 1) * HUB, :
            ].astype(jnp.float32)
            position += 1

    def gather(nodes, count, slots):
        for n in nodes:
            total = table[pl.ds(slots[0][n], 1), :]
            for s in range(1, count):
                total = total + table[pl.ds(slots[s][n], 1), :]
            sums[pl.ds(n, 1), :] = total

    todo.visit(gather)
    cot_copy.wait()

    @pl.loop(0, NODES // BLOCK)
    def _(i):
        cut = pl.ds(i * BLOCK, BLOCK)
        parts = []
        for k in range(BLOCK // LANES):
            row = counts[pl.ds(i * (BLOCK // LANES) + k, 1), :].astype(jnp.float32)
            parts.append(jnp.broadcast_to(row, (LANES, LANES)).T)
        divisor = jnp.concatenate(parts, axis=0)
        agg = (sums[cut, :] / divisor).astype(jnp.bfloat16)
        both = jnp.concatenate([features_at[cut, :], agg], axis=1)
        z = jnp.dot(both, weights[...], preferred_element_type=jnp.float32) + bias[...]
        scale = 0.7978845608028654
        cubic = 0.044715 * scale
        squared = z * z
        t = jnp.tanh(z * (scale + cubic * squared))
        half = 0.5 * z
        rest = half * t
        act_at[cut, :] = (half + rest).astype(jnp.bfloat16)
        slope = (0.5 + 0.5 * t) + (half - rest * t) * (scale + 3 * cubic * squared)
        dz = (cot_at[cut, :].astype(jnp.float32) * slope).astype(jnp.bfloat16)
        products = lax.dot_general(
            both, dz, (((0,), (0,)), ((), ())), preferred_element_type=jnp.float32
        )
        grads[0:F, :] += products[:F]
        grads[HALF : HALF + F, :] += products[F:]
        grads[F:HALF, :] += jnp.sum(
            dz.astype(jnp.float32).reshape(BLOCK // 8, 8, H), axis=0
        )
        back = lax.dot_general(
            dz, weights[...], (((1,), (1,)), ((), ())), preferred_element_type=jnp.float32
        )
        base_at[cut, :] = back[:, :F]
        src_at[cut, :] = back[:, F:] / divisor
        for k, (here, there) in enumerate(((act_at, act), (src_at, src), (base_at, base))):
            pltpu.make_async_copy(here.at[cut], there.at[cut], sem_out.at[k]).start()

    for k, (here, there) in enumerate(((act_at, act), (src_at, src), (base_at, base))):
        pltpu.make_async_copy(here, there, sem_out.at[k]).wait()


def forward(lists, features, lower, upper, hubs, counts, w_self, w_neigh, bias, cot):
    return pl.pallas_call(
        forward_kernel,
        out_shape=(
            jax.ShapeDtypeStruct((NODES, H), jnp.bfloat16),
            jax.ShapeDtypeStruct((NODES, F), jnp.float32),
            jax.ShapeDtypeStruct((NODES, F), jnp.float32),
            jax.ShapeDtypeStruct((2 * HALF, H), jnp.float32),
        ),
        in_specs=list_specs + [hbm] * (3 + len(hubs)) + [vmem] * 4 + [hbm],
        out_specs=(hbm, hbm, hbm, vmem),
        scratch_shapes=[
            pltpu.VMEM((EXTENT, F), jnp.float32),
            pltpu.VMEM((NODES, F), jnp.float32),
            pltpu.VMEM((NODES, F), jnp.bfloat16),
            pltpu.VMEM((2 * HALO, F), jnp.bfloat16),
            pltpu.VMEM((HUBS, F), jnp.bfloat16),
            pltpu.VMEM((NODES, H), jnp.bfloat16),
            pltpu.VMEM((NODES, H), jnp.bfloat16),
            pltpu.VMEM((NODES, F), jnp.float32),
            pltpu.VMEM((NODES, F), jnp.float32),
            pltpu.VMEM((2 * F, H), jnp.bfloat16),
        ]
        + list_scratch
        + [pltpu.SemaphoreType.DMA((10,)), pltpu.SemaphoreType.DMA((3,))],
        compiler_params=params,
        cost_estimate=cost(30),
        name="forward",
    )(*lists, features, lower, upper, *hubs, counts, w_self, w_neigh, bias, cot)


def chain_sum(chains, cut):
    out = chains[0][cut, :]
    for chain in chains[1:]:
        out = out + chain[cut, :]
    return out


def scatter_kernel(kind, ends, perm, slots, src, *refs):
    if kind == "own":
        base, refs = refs[0], refs[1:]
    outs, refs = refs[: 2 if kind == "hub" else 1], refs[2 if kind == "hub" else 1 :]
    lists_at, (src_at, out_at, sems), chains = refs[: FANOUT + 2], refs[FANOUT + 2 : FANOUT + 5], refs[
        FANOUT + 5 :
    ]
    todo = Lists(kind == "rim", ends, perm, slots, *lists_at)
    src_copy = pltpu.make_async_copy(src, src_at, sems.at[0])
    src_copy.start()
    rows = out_at.shape[0]
    if kind == "own":
        base_copy = pltpu.make_async_copy(base, chains[0], sems.at[1])
        base_copy.start()
    for chain in chains[1 if kind == "own" else 0 :]:
        clear(chain, 0, rows)
    if kind == "own":
        base_copy.wait()
    src_copy.wait()

    def scatter(nodes, count, slots):
        turn = 0
        for n in nodes:
            row = src_at[pl.ds(n, 1), :]
            for s in range(count):
                chain = chains[turn % len(chains)]
                turn += 1
                at = pl.ds(slots[s][n], 1)
                chain[at, :] = chain[at, :] + row

    todo.visit(scatter)

    part = rows // len(outs)
    for half, out in enumerate(outs):

        @pl.loop(0, part // HUB)
        def _(i, half=half, out=out):
            if kind == "hub":
                core = lax.axis_index("core") ^ half
                taken = (((i & 3) * 4) + (i >> 2)) * 2 + core
            else:
                taken = i
            to = pl.ds(i * HUB, HUB)
            at = pl.ds(half * part + i * HUB, HUB)
            out_at[at, :] = chain_sum(chains, pl.ds(taken * HUB, HUB)).astype(out_at.dtype)
            pltpu.make_async_copy(out_at.at[at], out.at[to], sems.at[2 + half]).start()

    for half, out in enumerate(outs):
        at = pl.ds(half * part, part)
        pltpu.make_async_copy(out_at.at[at], out, sems.at[2 + half]).wait()


def scatter(kind, rows, dtype, us, chains, lists, *inputs):
    parts = 2 if kind == "hub" else 1
    return pl.pallas_call(
        functools.partial(scatter_kernel, kind),
        out_shape=(jax.ShapeDtypeStruct((rows // parts, F), dtype),) * parts,
        in_specs=list_specs + [hbm] * len(inputs),
        out_specs=(hbm,) * parts,
        scratch_shapes=list_scratch
        + [
            pltpu.VMEM((NODES, F), jnp.float32),
            pltpu.VMEM((rows, F), dtype),
            pltpu.SemaphoreType.DMA((4,)),
        ]
        + [pltpu.VMEM((rows, F), jnp.float32)] * chains,
        compiler_params=params,
        cost_estimate=cost(us),
        name=kind + "_scatter",
    )(*lists, *inputs)


def finish_kernel(hub_rows, own, from_above, from_below, share, out, total, sem):
    copy = pltpu.make_async_copy(own, total, sem)
    copy.start()
    step = 256
    copy.wait()

    @pl.loop(0, HALO // step)
    def _(i):
        cut = pl.ds(i * step, step)
        total[cut, :] = total[cut, :] + from_above[cut, :].astype(jnp.float32)
        low = pl.ds(NODES - HALO + i * step, step)
        total[low, :] = total[low, :] + from_below[cut, :].astype(jnp.float32)

    @pl.loop(0, HUB // 16)
    def _(i):
        for u in range(16):
            at = pl.ds(hub_rows[i * 16 + u], 1)
            total[at, :] = total[at, :] + share[pl.ds(i * 16 + u, 1), :]

    @pl.loop(0, NODES // step)
    def _(i):
        cut = pl.ds(i * step, step)
        out[cut, :] = total[cut, :].astype(jnp.bfloat16)


def finish(hub_rows, own, from_above, from_below, share):
    return pl.pallas_call(
        finish_kernel,
        out_shape=jax.ShapeDtypeStruct((NODES, F), jnp.bfloat16),
        in_specs=[smem, hbm] + [vmem] * 3,
        out_specs=vmem,
        scratch_shapes=[pltpu.VMEM((NODES, F), jnp.float32), pltpu.SemaphoreType.DMA],
        compiler_params=params,
        cost_estimate=cost(3),
        name="finish",
    )(hub_rows, own, from_above, from_below, share)


def swap(value, axis, flip):
    count = lax.axis_size(axis)
    return lax.ppermute(value, axis, [(i, i ^ flip) for i in range(count)])


def shifted(value, axis, by):
    count = lax.axis_size(axis)
    pairs = [(i, i + by) for i in range(count) if 0 <= i + by < count]
    return lax.ppermute(value, axis, pairs)


def halves(value, bit):
    rows = value.shape[0] // 2
    keep = lax.dynamic_slice_in_dim(value, bit * rows, rows, axis=0)
    give = lax.dynamic_slice_in_dim(value, (1 - bit) * rows, rows, axis=0)
    return keep, give


def halve(value, axis, flip, bit):
    keep, give = halves(value, bit)
    return keep, swap(give.astype(jnp.bfloat16), axis, flip)


def plus(keep, got):
    return keep.astype(jnp.float32) + got.astype(jnp.float32)


def tie(*values):
    return lax.optimization_barrier(values)


def on_device(features, neighbors, counts, hub_rows, w_self, w_neigh, out_bias, cotangent):
    x, y, core = lax.axis_index("x"), lax.axis_index("y"), lax.axis_index("core")
    counts = counts.reshape(ROWS, LANES)

    h0 = pick_hubs(hub_rows, features)
    h1 = swap(h0, "y", 1)
    flat, perm, ends = plan(all_plan_kernel, (tiles, tile, line), 4, neighbors.T, counts)
    all_lists = lists(perm, ends, flat)
    h1, flat, features = tie(h1, flat, features)
    held = jnp.concatenate([h0, h1], axis=0)
    h2 = swap(held, "y", 3)
    lower = shifted(features[NODES - HALO :], "z", 1)
    upper = shifted(features[:HALO], "z", -1)
    h2, flat = tie(h2, flat)
    held = jnp.concatenate([held, h2], axis=0)
    h3 = swap(held, "x", 1)
    slots, perm, ends = plan(hub_plan_kernel, (tiles, tile, line), 4, flat, counts)
    hub_lists = lists(perm, ends, slots)
    h3, lower, upper, flat, *hub_lists = tie(h3, lower, upper, flat, *hub_lists)
    held = jnp.concatenate([held, h3], axis=0)
    h4 = swap(held, "x", 3)
    slots, perm, ends, own_perm, own_ends = plan(
        rim_plan_kernel, (tiles, tile, line, tile, line), 5, flat, counts
    )
    rim_lists = lists(perm, ends, slots)
    own_lists = lists(own_perm, own_ends, slots)
    h4, rim_lists, own_lists = tie(h4, rim_lists, own_lists)
    held = jnp.concatenate([held, h4], axis=0)
    h5 = swap(held, "core", 1)

    act, src, base, grads = forward(
        all_lists, features, lower, upper, (h0, h1, h2, h3, h4, h5), counts,
        w_self, w_neigh, out_bias.reshape(1, H), cotangent,
    )

    other = swap(grads, "z", 1)
    keep, give = scatter("hub", HUBS, jnp.bfloat16, 8, 6, hub_lists, src)
    keep, give, src, other = tie(keep, give, src, other)
    grads = grads + other
    got = swap(give, "core", 1)
    other = swap(grads, "z", 3)
    got, src = tie(got, src)
    keep, got = halve(plus(keep, got), "x", 3, x // 2)
    (rim,) = scatter("rim", 2 * HALO, jnp.bfloat16, 8, 6, rim_lists, src)
    keep, got, src, other, rim = tie(keep, got, src, other, rim)

    grads, give = halves(grads + other, core)
    other = swap(give, "core", 1)
    keep, got = halve(plus(keep, got), "x", 1, x % 2)
    other, src = tie(other, src)
    grads = grads + other
    other = swap(grads, "x", 3)
    (own,) = scatter("own", NODES, jnp.float32, 20, CHAINS, own_lists, src, base)
    keep, got, other, rim, own = tie(keep, got, other, rim, own)

    keep, got = halve(plus(keep, got), "y", 3, y // 2)
    grads = grads + other
    other = swap(grads, "x", 1)
    from_below = shifted(rim[:HALO], "z", -1)
    from_above = shifted(rim[HALO:], "z", 1)
    keep, got, other, from_below, from_above = tie(keep, got, other, from_below, from_above)
    keep, got = halve(plus(keep, got), "y", 1, y % 2)
    grads = grads + other
    other = swap(grads, "y", 3)
    keep, got, other = tie(keep, got, other)
    grads = grads + other
    other = swap(grads, "y", 1)
    grad_features = finish(hub_rows, own, from_above, from_below, plus(keep, got))
    other, grad_features = tie(other, grad_features)
    grads = grads + other
    other = swap(grads, "core", 1)
    first = jnp.where(core == 0, grads, other)
    second = jnp.where(core == 0, other, grads)
    return act, grad_features, first[:F], second[:F], jnp.sum(first[F:], axis=0)


def solution(mesh):
    mesh = Mesh(mesh.devices.reshape(4, 4, 4, 2), AXES)
    rows = P(AXES, None)
    placed = (rows, rows, P(AXES), P(AXES), P(), P(), P(), rows)
    return jax.shard_map(
        on_device,
        mesh=mesh,
        in_specs=placed,
        out_specs=(rows, rows, P(), P(), P()),
        check_vma=False,
    )
```

```python
import functools

import jax
import jax.numpy as jnp
from jax import lax
from jax.experimental import pallas as pl
from jax.experimental.pallas import tpu as pltpu
from jax.sharding import Mesh, PartitionSpec as P

F = 128
H = 256
NODES = 4096
HALO = 1024
HUB = 128
FANOUT = 10
COLS = 32
HUBS = HUB * COLS
OWN = HALO
UPPER = HALO + NODES
HUB_AT = 2 * HALO + NODES
EXTENT = HUB_AT + HUBS
LANES = 128
CHAINS = 8
VMEM_BYTES = 60 * 2**20
HALF = F + 8
AXES = ("z", "y", "x", "core")

smem = pl.BlockSpec(memory_space=pltpu.SMEM)
vmem = pl.BlockSpec(memory_space=pltpu.VMEM)
hbm = pl.BlockSpec(memory_space=pltpu.HBM)
anywhere = pl.BlockSpec(memory_space=pl.ANY)
params = pltpu.CompilerParams(vmem_limit_bytes=VMEM_BYTES)


def group_of(count):
    return 16 if count <= 3 else 8


def cost(us):
    return pl.CostEstimate(flops=int(us * 1e9), bytes_accessed=0, transcendentals=0)


def faces_up(half):
    return (lax.axis_index("z") & 1) ^ (1 - half)


def hub_kernel(hub_rows, features, out, *refs):
    rims, (here, wide, rows, sems) = refs[:2], refs[2:]
    part = NODES // 4
    copies = []
    for k in range(4):
        cut = pl.ds(k * part, part)
        copies.append(pltpu.make_async_copy(features.at[cut], here.at[cut], sems.at[k]))
        copies[k].start()
    for k in range(4):
        copies[k].wait()

        @pl.loop(0, part // 512)
        def _(i, k=k):
            cut = pl.ds(k * part + i * 512, 512)
            wide[cut, :] = here[cut, :].astype(jnp.float32)

    sends = []
    for half in range(2):
        at = pl.multiple_of(faces_up(half) * (NODES - HALO), HALO)
        sends.append(
            pltpu.make_async_copy(here.at[pl.ds(at, HALO)], rims[half], sems.at[4 + half])
        )
        sends[half].start()

    @pl.loop(0, HUB // 16)
    def _(i):
        for u in range(16):
            rows[pl.ds(i * 16 + u, 1), :] = wide[pl.ds(hub_rows[i * 16 + u], 1), :]

    out[...] = rows[...].astype(jnp.bfloat16)
    for send in sends:
        send.wait()


def pick_hubs(hub_rows, features):
    return pl.pallas_call(
        hub_kernel,
        out_shape=(jax.ShapeDtypeStruct((HUB, F), jnp.bfloat16),)
        + (jax.ShapeDtypeStruct((HALO, F), jnp.bfloat16),) * 2,
        in_specs=[smem, hbm],
        out_specs=(vmem, hbm, hbm),
        scratch_shapes=[
            pltpu.VMEM((NODES, F), jnp.bfloat16),
            pltpu.VMEM((NODES, F), jnp.float32),
            pltpu.VMEM((HUB, F), jnp.float32),
            pltpu.SemaphoreType.DMA((6,)),
        ],
        compiler_params=params,
        cost_estimate=cost(2),
        name="pick_hubs",
    )(hub_rows, features)


ROWS = NODES // LANES


def order_by(count, order):
    lane_r = lax.broadcasted_iota(jnp.int32, (LANES, LANES), 0)
    lane_c = lax.broadcasted_iota(jnp.int32, (LANES, LANES), 1)
    before = (lane_r < lane_c).astype(jnp.bfloat16)
    row_r = lax.broadcasted_iota(jnp.int32, (ROWS, ROWS), 0)
    row_c = lax.broadcasted_iota(jnp.int32, (ROWS, ROWS), 1)
    above = (row_c < row_r).astype(jnp.bfloat16)
    lane = lax.broadcasted_iota(jnp.int32, (1, LANES), 1)
    hits = [(count == c).astype(jnp.float32) for c in range(FANOUT + 1)]
    stacked = jnp.concatenate(hits, axis=0).astype(jnp.bfloat16)
    in_rows = jnp.dot(stacked, before, preferred_element_type=jnp.float32)
    place = jnp.zeros((ROWS, LANES), jnp.float32)
    start = jnp.zeros((1, 1), jnp.float32)
    end_row = jnp.zeros((1, LANES), jnp.float32)
    for c in range(FANOUT + 1):
        hit = hits[c]
        per_row = jnp.sum(hit, axis=1, keepdims=True)
        earlier = jnp.dot(
            above,
            jnp.broadcast_to(per_row, (ROWS, LANES)).astype(jnp.bfloat16),
            preferred_element_type=jnp.float32,
        )
        in_row = in_rows[c * ROWS : (c + 1) * ROWS]
        place = place + hit * (in_row + earlier + start)
        start = start + jnp.sum(per_row, axis=0, keepdims=True)
        end_row = end_row + jnp.where(lane == c, start, 0.0)
    place = place.astype(jnp.int32)
    high = place >> 7
    low = place & (LANES - 1)
    slot_row = lax.broadcasted_iota(jnp.int32, (ROWS, LANES), 0)
    slot_lane = lax.broadcasted_iota(jnp.int32, (LANES, LANES), 0)
    own_lane = lax.broadcasted_iota(jnp.int32, (ROWS, LANES), 1).astype(jnp.float32)
    total = jnp.zeros((ROWS, LANES), jnp.float32)
    for r in range(ROWS):
        to_row = (high[r : r + 1, :] == slot_row).astype(jnp.float32)
        to_lane = (low[r : r + 1, :] == slot_lane).astype(jnp.bfloat16)
        both = jnp.concatenate([to_row * own_lane, to_row * float(r)], axis=0)
        found = lax.dot_general(
            both.astype(jnp.bfloat16),
            to_lane,
            (((1,), (1,)), ((), ())),
            preferred_element_type=jnp.float32,
        )
        total = total + found[:ROWS] + found[ROWS:] * float(LANES)
    order[0:ROWS, :] = total.astype(jnp.int32)
    order[ROWS : ROWS + 8, :] = jnp.broadcast_to(end_row, (8, LANES)).astype(jnp.int32)


def compact(flat, count, is_kind, value, backwards, placed):
    found = jnp.zeros((ROWS, LANES), jnp.int32)
    for s in range(FANOUT):
        row = flat[s * ROWS : (s + 1) * ROWS, :]
        hit = jnp.logical_and(count > s, is_kind(row))
        at = jnp.where(hit, found, -1)
        for k in range(s + 1):
            place = FANOUT - 1 - k if backwards else k
            placed[place] = jnp.where(at == k, value(row), placed[place])
        found = found + hit.astype(jnp.int32)
    return found


def nothing_placed():
    return [jnp.zeros((ROWS, LANES), jnp.int32) for _ in range(FANOUT)]


def is_own(row):
    return jnp.logical_and(row >= OWN, row < UPPER)


def is_rim(row):
    return jnp.logical_or(row < OWN, jnp.logical_and(row >= UPPER, row < HUB_AT))


def all_plan_kernel(neighbors, counts, flat, order):
    for s in range(FANOUT):
        for r in range(ROWS):
            at = s * ROWS + r
            flat[at : at + 1, :] = neighbors[s : s + 1, r * LANES : (r + 1) * LANES]
    order_by(counts[...], order)


def hub_plan_kernel(flat, counts, slots, order):
    placed = nothing_placed()
    hubs = compact(
        flat, counts[...], lambda row: row >= HUB_AT, lambda row: row - HUB_AT, False, placed
    )
    for s in range(FANOUT):
        slots[s * ROWS : (s + 1) * ROWS, :] = placed[s]
    order_by(hubs, order)


def rim_plan_kernel(flat, counts, slots, order, own_order):
    placed = nothing_placed()
    owns = compact(flat, counts[...], is_own, lambda row: row - OWN, False, placed)
    rims = compact(
        flat, counts[...], is_rim, lambda row: jnp.where(row < OWN, row, row - NODES), True, placed
    )
    for s in range(FANOUT):
        slots[s * ROWS : (s + 1) * ROWS, :] = placed[s]
    order_by(rims, order)
    order_by(owns, own_order)


ORDER = NODES + 8 * LANES
ordered = jax.ShapeDtypeStruct((ROWS + 8, LANES), jnp.int32)
tiles = jax.ShapeDtypeStruct((FANOUT * ROWS, LANES), jnp.int32)


def plan(kernel, outs, us, *inputs):
    return pl.pallas_call(
        kernel,
        out_shape=outs,
        in_specs=[vmem] * len(inputs),
        out_specs=(vmem,) * len(outs),
        compiler_params=params,
        cost_estimate=cost(us),
        name=kernel.__name__,
    )(*inputs)


def lists(order, slots):
    return order.reshape(ORDER), slots.reshape(FANOUT * NODES)


list_specs = [hbm, hbm]
list_scratch = [pltpu.SMEM((ORDER,), jnp.int32)] + [pltpu.SMEM((NODES,), jnp.int32)] * FANOUT + [
    pltpu.SemaphoreType.DMA((1 + FANOUT,))
]


class Lists:
    def __init__(self, backwards, order, slots, order_at, *rest):
        slots_at, sems = rest[:FANOUT], rest[FANOUT]
        self.order, self.slots = order_at, slots_at
        self.copies = [pltpu.make_async_copy(order, order_at, sems.at[0])]
        for s in range(FANOUT):
            part = slots.at[pl.ds(s * NODES, NODES)]
            self.copies.append(pltpu.make_async_copy(part, slots_at[s], sems.at[1 + s]))
        if backwards:
            self.slots = self.slots[::-1]
            self.copies[1:] = self.copies[:0:-1]
        for copy in self.copies:
            copy.start()

    def visit(self, act):
        slots, copies = self.slots, self.copies[1:]
        self.copies[0].wait()
        for count in range(1, FANOUT + 1):
            copies[count - 1].wait()
            size = group_of(count)
            first = self.order[NODES + count - 1]
            last = self.order[NODES + count]
            groups = (last - first) // size
            rest = first + groups * size

            @pl.loop(0, groups)
            def _(g, count=count, size=size, first=first):
                at = first + g * size
                act([self.order[at + u] for u in range(size)], count, slots)

            @pl.loop(rest, last)
            def _(at, count=count):
                act([self.order[at]], count, slots)


def clear(ref, at, rows):
    step = 512

    @pl.loop(0, rows // step)
    def _(i):
        ref[pl.ds(at + i * step, step), :] = jnp.zeros((step, F), jnp.float32)


BLOCK = 512
HUB_PIECES = (1, 1, 2, 4, 8, 16)


def forward_kernel(order, slots, features, rim_up, rim_down, *refs):
    pieces, refs = refs[:6], refs[6:]
    small, cotangent, (act, src, base, grads) = refs[:4], refs[4], refs[5:9]
    table, sums, features_at, rims_at, hubs_at, cot_at, act_at, src_at, base_at = refs[9:18]
    small_at, lists_at, (sem_in, sem_out) = refs[18:21], refs[21:-2], refs[-2:]
    counts, weights, bias = small_at
    copies = [
        pltpu.make_async_copy(features, features_at, sem_in.at[0]),
        pltpu.make_async_copy(rim_up, rims_at.at[pl.ds(0, HALO)], sem_in.at[1]),
        pltpu.make_async_copy(rim_down, rims_at.at[pl.ds(HALO, HALO)], sem_in.at[2]),
    ]
    at = 0
    for k, piece in enumerate(pieces):
        rows = HUB_PIECES[k] * HUB
        copies.append(
            pltpu.make_async_copy(piece, hubs_at.at[pl.ds(at, rows)], sem_in.at[3 + k])
        )
        at += rows
    for copy in copies:
        copy.start()
    todo = Lists(False, order, slots, *lists_at)
    cot_copy = pltpu.make_async_copy(cotangent, cot_at, sem_in.at[9])
    cot_copy.start()
    to = (counts, weights.at[pl.ds(0, F)], weights.at[pl.ds(F, F)], bias)
    late = [pltpu.make_async_copy(small[k], to[k], sem_in.at[10 + k]) for k in range(4)]
    for copy in late:
        copy.start()
    late.append(cot_copy)
    grads[...] = jnp.zeros_like(grads)

    def widen(source, start, at, rows):
        step = 256

        @pl.loop(0, rows // step)
        def _(i):
            table[pl.ds(at + i * step, step), :] = source[
                pl.ds(start + i * step, step), :
            ].astype(jnp.float32)

    copies[0].wait()
    widen(features_at, 0, OWN, NODES)
    for half in range(2):
        copies[1 + half].wait()
        widen(rims_at, half * HALO, pl.multiple_of(faces_up(half) * UPPER, HALO), HALO)
    y, x, core = lax.axis_index("y"), lax.axis_index("x"), lax.axis_index("core")
    position = 0
    for k in range(6):
        copies[3 + k].wait()
        for _ in range(HUB_PIECES[k]):
            b = [(position >> k) & 1 for k in range(5)]
            owner_y = y ^ (b[0] * 1) ^ (b[1] * 3)
            owner_x = x ^ (b[2] * 1) ^ (b[3] * 3)
            owner = owner_y * 8 + owner_x * 2 + (core ^ b[4])
            table[pl.ds(HUB_AT + owner * HUB, HUB), :] = hubs_at[
                position * HUB : (position + 1) * HUB, :
            ].astype(jnp.float32)
            position += 1

    def gather(nodes, count, slots):
        for n in nodes:
            total = table[pl.ds(slots[0][n], 1), :]
            for s in range(1, count):
                total = total + table[pl.ds(slots[s][n], 1), :]
            sums[pl.ds(n, 1), :] = total

    todo.visit(gather)
    for copy in late:
        copy.wait()

    @pl.loop(0, NODES // BLOCK)
    def _(i):
        cut = pl.ds(i * BLOCK, BLOCK)
        parts = []
        for k in range(BLOCK // LANES):
            row = counts[pl.ds(i * (BLOCK // LANES) + k, 1), :].astype(jnp.float32)
            parts.append(jnp.broadcast_to(row, (LANES, LANES)).T)
        divisor = jnp.concatenate(parts, axis=0)
        agg = (sums[cut, :] / divisor).astype(jnp.bfloat16)
        both = jnp.concatenate([features_at[cut, :], agg], axis=1)
        z = jnp.dot(both, weights[...], preferred_element_type=jnp.float32) + bias[...]
        scale = 0.7978845608028654
        cubic = 0.044715 * scale
        squared = z * z
        t = jnp.tanh(z * (scale + cubic * squared))
        half = 0.5 * z
        rest = half * t
        act_at[cut, :] = (half + rest).astype(jnp.bfloat16)
        slope = (0.5 + 0.5 * t) + (half - rest * t) * (scale + 3 * cubic * squared)
        dz = (cot_at[cut, :].astype(jnp.float32) * slope).astype(jnp.bfloat16)
        products = lax.dot_general(
            both, dz, (((0,), (0,)), ((), ())), preferred_element_type=jnp.float32
        )
        grads[0:F, :] += products[:F]
        grads[HALF : HALF + F, :] += products[F:]
        grads[F:HALF, :] += jnp.sum(
            dz.astype(jnp.float32).reshape(BLOCK // 8, 8, H), axis=0
        )
        back = lax.dot_general(
            dz, weights[...], (((1,), (1,)), ((), ())), preferred_element_type=jnp.float32
        )
        base_at[cut, :] = back[:, :F]
        src_at[cut, :] = back[:, F:] / divisor
        for k, (here, there) in enumerate(((act_at, act), (src_at, src), (base_at, base))):
            pltpu.make_async_copy(here.at[cut], there.at[cut], sem_out.at[k]).start()

    for k, (here, there) in enumerate(((act_at, act), (src_at, src), (base_at, base))):
        pltpu.make_async_copy(here, there, sem_out.at[k]).wait()


def forward(lists, features, rims, hubs, counts, w_self, w_neigh, bias, cot):
    return pl.pallas_call(
        forward_kernel,
        out_shape=(
            jax.ShapeDtypeStruct((NODES, H), jnp.bfloat16),
            jax.ShapeDtypeStruct((NODES, F), jnp.float32),
            jax.ShapeDtypeStruct((NODES, F), jnp.float32),
            jax.ShapeDtypeStruct((2 * HALF, H), jnp.float32),
        ),
        in_specs=list_specs + [anywhere] * (3 + len(hubs)) + [hbm] * 5,
        out_specs=(hbm, hbm, hbm, vmem),
        scratch_shapes=[
            pltpu.VMEM((EXTENT, F), jnp.float32),
            pltpu.VMEM((NODES, F), jnp.float32),
            pltpu.VMEM((NODES, F), jnp.bfloat16),
            pltpu.VMEM((2 * HALO, F), jnp.bfloat16),
            pltpu.VMEM((HUBS, F), jnp.bfloat16),
            pltpu.VMEM((NODES, H), jnp.bfloat16),
            pltpu.VMEM((NODES, H), jnp.bfloat16),
            pltpu.VMEM((NODES, F), jnp.float32),
            pltpu.VMEM((NODES, F), jnp.float32),
            pltpu.VMEM((ROWS, LANES), jnp.int32),
            pltpu.VMEM((2 * F, H), jnp.bfloat16),
            pltpu.VMEM((1, H), jnp.float32),
        ]
        + list_scratch
        + [pltpu.SemaphoreType.DMA((14,)), pltpu.SemaphoreType.DMA((3,))],
        compiler_params=pltpu.CompilerParams(vmem_limit_bytes=40 * 2**20),
        cost_estimate=cost(30),
        name="forward",
    )(*lists, features, *rims, *hubs, counts, w_self, w_neigh, bias, cot)


def chain_sum(chains, cut):
    out = chains[0][cut, :]
    for chain in chains[1:]:
        out = out + chain[cut, :]
    return out


def scatter_kernel(kind, order, slots, src, *refs):
    if kind == "own":
        base, refs = refs[0], refs[1:]
    parts = 1 if kind == "own" else 2
    outs, refs = refs[:parts], refs[parts:]
    lists_at, (src_at, out_at, sems), chains = refs[: FANOUT + 2], refs[FANOUT + 2 : FANOUT + 5], refs[
        FANOUT + 5 :
    ]
    todo = Lists(kind == "rim", order, slots, *lists_at)
    src_copy = pltpu.make_async_copy(src, src_at, sems.at[0])
    src_copy.start()
    rows = out_at.shape[0]
    if kind == "own":
        base_copy = pltpu.make_async_copy(base, chains[0], sems.at[1])
        base_copy.start()
    for chain in chains[1 if kind == "own" else 0 :]:
        clear(chain, 0, rows)
    if kind == "own":
        base_copy.wait()
    src_copy.wait()

    def scatter(nodes, count, slots):
        turn = 0
        for n in nodes:
            row = src_at[pl.ds(n, 1), :]
            for s in range(count):
                chain = chains[turn % len(chains)]
                turn += 1
                at = pl.ds(slots[s][n], 1)
                chain[at, :] = chain[at, :] + row

    todo.visit(scatter)

    part = rows // len(outs)
    for half, out in enumerate(outs):

        @pl.loop(0, part // HUB)
        def _(i, half=half, out=out):
            if kind == "hub":
                core = lax.axis_index("core") ^ half
                taken = (((i & 3) * 4) + (i >> 2)) * 2 + core
            elif kind == "rim":
                taken = i + faces_up(half) * (HALO // HUB)
            else:
                taken = i
            to = pl.ds(i * HUB, HUB)
            at = pl.ds(half * part + i * HUB, HUB)
            out_at[at, :] = chain_sum(chains, pl.ds(taken * HUB, HUB)).astype(out_at.dtype)
            pltpu.make_async_copy(out_at.at[at], out.at[to], sems.at[2 + half]).start()

    for half, out in enumerate(outs):
        at = pl.ds(half * part, part)
        pltpu.make_async_copy(out_at.at[at], out, sems.at[2 + half]).wait()


def scatter(kind, rows, dtype, us, chains, lists, *inputs):
    parts = 1 if kind == "own" else 2
    return pl.pallas_call(
        functools.partial(scatter_kernel, kind),
        out_shape=(jax.ShapeDtypeStruct((rows // parts, F), dtype),) * parts,
        in_specs=list_specs + [hbm] * len(inputs),
        out_specs=(hbm,) * parts,
        scratch_shapes=list_scratch
        + [
            pltpu.VMEM((NODES, F), jnp.float32),
            pltpu.VMEM((rows, F), dtype),
            pltpu.SemaphoreType.DMA((4,)),
        ]
        + [pltpu.VMEM((rows, F), jnp.float32)] * chains,
        compiler_params=params,
        cost_estimate=cost(us),
        name=kind + "_scatter",
    )(*lists, *inputs)


def finish_kernel(hub_rows, own, rim_0, rim_1, share, out, total, rims, share_at, out_at, rows, sems):
    to = (total, rims.at[pl.ds(0, HALO)], rims.at[pl.ds(HALO, HALO)], share_at, rows)
    copies = [
        pltpu.make_async_copy(source, to[k], sems.at[k])
        for k, source in enumerate((own, rim_0, rim_1, share, hub_rows))
    ]
    for copy in copies:
        copy.start()
    for copy in copies:
        copy.wait()
    step = 256
    for half in range(2):
        start = pl.multiple_of(faces_up(half) * (NODES - HALO), HALO)

        @pl.loop(0, HALO // step)
        def _(i, half=half, start=start):
            cut = pl.ds(start + i * step, step)
            rim = rims[pl.ds(half * HALO + i * step, step), :]
            total[cut, :] = total[cut, :] + rim.astype(jnp.float32)

    @pl.loop(0, HUB // 16)
    def _(i):
        for u in range(16):
            at = pl.ds(rows[i * 16 + u], 1)
            total[at, :] = total[at, :] + share_at[pl.ds(i * 16 + u, 1), :]

    @pl.loop(0, NODES // 512)
    def _(i):
        cut = pl.ds(i * 512, 512)
        out_at[cut, :] = total[cut, :].astype(jnp.bfloat16)
        pltpu.make_async_copy(out_at.at[cut], out.at[cut], sems.at[5]).start()

    pltpu.make_async_copy(out_at, out, sems.at[5]).wait()


def finish(hub_rows, own, rim_0, rim_1, share):
    return pl.pallas_call(
        finish_kernel,
        out_shape=jax.ShapeDtypeStruct((NODES, F), jnp.bfloat16),
        in_specs=[anywhere] * 5,
        out_specs=hbm,
        scratch_shapes=[
            pltpu.VMEM((NODES, F), jnp.float32),
            pltpu.VMEM((2 * HALO, F), jnp.bfloat16),
            pltpu.VMEM((HUB, F), jnp.float32),
            pltpu.VMEM((NODES, F), jnp.bfloat16),
            pltpu.SMEM((HUB,), jnp.int32),
            pltpu.SemaphoreType.DMA((6,)),
        ],
        compiler_params=pltpu.CompilerParams(vmem_limit_bytes=16 * 2**20),
        cost_estimate=cost(3),
        name="finish",
    )(hub_rows, own, rim_0, rim_1, share)


def swap(value, axis, flip):
    count = lax.axis_size(axis)
    return lax.ppermute(value, axis, [(i, i ^ flip) for i in range(count)])


def swap_rims(first, second):
    above = lax.ppermute(first, "z", [(0, 1), (1, 0), (2, 3), (3, 2)])
    return above, lax.ppermute(second, "z", [(1, 2), (2, 1)])


def halves(value, bit):
    rows = value.shape[0] // 2
    keep = lax.dynamic_slice_in_dim(value, bit * rows, rows, axis=0)
    give = lax.dynamic_slice_in_dim(value, (1 - bit) * rows, rows, axis=0)
    return keep, give


def halve(keep, got, axis, flip, bit):
    mine, other_mine = halves(keep, bit)
    theirs, other_theirs = halves(got, bit)
    give = (other_mine.astype(jnp.float32) + other_theirs.astype(jnp.float32)).astype(jnp.bfloat16)
    return plus(mine, theirs), swap(give, axis, flip)


def plus(keep, got):
    return keep.astype(jnp.float32) + got.astype(jnp.float32)


def tie(*values):
    return lax.optimization_barrier(values)


def on_device(features, neighbors, counts, hub_rows, w_self, w_neigh, out_bias, cotangent):
    x, y, core = lax.axis_index("x"), lax.axis_index("y"), lax.axis_index("core")
    counts = counts.reshape(ROWS, LANES)

    h0, *rims = pick_hubs(hub_rows, features)
    h1 = swap(h0, "y", 1)
    flat, order = plan(all_plan_kernel, (tiles, ordered), 4, neighbors.T, counts)
    all_lists = lists(order, flat)
    h1, flat = tie(h1, flat)
    held = jnp.concatenate([h0, h1], axis=0)
    h2 = swap(held, "y", 3)
    slots, order = plan(hub_plan_kernel, (tiles, ordered), 4, flat, counts)
    hub_lists = lists(order, slots)
    h2, flat, hub_lists, *rims = tie(h2, flat, hub_lists, *rims)
    held = jnp.concatenate([held, h2], axis=0)
    h3 = swap(held, "x", 1)
    rims = swap_rims(*rims)
    h3, flat = tie(h3, flat)
    held = jnp.concatenate([held, h3], axis=0)
    h4 = swap(held, "x", 3)
    slots, order, own_order = plan(rim_plan_kernel, (tiles, ordered, ordered), 5, flat, counts)
    rim_lists = lists(order, slots)
    own_lists = lists(own_order, slots)
    h4, rim_lists, own_lists, *rims = tie(h4, rim_lists, own_lists, *rims)
    held = jnp.concatenate([held, h4], axis=0)
    h5 = swap(held, "core", 1)

    act, src, base, grads = forward(
        all_lists, features, rims, (h0, h1, h2, h3, h4, h5), counts,
        w_self, w_neigh, out_bias.reshape(1, H), cotangent,
    )

    other = swap(grads, "z", 1)
    keep, give = scatter("hub", HUBS, jnp.bfloat16, 8, 6, hub_lists, src)
    keep, give, src, other = tie(keep, give, src, other)
    grads = grads + other
    got = swap(give, "core", 1)
    other = swap(grads, "z", 3)
    got, src = tie(got, src)
    keep, got = halve(keep, got, "x", 3, x // 2)
    rims = scatter("rim", 2 * HALO, jnp.bfloat16, 8, 6, rim_lists, src)
    keep, got, src, other, *rims = tie(keep, got, src, other, *rims)

    grads, give = halves(grads + other, core)
    other = swap(give, "core", 1)
    keep, got = halve(keep, got, "x", 1, x % 2)
    other, src = tie(other, src)
    grads = grads + other
    other = swap(grads, "x", 3)
    rims = swap_rims(*rims)
    (own,) = scatter("own", NODES, jnp.float32, 20, CHAINS, own_lists, src, base)
    keep, got, other, own, *rims = tie(keep, got, other, own, *rims)

    keep, got = halve(keep, got, "y", 3, y // 2)
    grads = grads + other
    other = swap(grads, "x", 1)
    keep, got, other = tie(keep, got, other)
    keep, got = halve(keep, got, "y", 1, y % 2)
    grads = grads + other
    other = swap(grads, "y", 3)
    keep, got, other = tie(keep, got, other)
    grads = grads + other
    other = swap(grads, "y", 1)
    grad_features = finish(hub_rows, own, *rims, plus(keep, got))
    other, grad_features = tie(other, grad_features)
    grads = grads + other
    other = swap(grads, "core", 1)
    first = jnp.where(core == 0, grads, other)
    second = jnp.where(core == 0, other, grads)
    return act, grad_features, first[:F], second[:F], jnp.sum(first[F:], axis=0)


def solution(mesh):
    mesh = Mesh(mesh.devices.reshape(4, 4, 4, 2), AXES)
    rows = P(AXES, None)
    placed = (rows, rows, P(AXES), P(AXES), P(), P(), P(), rows)
    return jax.shard_map(
        on_device,
        mesh=mesh,
        in_specs=placed,
        out_specs=(rows, rows, P(), P(), P()),
        check_vma=False,
    )
```

```python
import functools

import jax
import jax.numpy as jnp
from jax import lax
from jax.experimental import pallas as pl
from jax.experimental.pallas import tpu as pltpu
from jax.sharding import Mesh, PartitionSpec as P

F = 128
H = 256
NODES = 4096
HALO = 1024
HUB = 128
FANOUT = 10
COLS = 32
HUBS = HUB * COLS
OWN = HALO
UPPER = HALO + NODES
HUB_AT = 2 * HALO + NODES
EXTENT = HUB_AT + HUBS
LANES = 128
CHAINS = 8
VMEM_BYTES = 60 * 2**20
HALF = F + 8
AXES = ("z", "y", "x", "core")

smem = pl.BlockSpec(memory_space=pltpu.SMEM)
vmem = pl.BlockSpec(memory_space=pltpu.VMEM)
hbm = pl.BlockSpec(memory_space=pltpu.HBM)
anywhere = pl.BlockSpec(memory_space=pl.ANY)
params = pltpu.CompilerParams(vmem_limit_bytes=VMEM_BYTES)


def group_of(count):
    return 16 if count <= 3 else 8


def wide_group_of(count):
    return 32 if count == 1 else 16


def cost(us):
    return pl.CostEstimate(flops=int(us * 1e9), bytes_accessed=0, transcendentals=0)


def faces_up(half):
    return (lax.axis_index("z") & 1) ^ (1 - half)


def faces_up(half):
    return (lax.axis_index("z") & 1) ^ (1 - half)


def hub_kernel(hub_rows, features, out, wide, rows):
    @pl.loop(0, NODES // 512)
    def _(i):
        cut = pl.ds(i * 512, 512)
        wide[cut, :] = features[cut, :].astype(jnp.float32)

    @pl.loop(0, HUB // 16)
    def _(i):
        for u in range(16):
            rows[pl.ds(i * 16 + u, 1), :] = wide[pl.ds(hub_rows[i * 16 + u], 1), :]

    out[...] = rows[...].astype(jnp.bfloat16)


def pick_hubs(hub_rows, features):
    return pl.pallas_call(
        hub_kernel,
        out_shape=jax.ShapeDtypeStruct((HUB, F), jnp.bfloat16),
        in_specs=[smem, vmem],
        out_specs=vmem,
        scratch_shapes=[pltpu.VMEM((NODES, F), jnp.float32), pltpu.VMEM((HUB, F), jnp.float32)],
        compiler_params=params,
        cost_estimate=cost(2),
        name="pick_hubs",
    )(hub_rows, features)


ROWS = NODES // LANES


def order_by(count, order):
    lane_r = lax.broadcasted_iota(jnp.int32, (LANES, LANES), 0)
    lane_c = lax.broadcasted_iota(jnp.int32, (LANES, LANES), 1)
    before = (lane_r < lane_c).astype(jnp.bfloat16)
    row_r = lax.broadcasted_iota(jnp.int32, (ROWS, ROWS), 0)
    row_c = lax.broadcasted_iota(jnp.int32, (ROWS, ROWS), 1)
    above = (row_c < row_r).astype(jnp.bfloat16)
    lane = lax.broadcasted_iota(jnp.int32, (1, LANES), 1)
    hits = [(count == c).astype(jnp.float32) for c in range(FANOUT + 1)]
    stacked = jnp.concatenate(hits, axis=0).astype(jnp.bfloat16)
    in_rows = jnp.dot(stacked, before, preferred_element_type=jnp.float32)
    place = jnp.zeros((ROWS, LANES), jnp.float32)
    start = jnp.zeros((1, 1), jnp.float32)
    end_row = jnp.zeros((1, LANES), jnp.float32)
    for c in range(FANOUT + 1):
        hit = hits[c]
        per_row = jnp.sum(hit, axis=1, keepdims=True)
        earlier = jnp.dot(
            above,
            jnp.broadcast_to(per_row, (ROWS, LANES)).astype(jnp.bfloat16),
            preferred_element_type=jnp.float32,
        )
        in_row = in_rows[c * ROWS : (c + 1) * ROWS]
        place = place + hit * (in_row + earlier + start)
        start = start + jnp.sum(per_row, axis=0, keepdims=True)
        end_row = end_row + jnp.where(lane == c, start, 0.0)
    place = place.astype(jnp.int32)
    high = place >> 7
    low = place & (LANES - 1)
    slot_row = lax.broadcasted_iota(jnp.int32, (ROWS, LANES), 0)
    slot_lane = lax.broadcasted_iota(jnp.int32, (LANES, LANES), 0)
    own_lane = lax.broadcasted_iota(jnp.int32, (ROWS, LANES), 1).astype(jnp.float32)
    total = jnp.zeros((ROWS, LANES), jnp.float32)
    for r in range(ROWS):
        to_row = (high[r : r + 1, :] == slot_row).astype(jnp.float32)
        to_lane = (low[r : r + 1, :] == slot_lane).astype(jnp.bfloat16)
        both = jnp.concatenate([to_row * own_lane, to_row * float(r)], axis=0)
        found = lax.dot_general(
            both.astype(jnp.bfloat16),
            to_lane,
            (((1,), (1,)), ((), ())),
            preferred_element_type=jnp.float32,
        )
        total = total + found[:ROWS] + found[ROWS:] * float(LANES)
    order[0:ROWS, :] = total.astype(jnp.int32)
    order[ROWS : ROWS + 8, :] = jnp.broadcast_to(end_row, (8, LANES)).astype(jnp.int32)


def compact(flat, count, is_kind, value, backwards, placed):
    found = jnp.zeros((ROWS, LANES), jnp.int32)
    for s in range(FANOUT):
        row = flat[s * ROWS : (s + 1) * ROWS, :]
        hit = jnp.logical_and(count > s, is_kind(row))
        at = jnp.where(hit, found, -1)
        for k in range(s + 1):
            place = FANOUT - 1 - k if backwards else k
            placed[place] = jnp.where(at == k, value(row), placed[place])
        found = found + hit.astype(jnp.int32)
    return found


def nothing_placed():
    return [jnp.zeros((ROWS, LANES), jnp.int32) for _ in range(FANOUT)]


def is_own(row):
    return jnp.logical_and(row >= OWN, row < UPPER)


def is_rim(row):
    return jnp.logical_or(row < OWN, jnp.logical_and(row >= UPPER, row < HUB_AT))


def all_plan_kernel(neighbors, counts, flat, order):
    for s in range(FANOUT):
        for r in range(ROWS):
            at = s * ROWS + r
            flat[at : at + 1, :] = neighbors[s : s + 1, r * LANES : (r + 1) * LANES]
    order_by(counts[...], order)


def hub_plan_kernel(flat, counts, slots, order):
    placed = nothing_placed()
    hubs = compact(
        flat, counts[...], lambda row: row >= HUB_AT, lambda row: row - HUB_AT, False, placed
    )
    for s in range(FANOUT):
        slots[s * ROWS : (s + 1) * ROWS, :] = placed[s]
    order_by(hubs, order)


def rim_plan_kernel(flat, counts, slots, order, own_order):
    placed = nothing_placed()
    owns = compact(flat, counts[...], is_own, lambda row: row - OWN, False, placed)
    rims = compact(
        flat, counts[...], is_rim, lambda row: jnp.where(row < OWN, row, row - NODES), True, placed
    )
    for s in range(FANOUT):
        slots[s * ROWS : (s + 1) * ROWS, :] = placed[s]
    order_by(rims, order)
    order_by(owns, own_order)


ORDER = NODES + 8 * LANES
ordered = jax.ShapeDtypeStruct((ROWS + 8, LANES), jnp.int32)
tiles = jax.ShapeDtypeStruct((FANOUT * ROWS, LANES), jnp.int32)


def plan(kernel, outs, us, *inputs):
    return pl.pallas_call(
        kernel,
        out_shape=outs,
        in_specs=[vmem] * len(inputs),
        out_specs=(vmem,) * len(outs),
        compiler_params=params,
        cost_estimate=cost(us),
        name=kernel.__name__,
    )(*inputs)


def lists(order, slots):
    return order.reshape(ORDER), slots.reshape(FANOUT * NODES)


list_specs = [hbm, hbm]
list_scratch = [pltpu.SMEM((ORDER,), jnp.int32)] + [pltpu.SMEM((NODES,), jnp.int32)] * FANOUT + [
    pltpu.SemaphoreType.DMA((1 + FANOUT,))
]


class Lists:
    def __init__(self, backwards, order, slots, order_at, *rest):
        slots_at, sems = rest[:FANOUT], rest[FANOUT]
        self.order, self.slots = order_at, slots_at
        self.copies = [pltpu.make_async_copy(order, order_at, sems.at[0])]
        for s in range(FANOUT):
            part = slots.at[pl.ds(s * NODES, NODES)]
            self.copies.append(pltpu.make_async_copy(part, slots_at[s], sems.at[1 + s]))
        if backwards:
            self.slots = self.slots[::-1]
            self.copies[1:] = self.copies[:0:-1]
        for copy in self.copies:
            copy.start()

    def visit(self, act, group_of):
        slots, copies = self.slots, self.copies[1:]
        self.copies[0].wait()
        for count in range(1, FANOUT + 1):
            copies[count - 1].wait()
            size = group_of(count)
            first = self.order[NODES + count - 1]
            last = self.order[NODES + count]
            groups = (last - first) // size
            rest = first + groups * size

            @pl.loop(0, groups)
            def _(g, count=count, size=size, first=first):
                at = first + g * size
                act([self.order[at + u] for u in range(size)], count, slots)

            @pl.loop(rest, last)
            def _(at, count=count):
                act([self.order[at]], count, slots)


def clear(ref, at, rows):
    step = 512

    @pl.loop(0, rows // step)
    def _(i):
        ref[pl.ds(at + i * step, step), :] = jnp.zeros((step, F), jnp.float32)


BLOCK = 1024
HUB_PIECES = (1, 1, 2, 4, 8, 16)


def forward_kernel(order, slots, features, rim_up, rim_down, *refs):
    pieces, refs = refs[:6], refs[6:]
    small, cotangent, (act, src, base, grads) = refs[:4], refs[4], refs[5:9]
    table, sums, features_at, rims_at, hubs_at, cot_at, act_at, src_at, base_at = refs[9:18]
    small_at, lists_at, (sem_in, sem_out) = refs[18:21], refs[21:-2], refs[-2:]
    counts, weights, bias = small_at
    copies = [
        pltpu.make_async_copy(features, features_at, sem_in.at[0]),
        pltpu.make_async_copy(rim_up, rims_at.at[pl.ds(0, HALO)], sem_in.at[1]),
        pltpu.make_async_copy(rim_down, rims_at.at[pl.ds(HALO, HALO)], sem_in.at[2]),
    ]
    at = 0
    for k, piece in enumerate(pieces):
        rows = HUB_PIECES[k] * HUB
        copies.append(
            pltpu.make_async_copy(piece, hubs_at.at[pl.ds(at, rows)], sem_in.at[3 + k])
        )
        at += rows
    for copy in copies:
        copy.start()
    todo = Lists(False, order, slots, *lists_at)
    cot_copy = pltpu.make_async_copy(cotangent, cot_at, sem_in.at[9])
    cot_copy.start()
    to = (counts, weights.at[pl.ds(0, F)], weights.at[pl.ds(F, F)], bias)
    late = [pltpu.make_async_copy(small[k], to[k], sem_in.at[10 + k]) for k in range(4)]
    for copy in late:
        copy.start()
    late.append(cot_copy)
    grads[...] = jnp.zeros_like(grads)
    self_at = pl.multiple_of(lax.axis_index("core") * HALF, 8)
    neigh_at = pl.multiple_of((1 - lax.axis_index("core")) * HALF, 8)

    def widen(source, start, at, rows):
        step = 256

        @pl.loop(0, rows // step)
        def _(i):
            table[pl.ds(at + i * step, step), :] = source[
                pl.ds(start + i * step, step), :
            ].astype(jnp.float32)

    copies[0].wait()
    widen(features_at, 0, OWN, NODES)
    for half in range(2):
        copies[1 + half].wait()
        widen(rims_at, half * HALO, pl.multiple_of(faces_up(half) * UPPER, HALO), HALO)
    y, x, core = lax.axis_index("y"), lax.axis_index("x"), lax.axis_index("core")
    position = 0
    for k in range(6):
        copies[3 + k].wait()
        for _ in range(HUB_PIECES[k]):
            b = [(position >> k) & 1 for k in range(5)]
            owner_y = y ^ (b[0] * 1) ^ (b[1] * 3)
            owner_x = x ^ (b[2] * 1) ^ (b[3] * 3)
            owner = owner_y * 8 + owner_x * 2 + (core ^ b[4])
            table[pl.ds(HUB_AT + owner * HUB, HUB), :] = hubs_at[
                position * HUB : (position + 1) * HUB, :
            ].astype(jnp.float32)
            position += 1

    def gather(nodes, count, slots):
        for n in nodes:
            total = table[pl.ds(slots[0][n], 1), :]
            for s in range(1, count):
                total = total + table[pl.ds(slots[s][n], 1), :]
            sums[pl.ds(n, 1), :] = total

    todo.visit(gather, wide_group_of)
    for copy in late:
        copy.wait()

    @pl.loop(0, NODES // BLOCK)
    def _(i):
        cut = pl.ds(i * BLOCK, BLOCK)
        parts = []
        for k in range(BLOCK // LANES):
            row = counts[pl.ds(i * (BLOCK // LANES) + k, 1), :].astype(jnp.float32)
            parts.append(jnp.broadcast_to(row, (LANES, LANES)).T)
        divisor = jnp.concatenate(parts, axis=0)
        agg = (sums[cut, :] / divisor).astype(jnp.bfloat16)
        both = jnp.concatenate([features_at[cut, :], agg], axis=1)
        z = jnp.dot(both, weights[...], preferred_element_type=jnp.float32) + bias[...]
        scale = 0.7978845608028654
        cubic = 0.044715 * scale
        squared = z * z
        t = jnp.tanh(z * (scale + cubic * squared))
        half = 0.5 * z
        rest = half * t
        act_at[cut, :] = (half + rest).astype(jnp.bfloat16)
        slope = (0.5 + 0.5 * t) + (half - rest * t) * (scale + 3 * cubic * squared)
        dz = (cot_at[cut, :].astype(jnp.float32) * slope).astype(jnp.bfloat16)
        products = lax.dot_general(
            both, dz, (((0,), (0,)), ((), ())), preferred_element_type=jnp.float32
        )
        grads[pl.ds(self_at, F), :] += products[:F]
        grads[pl.ds(neigh_at, F), :] += products[F:]
        grads[pl.ds(self_at + F, 8), :] += jnp.sum(
            dz.astype(jnp.float32).reshape(BLOCK // 8, 8, H), axis=0
        )
        back = lax.dot_general(
            dz, weights[...], (((1,), (1,)), ((), ())), preferred_element_type=jnp.float32
        )
        base_at[cut, :] = back[:, :F]
        src_at[cut, :] = back[:, F:] / divisor
        for k, (here, there) in enumerate(((act_at, act), (src_at, src), (base_at, base))):
            pltpu.make_async_copy(here.at[cut], there.at[cut], sem_out.at[k]).start()

    for k, (here, there) in enumerate(((act_at, act), (src_at, src), (base_at, base))):
        pltpu.make_async_copy(here, there, sem_out.at[k]).wait()


def forward(lists, features, rims, hubs, counts, w_self, w_neigh, bias, cot):
    return pl.pallas_call(
        forward_kernel,
        out_shape=(
            jax.ShapeDtypeStruct((NODES, H), jnp.bfloat16),
            jax.ShapeDtypeStruct((NODES, F), jnp.float32),
            jax.ShapeDtypeStruct((NODES, F), jnp.float32),
            jax.ShapeDtypeStruct((2 * HALF, H), jnp.float32),
        ),
        in_specs=list_specs + [hbm] * (3 + len(hubs)) + [hbm] * 5,
        out_specs=(hbm, hbm, hbm, vmem),
        scratch_shapes=[
            pltpu.VMEM((EXTENT, F), jnp.float32),
            pltpu.VMEM((NODES, F), jnp.float32),
            pltpu.VMEM((NODES, F), jnp.bfloat16),
            pltpu.VMEM((2 * HALO, F), jnp.bfloat16),
            pltpu.VMEM((HUBS, F), jnp.bfloat16),
            pltpu.VMEM((NODES, H), jnp.bfloat16),
            pltpu.VMEM((NODES, H), jnp.bfloat16),
            pltpu.VMEM((NODES, F), jnp.float32),
            pltpu.VMEM((NODES, F), jnp.float32),
            pltpu.VMEM((ROWS, LANES), jnp.int32),
            pltpu.VMEM((2 * F, H), jnp.bfloat16),
            pltpu.VMEM((1, H), jnp.float32),
        ]
        + list_scratch
        + [pltpu.SemaphoreType.DMA((14,)), pltpu.SemaphoreType.DMA((3,))],
        compiler_params=params,
        cost_estimate=cost(30),
        name="forward",
    )(*lists, features, *rims, *hubs, counts, w_self, w_neigh, bias, cot)


def chain_sum(chains, cut):
    out = chains[0][cut, :]
    for chain in chains[1:]:
        out = out + chain[cut, :]
    return out


def scatter_kernel(kind, order, slots, src, *refs):
    if kind == "own":
        base, refs = refs[0], refs[1:]
    parts = 1 if kind == "own" else 2
    outs, refs = refs[:parts], refs[parts:]
    lists_at, (src_at, out_at, sems), chains = refs[: FANOUT + 2], refs[FANOUT + 2 : FANOUT + 5], refs[
        FANOUT + 5 :
    ]
    todo = Lists(kind == "rim", order, slots, *lists_at)
    src_copy = pltpu.make_async_copy(src, src_at, sems.at[0])
    src_copy.start()
    rows = out_at.shape[0]
    if kind == "own":
        base_copy = pltpu.make_async_copy(base, chains[0], sems.at[1])
        base_copy.start()
    for chain in chains[1 if kind == "own" else 0 :]:
        clear(chain, 0, rows)
    if kind == "own":
        base_copy.wait()
    src_copy.wait()

    def scatter(nodes, count, slots):
        turn = 0
        for n in nodes:
            row = src_at[pl.ds(n, 1), :]
            for s in range(count):
                chain = chains[turn % len(chains)]
                turn += 1
                at = pl.ds(slots[s][n], 1)
                chain[at, :] = chain[at, :] + row

    todo.visit(scatter, group_of)

    part = rows // len(outs)
    for half, out in enumerate(outs):

        @pl.loop(0, part // HUB)
        def _(i, half=half, out=out):
            if kind == "hub":
                flip_x, flip_y = (i >> 2) ^ (i >> 3), (i & 3) ^ ((i >> 1) & 1)
                owner_y = lax.axis_index("y") ^ flip_y
                owner_x = lax.axis_index("x") ^ flip_x
                taken = owner_y * 8 + owner_x * 2 + (lax.axis_index("core") ^ half)
            elif kind == "rim":
                taken = i + faces_up(half) * (HALO // HUB)
            else:
                taken = i
            to = pl.ds(i * HUB, HUB)
            at = pl.ds(half * part + i * HUB, HUB)
            out_at[at, :] = chain_sum(chains, pl.ds(taken * HUB, HUB)).astype(out_at.dtype)
            pltpu.make_async_copy(out_at.at[at], out.at[to], sems.at[2 + half]).start()

    for half, out in enumerate(outs):
        at = pl.ds(half * part, part)
        pltpu.make_async_copy(out_at.at[at], out, sems.at[2 + half]).wait()


def scatter(kind, rows, dtype, us, chains, lists, *inputs):
    parts = 1 if kind == "own" else 2
    return pl.pallas_call(
        functools.partial(scatter_kernel, kind),
        out_shape=(jax.ShapeDtypeStruct((rows // parts, F), dtype),) * parts,
        in_specs=list_specs + [hbm] * len(inputs),
        out_specs=(hbm,) * parts,
        scratch_shapes=list_scratch
        + [
            pltpu.VMEM((NODES, F), jnp.float32),
            pltpu.VMEM((rows, F), dtype),
            pltpu.SemaphoreType.DMA((4,)),
        ]
        + [pltpu.VMEM((rows, F), jnp.float32)] * chains,
        compiler_params=params,
        cost_estimate=cost(us),
        name=kind + "_scatter",
    )(*lists, *inputs)


def finish_kernel(hub_rows, own, rim_0, rim_1, share, out, total, rims, share_at, out_at, rows, sems):
    to = (total, rims.at[pl.ds(0, HALO)], rims.at[pl.ds(HALO, HALO)], share_at, rows)
    copies = [
        pltpu.make_async_copy(source, to[k], sems.at[k])
        for k, source in enumerate((own, rim_0, rim_1, share, hub_rows))
    ]
    for copy in copies:
        copy.start()
    for copy in copies:
        copy.wait()
    step = 256
    for half in range(2):
        start = pl.multiple_of(faces_up(half) * (NODES - HALO), HALO)

        @pl.loop(0, HALO // step)
        def _(i, half=half, start=start):
            cut = pl.ds(start + i * step, step)
            rim = rims[pl.ds(half * HALO + i * step, step), :]
            total[cut, :] = total[cut, :] + rim.astype(jnp.float32)

    @pl.loop(0, HUB // 16)
    def _(i):
        for u in range(16):
            at = pl.ds(rows[i * 16 + u], 1)
            total[at, :] = total[at, :] + share_at[pl.ds(i * 16 + u, 1), :]

    @pl.loop(0, NODES // 512)
    def _(i):
        cut = pl.ds(i * 512, 512)
        out_at[cut, :] = total[cut, :].astype(jnp.bfloat16)
        pltpu.make_async_copy(out_at.at[cut], out.at[cut], sems.at[5]).start()

    pltpu.make_async_copy(out_at, out, sems.at[5]).wait()


def finish(hub_rows, own, rim_0, rim_1, share):
    return pl.pallas_call(
        finish_kernel,
        out_shape=jax.ShapeDtypeStruct((NODES, F), jnp.bfloat16),
        in_specs=[anywhere] * 5,
        out_specs=hbm,
        scratch_shapes=[
            pltpu.VMEM((NODES, F), jnp.float32),
            pltpu.VMEM((2 * HALO, F), jnp.bfloat16),
            pltpu.VMEM((HUB, F), jnp.float32),
            pltpu.VMEM((NODES, F), jnp.bfloat16),
            pltpu.SMEM((HUB,), jnp.int32),
            pltpu.SemaphoreType.DMA((6,)),
        ],
        compiler_params=pltpu.CompilerParams(vmem_limit_bytes=16 * 2**20),
        cost_estimate=cost(3),
        name="finish",
    )(hub_rows, own, rim_0, rim_1, share)


def hand_out_kernel(mine, other, grad_self, grad_neigh, grad_bias):
    first = lax.axis_index("core") == 0
    grad_self[...] = jnp.where(first, mine[0:F, :], other[0:F, :])
    grad_neigh[...] = jnp.where(first, other[0:F, :], mine[0:F, :])
    bias = jnp.where(first, mine[F:HALF, :], other[F:HALF, :])
    grad_bias[...] = jnp.sum(bias, axis=0, keepdims=True)


def hand_out(mine, other):
    return pl.pallas_call(
        hand_out_kernel,
        out_shape=(jax.ShapeDtypeStruct((F, H), jnp.float32),) * 2
        + (jax.ShapeDtypeStruct((1, H), jnp.float32),),
        in_specs=[vmem] * 2,
        out_specs=(vmem,) * 3,
        compiler_params=pltpu.CompilerParams(vmem_limit_bytes=8 * 2**20),
        cost_estimate=cost(1),
        name="hand_out",
    )(mine, other)


def swap(value, axis, flip):
    count = lax.axis_size(axis)
    return lax.ppermute(value, axis, [(i, i ^ flip) for i in range(count)])


def swap_rims(first, second):
    above = lax.ppermute(first, "z", [(0, 1), (1, 0), (2, 3), (3, 2)])
    return above, lax.ppermute(second, "z", [(1, 2), (2, 1)])


def halves(value):
    rows = value.shape[0] // 2
    return value[:rows], value[rows:]


def halve(keep, got, axis, flip):
    mine, give = halves(plus(keep, got))
    return mine, swap(give.astype(jnp.bfloat16), axis, flip)


def plus(keep, got):
    return keep.astype(jnp.float32) + got.astype(jnp.float32)


def tie(*values):
    return lax.optimization_barrier(values)


def on_device(features, neighbors, counts, hub_rows, w_self, w_neigh, out_bias, cotangent):
    counts = counts.reshape(ROWS, LANES)

    h0 = pick_hubs(hub_rows, features)
    h1 = swap(h0, "y", 1)
    flat, order = plan(all_plan_kernel, (tiles, ordered), 4, neighbors.T, counts)
    all_lists = lists(order, flat)
    h1, flat = tie(h1, flat)
    held = jnp.concatenate([h0, h1], axis=0)
    h2 = swap(held, "y", 3)
    slots, order = plan(hub_plan_kernel, (tiles, ordered), 4, flat, counts)
    hub_lists = lists(order, slots)
    h2, flat, edges, *hub_lists = tie(h2, flat, features, *hub_lists)
    held = jnp.concatenate([held, h2], axis=0)
    h3 = swap(held, "x", 1)
    rims = swap_rims(*(
        lax.dynamic_slice_in_dim(edges, faces_up(half) * (NODES - HALO), HALO, axis=0)
        for half in range(2)
    ))
    h3, flat = tie(h3, flat)
    held = jnp.concatenate([held, h3], axis=0)
    h4 = swap(held, "x", 3)
    slots, order, own_order = plan(rim_plan_kernel, (tiles, ordered, ordered), 5, flat, counts)
    rim_lists = lists(order, slots)
    own_lists = lists(own_order, slots)
    h4, rim_lists, own_lists, *rims = tie(h4, rim_lists, own_lists, *rims)
    held = jnp.concatenate([held, h4], axis=0)
    h5 = swap(held, "core", 1)

    act, src, base, grads = forward(
        all_lists, features, rims, (h0, h1, h2, h3, h4, h5), counts,
        w_self, w_neigh, out_bias.reshape(1, H), cotangent,
    )

    other = swap(grads, "z", 1)
    keep, give = scatter("hub", HUBS, jnp.bfloat16, 8, 6, hub_lists, src)
    keep, give, src, other = tie(keep, give, src, other)
    grads = grads + other
    got = swap(give, "core", 1)
    other = swap(grads, "z", 3)
    got, src = tie(got, src)
    keep, got = halve(keep, got, "x", 3)
    rims = scatter("rim", 2 * HALO, jnp.bfloat16, 8, 6, rim_lists, src)
    keep, got, src, other, *rims = tie(keep, got, src, other, *rims)

    grads, give = halves(grads + other)
    other = swap(give, "core", 1)
    keep, got = halve(keep, got, "x", 1)
    other, src = tie(other, src)
    grads = grads + other
    other = swap(grads, "x", 3)
    rims = swap_rims(*rims)
    (own,) = scatter("own", NODES, jnp.float32, 20, CHAINS, own_lists, src, base)
    keep, got, other, own, *rims = tie(keep, got, other, own, *rims)

    keep, got = halve(keep, got, "y", 3)
    grads = grads + other
    other = swap(grads, "x", 1)
    keep, got, other = tie(keep, got, other)
    keep, got = halve(keep, got, "y", 1)
    grads = grads + other
    other = swap(grads, "y", 3)
    keep, got, other = tie(keep, got, other)
    grads = grads + other
    other = swap(grads, "y", 1)
    grad_features = finish(hub_rows, own, *rims, plus(keep, got))
    other, grad_features = tie(other, grad_features)
    grads = grads + other
    other = swap(grads, "core", 1)
    grad_self, grad_neigh, grad_bias = hand_out(grads, other)
    return act, grad_features, grad_self, grad_neigh, grad_bias.reshape(H)


def solution(mesh):
    mesh = Mesh(mesh.devices.reshape(4, 4, 4, 2), AXES)
    rows = P(AXES, None)
    placed = (rows, rows, P(AXES), P(AXES), P(), P(), P(), rows)
    return jax.shard_map(
        on_device,
        mesh=mesh,
        in_specs=placed,
        out_specs=(rows, rows, P(), P(), P()),
        check_vma=False,
    )
```

```python
import functools

import jax
import jax.numpy as jnp
from jax import lax
from jax.experimental import pallas as pl
from jax.experimental.pallas import tpu as pltpu
from jax.sharding import Mesh, PartitionSpec as P

F = 128
H = 256
NODES = 4096
HALO = 1024
HUB = 128
FANOUT = 10
COLS = 32
HUBS = HUB * COLS
OWN = HALO
UPPER = HALO + NODES
HUB_AT = 2 * HALO + NODES
EXTENT = HUB_AT + HUBS
LANES = 128
CHAINS = 8
VMEM_BYTES = 60 * 2**20
HALF = F + 8
AXES = ("z", "y", "x", "core")

smem = pl.BlockSpec(memory_space=pltpu.SMEM)
vmem = pl.BlockSpec(memory_space=pltpu.VMEM)
hbm = pl.BlockSpec(memory_space=pltpu.HBM)
anywhere = pl.BlockSpec(memory_space=pl.ANY)
params = pltpu.CompilerParams(vmem_limit_bytes=VMEM_BYTES)


def group_of(count):
    return 16 if count <= 3 else 8


def wide_group_of(count):
    return 32 if count == 1 else 16


def cost(us):
    return pl.CostEstimate(flops=int(us * 1e9), bytes_accessed=0, transcendentals=0)


def faces_up(half):
    return (lax.axis_index("z") & 1) ^ (1 - half)


def faces_up(half):
    return (lax.axis_index("z") & 1) ^ (1 - half)


def hub_kernel(hub_rows, features, out, wide, rows):
    @pl.loop(0, NODES // 512)
    def _(i):
        cut = pl.ds(i * 512, 512)
        wide[cut, :] = features[cut, :].astype(jnp.float32)

    @pl.loop(0, HUB // 16)
    def _(i):
        for u in range(16):
            rows[pl.ds(i * 16 + u, 1), :] = wide[pl.ds(hub_rows[i * 16 + u], 1), :]

    out[...] = rows[...].astype(jnp.bfloat16)


def pick_hubs(hub_rows, features):
    return pl.pallas_call(
        hub_kernel,
        out_shape=jax.ShapeDtypeStruct((HUB, F), jnp.bfloat16),
        in_specs=[smem, vmem],
        out_specs=vmem,
        scratch_shapes=[pltpu.VMEM((NODES, F), jnp.float32), pltpu.VMEM((HUB, F), jnp.float32)],
        compiler_params=params,
        cost_estimate=cost(2),
        name="pick_hubs",
    )(hub_rows, features)


ROWS = NODES // LANES


def order_by(count, order):
    lane_r = lax.broadcasted_iota(jnp.int32, (LANES, LANES), 0)
    lane_c = lax.broadcasted_iota(jnp.int32, (LANES, LANES), 1)
    before = (lane_r < lane_c).astype(jnp.bfloat16)
    row_r = lax.broadcasted_iota(jnp.int32, (ROWS, ROWS), 0)
    row_c = lax.broadcasted_iota(jnp.int32, (ROWS, ROWS), 1)
    above = (row_c < row_r).astype(jnp.bfloat16)
    lane = lax.broadcasted_iota(jnp.int32, (1, LANES), 1)
    hits = [(count == c).astype(jnp.float32) for c in range(FANOUT + 1)]
    stacked = jnp.concatenate(hits, axis=0).astype(jnp.bfloat16)
    in_rows = jnp.dot(stacked, before, preferred_element_type=jnp.float32)
    place = jnp.zeros((ROWS, LANES), jnp.float32)
    start = jnp.zeros((1, 1), jnp.float32)
    end_row = jnp.zeros((1, LANES), jnp.float32)
    for c in range(FANOUT + 1):
        hit = hits[c]
        per_row = jnp.sum(hit, axis=1, keepdims=True)
        earlier = jnp.dot(
            above,
            jnp.broadcast_to(per_row, (ROWS, LANES)).astype(jnp.bfloat16),
            preferred_element_type=jnp.float32,
        )
        in_row = in_rows[c * ROWS : (c + 1) * ROWS]
        place = place + hit * (in_row + earlier + start)
        start = start + jnp.sum(per_row, axis=0, keepdims=True)
        end_row = end_row + jnp.where(lane == c, start, 0.0)
    place = place.astype(jnp.int32)
    high = place >> 7
    low = place & (LANES - 1)
    slot_row = lax.broadcasted_iota(jnp.int32, (ROWS, LANES), 0)
    slot_lane = lax.broadcasted_iota(jnp.int32, (LANES, LANES), 0)
    own_lane = lax.broadcasted_iota(jnp.int32, (ROWS, LANES), 1).astype(jnp.float32)
    total = jnp.zeros((ROWS, LANES), jnp.float32)
    for r in range(ROWS):
        to_row = (high[r : r + 1, :] == slot_row).astype(jnp.float32)
        to_lane = (low[r : r + 1, :] == slot_lane).astype(jnp.bfloat16)
        both = jnp.concatenate([to_row * own_lane, to_row * float(r)], axis=0)
        found = lax.dot_general(
            both.astype(jnp.bfloat16),
            to_lane,
            (((1,), (1,)), ((), ())),
            preferred_element_type=jnp.float32,
        )
        total = total + found[:ROWS] + found[ROWS:] * float(LANES)
    order[0:ROWS, :] = total.astype(jnp.int32)
    order[ROWS : ROWS + 8, :] = jnp.broadcast_to(end_row, (8, LANES)).astype(jnp.int32)


def compact(flat, count, is_kind, value, backwards, placed):
    found = jnp.zeros((ROWS, LANES), jnp.int32)
    for s in range(FANOUT):
        row = flat[s * ROWS : (s + 1) * ROWS, :]
        hit = jnp.logical_and(count > s, is_kind(row))
        at = jnp.where(hit, found, -1)
        for k in range(s + 1):
            place = FANOUT - 1 - k if backwards else k
            placed[place] = jnp.where(at == k, value(row), placed[place])
        found = found + hit.astype(jnp.int32)
    return found


def nothing_placed():
    return [jnp.zeros((ROWS, LANES), jnp.int32) for _ in range(FANOUT)]


def is_own(row):
    return jnp.logical_and(row >= OWN, row < UPPER)


def is_rim(row):
    return jnp.logical_or(row < OWN, jnp.logical_and(row >= UPPER, row < HUB_AT))


def all_plan_kernel(neighbors, counts, flat, order):
    for s in range(FANOUT):
        for r in range(ROWS):
            at = s * ROWS + r
            flat[at : at + 1, :] = neighbors[s : s + 1, r * LANES : (r + 1) * LANES]
    order_by(counts[...], order)


def hub_plan_kernel(flat, counts, slots, order):
    placed = nothing_placed()
    hubs = compact(
        flat, counts[...], lambda row: row >= HUB_AT, lambda row: row - HUB_AT, False, placed
    )
    for s in range(FANOUT):
        slots[s * ROWS : (s + 1) * ROWS, :] = placed[s]
    order_by(hubs, order)


def rim_plan_kernel(flat, counts, slots, order, own_order):
    placed = nothing_placed()
    owns = compact(flat, counts[...], is_own, lambda row: row - OWN, False, placed)
    rims = compact(
        flat, counts[...], is_rim, lambda row: jnp.where(row < OWN, row, row - NODES), True, placed
    )
    for s in range(FANOUT):
        slots[s * ROWS : (s + 1) * ROWS, :] = placed[s]
    order_by(rims, order)
    order_by(owns, own_order)


ORDER = NODES + 8 * LANES
ordered = jax.ShapeDtypeStruct((ROWS + 8, LANES), jnp.int32)
tiles = jax.ShapeDtypeStruct((FANOUT * ROWS, LANES), jnp.int32)


def plan(kernel, outs, us, *inputs):
    return pl.pallas_call(
        kernel,
        out_shape=outs,
        in_specs=[vmem] * len(inputs),
        out_specs=(vmem,) * len(outs),
        compiler_params=params,
        cost_estimate=cost(us),
        name=kernel.__name__,
    )(*inputs)


def lists(order, slots):
    return order.reshape(ORDER), slots.reshape(FANOUT * NODES)


list_specs = [hbm, hbm]
list_scratch = [pltpu.SMEM((ORDER,), jnp.int32)] + [pltpu.SMEM((NODES,), jnp.int32)] * FANOUT + [
    pltpu.SemaphoreType.DMA((1 + FANOUT,))
]


class Lists:
    def __init__(self, backwards, order, slots, order_at, *rest):
        slots_at, sems = rest[:FANOUT], rest[FANOUT]
        self.order, self.slots = order_at, slots_at
        self.copies = [pltpu.make_async_copy(order, order_at, sems.at[0])]
        for s in range(FANOUT):
            part = slots.at[pl.ds(s * NODES, NODES)]
            self.copies.append(pltpu.make_async_copy(part, slots_at[s], sems.at[1 + s]))
        if backwards:
            self.slots = self.slots[::-1]
            self.copies[1:] = self.copies[:0:-1]
        for copy in self.copies:
            copy.start()

    def visit(self, act, group_of):
        slots, copies = self.slots, self.copies[1:]
        self.copies[0].wait()
        for count in range(1, FANOUT + 1):
            copies[count - 1].wait()
            size = group_of(count)
            first = self.order[NODES + count - 1]
            last = self.order[NODES + count]
            groups = (last - first) // size
            rest = first + groups * size

            @pl.loop(0, groups)
            def _(g, count=count, size=size, first=first):
                at = first + g * size
                act([self.order[at + u] for u in range(size)], count, slots)

            @pl.loop(rest, last)
            def _(at, count=count):
                act([self.order[at]], count, slots)


def clear(ref, at, rows):
    step = 512

    @pl.loop(0, rows // step)
    def _(i):
        ref[pl.ds(at + i * step, step), :] = jnp.zeros((step, F), jnp.float32)


BLOCK = 1024
HUB_PIECES = (1, 1, 2, 4, 8, 16)


def forward_kernel(order, slots, features, rim_up, rim_down, *refs):
    pieces, refs = refs[:6], refs[6:]
    small, cotangent, (act, src, base, grads) = refs[:4], refs[4], refs[5:9]
    table, sums, features_at, rims_at, hubs_at, cot_at, act_at, src_at, base_at = refs[9:18]
    small_at, lists_at, (sem_in, sem_out) = refs[18:21], refs[21:-2], refs[-2:]
    counts, weights, bias = small_at
    copies = [
        pltpu.make_async_copy(features, features_at, sem_in.at[0]),
        pltpu.make_async_copy(rim_up, rims_at.at[pl.ds(0, HALO)], sem_in.at[1]),
        pltpu.make_async_copy(rim_down, rims_at.at[pl.ds(HALO, HALO)], sem_in.at[2]),
    ]
    at = 0
    for k, piece in enumerate(pieces):
        rows = HUB_PIECES[k] * HUB
        copies.append(
            pltpu.make_async_copy(piece, hubs_at.at[pl.ds(at, rows)], sem_in.at[3 + k])
        )
        at += rows
    for copy in copies:
        copy.start()
    todo = Lists(False, order, slots, *lists_at)
    cot_copy = pltpu.make_async_copy(cotangent, cot_at, sem_in.at[9])
    cot_copy.start()
    to = (counts, weights.at[pl.ds(0, F)], weights.at[pl.ds(F, F)], bias)
    late = [pltpu.make_async_copy(small[k], to[k], sem_in.at[10 + k]) for k in range(4)]
    for copy in late:
        copy.start()
    late.append(cot_copy)
    grads[...] = jnp.zeros_like(grads)
    self_at = pl.multiple_of(lax.axis_index("core") * HALF, 8)
    neigh_at = pl.multiple_of((1 - lax.axis_index("core")) * HALF, 8)

    def widen(source, start, at, rows):
        step = 256

        @pl.loop(0, rows // step)
        def _(i):
            table[pl.ds(at + i * step, step), :] = source[
                pl.ds(start + i * step, step), :
            ].astype(jnp.float32)

    copies[0].wait()
    widen(features_at, 0, OWN, NODES)
    for half in range(2):
        copies[1 + half].wait()
        widen(rims_at, half * HALO, pl.multiple_of(faces_up(half) * UPPER, HALO), HALO)
    y, x, core = lax.axis_index("y"), lax.axis_index("x"), lax.axis_index("core")
    position = 0
    for k in range(6):
        copies[3 + k].wait()
        for _ in range(HUB_PIECES[k]):
            b = [(position >> k) & 1 for k in range(5)]
            owner_y = y ^ (b[0] * 1) ^ (b[1] * 3)
            owner_x = x ^ (b[2] * 1) ^ (b[3] * 3)
            owner = owner_y * 8 + owner_x * 2 + (core ^ b[4])
            table[pl.ds(HUB_AT + owner * HUB, HUB), :] = hubs_at[
                position * HUB : (position + 1) * HUB, :
            ].astype(jnp.float32)
            position += 1

    def gather(nodes, count, slots):
        for n in nodes:
            total = table[pl.ds(slots[0][n], 1), :]
            for s in range(1, count):
                total = total + table[pl.ds(slots[s][n], 1), :]
            sums[pl.ds(n, 1), :] = total

    todo.visit(gather, wide_group_of)
    for copy in late:
        copy.wait()

    @pl.loop(0, NODES // BLOCK)
    def _(i):
        cut = pl.ds(i * BLOCK, BLOCK)
        parts = []
        for k in range(BLOCK // LANES):
            row = counts[pl.ds(i * (BLOCK // LANES) + k, 1), :].astype(jnp.float32)
            parts.append(jnp.broadcast_to(row, (LANES, LANES)).T)
        divisor = jnp.concatenate(parts, axis=0)
        agg = (sums[cut, :] / divisor).astype(jnp.bfloat16)
        both = jnp.concatenate([features_at[cut, :], agg], axis=1)
        z = jnp.dot(both, weights[...], preferred_element_type=jnp.float32) + bias[...]
        scale = 0.7978845608028654
        cubic = 0.044715 * scale
        squared = z * z
        t = jnp.tanh(z * (scale + cubic * squared))
        half = 0.5 * z
        rest = half * t
        act_at[cut, :] = (half + rest).astype(jnp.bfloat16)
        slope = (0.5 + 0.5 * t) + (half - rest * t) * (scale + 3 * cubic * squared)
        dz = (cot_at[cut, :].astype(jnp.float32) * slope).astype(jnp.bfloat16)
        products = lax.dot_general(
            both, dz, (((0,), (0,)), ((), ())), preferred_element_type=jnp.float32
        )
        grads[pl.ds(self_at, F), :] += products[:F]
        grads[pl.ds(neigh_at, F), :] += products[F:]
        grads[pl.ds(self_at + F, 8), :] += jnp.sum(
            dz.astype(jnp.float32).reshape(BLOCK // 8, 8, H), axis=0
        )
        back = lax.dot_general(
            dz, weights[...], (((1,), (1,)), ((), ())), preferred_element_type=jnp.float32
        )
        base_at[cut, :] = back[:, :F]
        src_at[cut, :] = back[:, F:] / divisor
        for k, (here, there) in enumerate(((act_at, act), (src_at, src), (base_at, base))):
            pltpu.make_async_copy(here.at[cut], there.at[cut], sem_out.at[k]).start()

    for k, (here, there) in enumerate(((act_at, act), (src_at, src), (base_at, base))):
        pltpu.make_async_copy(here, there, sem_out.at[k]).wait()


def forward(lists, features, rims, hubs, counts, w_self, w_neigh, bias, cot):
    return pl.pallas_call(
        forward_kernel,
        out_shape=(
            jax.ShapeDtypeStruct((NODES, H), jnp.bfloat16),
            jax.ShapeDtypeStruct((NODES, F), jnp.float32),
            jax.ShapeDtypeStruct((NODES, F), jnp.float32),
            jax.ShapeDtypeStruct((2 * HALF, H), jnp.float32),
        ),
        in_specs=list_specs + [hbm] * (3 + len(hubs)) + [hbm] * 5,
        out_specs=(hbm, hbm, hbm, vmem),
        scratch_shapes=[
            pltpu.VMEM((EXTENT, F), jnp.float32),
            pltpu.VMEM((NODES, F), jnp.float32),
            pltpu.VMEM((NODES, F), jnp.bfloat16),
            pltpu.VMEM((2 * HALO, F), jnp.bfloat16),
            pltpu.VMEM((HUBS, F), jnp.bfloat16),
            pltpu.VMEM((NODES, H), jnp.bfloat16),
            pltpu.VMEM((NODES, H), jnp.bfloat16),
            pltpu.VMEM((NODES, F), jnp.float32),
            pltpu.VMEM((NODES, F), jnp.float32),
            pltpu.VMEM((ROWS, LANES), jnp.int32),
            pltpu.VMEM((2 * F, H), jnp.bfloat16),
            pltpu.VMEM((1, H), jnp.float32),
        ]
        + list_scratch
        + [pltpu.SemaphoreType.DMA((14,)), pltpu.SemaphoreType.DMA((3,))],
        compiler_params=params,
        cost_estimate=cost(30),
        name="forward",
    )(*lists, features, *rims, *hubs, counts, w_self, w_neigh, bias, cot)


def chain_sum(chains, cut):
    out = chains[0][cut, :]
    for chain in chains[1:]:
        out = out + chain[cut, :]
    return out


def scatter_kernel(kind, order, slots, src, *refs):
    if kind == "own":
        base, refs = refs[0], refs[1:]
    parts = 1 if kind == "own" else 2
    outs, refs = refs[:parts], refs[parts:]
    lists_at, (src_at, out_at, sems), chains = refs[: FANOUT + 2], refs[FANOUT + 2 : FANOUT + 5], refs[
        FANOUT + 5 :
    ]
    todo = Lists(kind == "rim", order, slots, *lists_at)
    src_copy = pltpu.make_async_copy(src, src_at, sems.at[0])
    src_copy.start()
    rows = out_at.shape[0]
    if kind == "own":
        base_copy = pltpu.make_async_copy(base, chains[0], sems.at[1])
        base_copy.start()
    for chain in chains[1 if kind == "own" else 0 :]:
        clear(chain, 0, rows)
    if kind == "own":
        base_copy.wait()
    src_copy.wait()

    def scatter(nodes, count, slots):
        turn = 0
        for n in nodes:
            row = src_at[pl.ds(n, 1), :]
            for s in range(count):
                chain = chains[turn % len(chains)]
                turn += 1
                at = pl.ds(slots[s][n], 1)
                chain[at, :] = chain[at, :] + row

    todo.visit(scatter, group_of)

    part = rows // len(outs)
    for half, out in enumerate(outs):

        @pl.loop(0, part // HUB)
        def _(i, half=half, out=out):
            if kind == "hub":
                flip_x, flip_y = (i >> 2) ^ (i >> 3), (i & 3) ^ ((i >> 1) & 1)
                owner_y = lax.axis_index("y") ^ flip_y
                owner_x = lax.axis_index("x") ^ flip_x
                taken = owner_y * 8 + owner_x * 2 + (lax.axis_index("core") ^ half)
            elif kind == "rim":
                taken = i + faces_up(half) * (HALO // HUB)
            else:
                taken = i
            to = pl.ds(i * HUB, HUB)
            at = pl.ds(half * part + i * HUB, HUB)
            out_at[at, :] = chain_sum(chains, pl.ds(taken * HUB, HUB)).astype(out_at.dtype)
            pltpu.make_async_copy(out_at.at[at], out.at[to], sems.at[2 + half]).start()

    for half, out in enumerate(outs):
        at = pl.ds(half * part, part)
        pltpu.make_async_copy(out_at.at[at], out, sems.at[2 + half]).wait()


def scatter(kind, rows, dtype, us, chains, lists, *inputs):
    parts = 1 if kind == "own" else 2
    return pl.pallas_call(
        functools.partial(scatter_kernel, kind),
        out_shape=(jax.ShapeDtypeStruct((rows // parts, F), dtype),) * parts,
        in_specs=list_specs + [hbm] * len(inputs),
        out_specs=(hbm,) * parts,
        scratch_shapes=list_scratch
        + [
            pltpu.VMEM((NODES, F), jnp.float32),
            pltpu.VMEM((rows, F), dtype),
            pltpu.SemaphoreType.DMA((4,)),
        ]
        + [pltpu.VMEM((rows, F), jnp.float32)] * chains,
        compiler_params=params,
        cost_estimate=cost(us),
        name=kind + "_scatter",
    )(*lists, *inputs)


def finish_kernel(hub_rows, own, rim_0, rim_1, share, out, total, rims, share_at, out_at, rows, sems):
    to = (total, rims.at[pl.ds(0, HALO)], rims.at[pl.ds(HALO, HALO)], share_at, rows)
    copies = [
        pltpu.make_async_copy(source, to[k], sems.at[k])
        for k, source in enumerate((own, rim_0, rim_1, share, hub_rows))
    ]
    for copy in copies:
        copy.start()
    for copy in copies:
        copy.wait()
    step = 256
    for half in range(2):
        start = pl.multiple_of(faces_up(half) * (NODES - HALO), HALO)

        @pl.loop(0, HALO // step)
        def _(i, half=half, start=start):
            cut = pl.ds(start + i * step, step)
            rim = rims[pl.ds(half * HALO + i * step, step), :]
            total[cut, :] = total[cut, :] + rim.astype(jnp.float32)

    @pl.loop(0, HUB // 16)
    def _(i):
        for u in range(16):
            at = pl.ds(rows[i * 16 + u], 1)
            total[at, :] = total[at, :] + share_at[pl.ds(i * 16 + u, 1), :]

    @pl.loop(0, NODES // 512)
    def _(i):
        cut = pl.ds(i * 512, 512)
        out_at[cut, :] = total[cut, :].astype(jnp.bfloat16)
        pltpu.make_async_copy(out_at.at[cut], out.at[cut], sems.at[5]).start()

    pltpu.make_async_copy(out_at, out, sems.at[5]).wait()


def finish(hub_rows, own, rim_0, rim_1, share):
    return pl.pallas_call(
        finish_kernel,
        out_shape=jax.ShapeDtypeStruct((NODES, F), jnp.bfloat16),
        in_specs=[anywhere] * 5,
        out_specs=hbm,
        scratch_shapes=[
            pltpu.VMEM((NODES, F), jnp.float32),
            pltpu.VMEM((2 * HALO, F), jnp.bfloat16),
            pltpu.VMEM((HUB, F), jnp.float32),
            pltpu.VMEM((NODES, F), jnp.bfloat16),
            pltpu.SMEM((HUB,), jnp.int32),
            pltpu.SemaphoreType.DMA((6,)),
        ],
        compiler_params=pltpu.CompilerParams(vmem_limit_bytes=16 * 2**20),
        cost_estimate=cost(3),
        name="finish",
    )(hub_rows, own, rim_0, rim_1, share)


def hand_out_kernel(mine, other, grad_self, grad_neigh, grad_bias):
    first = lax.axis_index("core") == 0
    grad_self[...] = jnp.where(first, mine[0:F, :], other[0:F, :])
    grad_neigh[...] = jnp.where(first, other[0:F, :], mine[0:F, :])
    bias = jnp.where(first, mine[F:HALF, :], other[F:HALF, :])
    grad_bias[...] = jnp.sum(bias, axis=0, keepdims=True)


def hand_out(mine, other):
    return pl.pallas_call(
        hand_out_kernel,
        out_shape=(jax.ShapeDtypeStruct((F, H), jnp.float32),) * 2
        + (jax.ShapeDtypeStruct((1, H), jnp.float32),),
        in_specs=[vmem] * 2,
        out_specs=(vmem,) * 3,
        compiler_params=pltpu.CompilerParams(vmem_limit_bytes=8 * 2**20),
        cost_estimate=cost(1),
        name="hand_out",
    )(mine, other)


def swap(value, axis, flip):
    count = lax.axis_size(axis)
    return lax.ppermute(value, axis, [(i, i ^ flip) for i in range(count)])


def swap_rims(first, second):
    above = lax.ppermute(first, "z", [(0, 1), (1, 0), (2, 3), (3, 2)])
    return above, lax.ppermute(second, "z", [(1, 2), (2, 1)])


def halves(value):
    rows = value.shape[0] // 2
    return value[:rows], value[rows:]


def give_half(parts, axis, flip):
    rows = min(part.shape[0] for part in parts)
    return swap(add_up(parts, rows // 2, rows).astype(jnp.bfloat16), axis, flip)


def add_up(parts, start, stop):
    total = parts[0][start:stop].astype(jnp.float32)
    for part in parts[1:]:
        total = total + part[start:stop].astype(jnp.float32)
    return total


def tie(*values):
    return lax.optimization_barrier(values)


def on_device(features, neighbors, counts, hub_rows, w_self, w_neigh, out_bias, cotangent):
    counts = counts.reshape(ROWS, LANES)

    h0 = pick_hubs(hub_rows, features)
    h1 = swap(h0, "y", 1)
    flat, order = plan(all_plan_kernel, (tiles, ordered), 4, neighbors.T, counts)
    all_lists = lists(order, flat)
    h1, flat = tie(h1, flat)
    held = jnp.concatenate([h0, h1], axis=0)
    h2 = swap(held, "y", 3)
    slots, order = plan(hub_plan_kernel, (tiles, ordered), 4, flat, counts)
    hub_lists = lists(order, slots)
    h2, flat, edges, *hub_lists = tie(h2, flat, features, *hub_lists)
    held = jnp.concatenate([held, h2], axis=0)
    h3 = swap(held, "x", 1)
    rims = swap_rims(*(
        lax.dynamic_slice_in_dim(edges, faces_up(half) * (NODES - HALO), HALO, axis=0)
        for half in range(2)
    ))
    h3, flat = tie(h3, flat)
    held = jnp.concatenate([held, h3], axis=0)
    h4 = swap(held, "x", 3)
    slots, order, own_order = plan(rim_plan_kernel, (tiles, ordered, ordered), 5, flat, counts)
    rim_lists = lists(order, slots)
    own_lists = lists(own_order, slots)
    h4, rim_lists, own_lists, *rims = tie(h4, rim_lists, own_lists, *rims)
    held = jnp.concatenate([held, h4], axis=0)
    h5 = swap(held, "core", 1)

    act, src, base, grads = forward(
        all_lists, features, rims, (h0, h1, h2, h3, h4, h5), counts,
        w_self, w_neigh, out_bias.reshape(1, H), cotangent,
    )

    other = swap(grads, "z", 1)
    keep, give = scatter("hub", HUBS, jnp.bfloat16, 8, 6, hub_lists, src)
    keep, give, src, other = tie(keep, give, src, other)
    grads = grads + other
    parts = [keep, swap(give, "core", 1)]
    other = swap(grads, "z", 3)
    parts, src = tie(parts, src)
    got = give_half(parts, "x", 3)
    rims = scatter("rim", 2 * HALO, jnp.bfloat16, 8, 6, rim_lists, src)
    parts, src, other, rims = tie(parts + [got], src, other, rims)

    grads, give = halves(grads + other)
    other = swap(give, "core", 1)
    got = give_half(parts, "x", 1)
    other, src = tie(other, src)
    grads = grads + other
    others = [swap(grads, "x", flip) for flip in (1, 3, 2)]
    (own,) = scatter("own", NODES, jnp.float32, 20, CHAINS, own_lists, src, base)
    parts, others, own, rims = tie(parts + [got], others, own, rims)

    grads = (grads + others[0]) + (others[1] + others[2])
    got = give_half(parts, "y", 3)
    other = swap(grads, "y", 1)
    rims = swap_rims(*rims)
    parts, other = tie(parts + [got], other)
    got = give_half(parts, "y", 1)
    grads = grads + other
    other = swap(grads, "y", 3)
    parts, other, rims = tie(parts + [got], other, rims)
    grads = grads + other
    other = swap(grads, "core", 1)
    grad_features = finish(hub_rows, own, *rims, add_up(parts, 0, HUB))
    other, grad_features = tie(other, grad_features)
    grad_self, grad_neigh, grad_bias = hand_out(grads, other)
    return act, grad_features, grad_self, grad_neigh, grad_bias.reshape(H)


def solution(mesh):
    mesh = Mesh(mesh.devices.reshape(4, 4, 4, 2), AXES)
    rows = P(AXES, None)
    placed = (rows, rows, P(AXES), P(AXES), P(), P(), P(), rows)
    return jax.shard_map(
        on_device,
        mesh=mesh,
        in_specs=placed,
        out_specs=(rows, rows, P(), P(), P()),
        check_vma=False,
    )
```

```python
import functools

import jax
import jax.numpy as jnp
from jax import lax
from jax.experimental import pallas as pl
from jax.experimental.pallas import tpu as pltpu
from jax.sharding import Mesh, PartitionSpec as P

F = 128
H = 256
NODES = 4096
HALO = 1024
HUB = 128
FANOUT = 10
COLS = 32
HUBS = HUB * COLS
OWN = HALO
UPPER = HALO + NODES
HUB_AT = 2 * HALO + NODES
EXTENT = HUB_AT + HUBS
LANES = 128
VMEM_BYTES = 60 * 2**20
HALF = F + 8
AXES = ("z", "y", "x", "core")

smem = pl.BlockSpec(memory_space=pltpu.SMEM)
vmem = pl.BlockSpec(memory_space=pltpu.VMEM)
hbm = pl.BlockSpec(memory_space=pltpu.HBM)
anywhere = pl.BlockSpec(memory_space=pl.ANY)
params = pltpu.CompilerParams(vmem_limit_bytes=VMEM_BYTES)


def group_of(count):
    return 16 if count <= 3 else 8


def wide_group_of(count):
    return 32 if count == 1 else 16


def cost(us):
    return pl.CostEstimate(flops=int(us * 1e9), bytes_accessed=0, transcendentals=0)


def faces_up(half):
    return (lax.axis_index("z") & 1) ^ (1 - half)


def faces_up(half):
    return (lax.axis_index("z") & 1) ^ (1 - half)


def hub_kernel(hub_rows, features, out, wide, rows):
    @pl.loop(0, NODES // 512)
    def _(i):
        cut = pl.ds(i * 512, 512)
        wide[cut, :] = features[cut, :].astype(jnp.float32)

    @pl.loop(0, HUB // 16)
    def _(i):
        for u in range(16):
            rows[pl.ds(i * 16 + u, 1), :] = wide[pl.ds(hub_rows[i * 16 + u], 1), :]

    out[...] = rows[...].astype(jnp.bfloat16)


def pick_hubs(hub_rows, features):
    return pl.pallas_call(
        hub_kernel,
        out_shape=jax.ShapeDtypeStruct((HUB, F), jnp.bfloat16),
        in_specs=[smem, vmem],
        out_specs=vmem,
        scratch_shapes=[pltpu.VMEM((NODES, F), jnp.float32), pltpu.VMEM((HUB, F), jnp.float32)],
        compiler_params=params,
        cost_estimate=cost(2),
        name="pick_hubs",
    )(hub_rows, features)


ROWS = NODES // LANES


def order_by(count, order):
    lane_r = lax.broadcasted_iota(jnp.int32, (LANES, LANES), 0)
    lane_c = lax.broadcasted_iota(jnp.int32, (LANES, LANES), 1)
    before = (lane_r < lane_c).astype(jnp.bfloat16)
    row_r = lax.broadcasted_iota(jnp.int32, (ROWS, ROWS), 0)
    row_c = lax.broadcasted_iota(jnp.int32, (ROWS, ROWS), 1)
    above = (row_c < row_r).astype(jnp.bfloat16)
    lane = lax.broadcasted_iota(jnp.int32, (1, LANES), 1)
    hits = [(count == c).astype(jnp.float32) for c in range(FANOUT + 1)]
    stacked = jnp.concatenate(hits, axis=0).astype(jnp.bfloat16)
    in_rows = jnp.dot(stacked, before, preferred_element_type=jnp.float32)
    place = jnp.zeros((ROWS, LANES), jnp.float32)
    start = jnp.zeros((1, 1), jnp.float32)
    end_row = jnp.zeros((1, LANES), jnp.float32)
    for c in range(FANOUT + 1):
        hit = hits[c]
        per_row = jnp.sum(hit, axis=1, keepdims=True)
        earlier = jnp.dot(
            above,
            jnp.broadcast_to(per_row, (ROWS, LANES)).astype(jnp.bfloat16),
            preferred_element_type=jnp.float32,
        )
        in_row = in_rows[c * ROWS : (c + 1) * ROWS]
        place = place + hit * (in_row + earlier + start)
        start = start + jnp.sum(per_row, axis=0, keepdims=True)
        end_row = end_row + jnp.where(lane == c, start, 0.0)
    place = place.astype(jnp.int32)
    high = place >> 7
    low = place & (LANES - 1)
    slot_row = lax.broadcasted_iota(jnp.int32, (ROWS, LANES), 0)
    slot_lane = lax.broadcasted_iota(jnp.int32, (LANES, LANES), 0)
    own_lane = lax.broadcasted_iota(jnp.int32, (ROWS, LANES), 1).astype(jnp.float32)
    total = jnp.zeros((ROWS, LANES), jnp.float32)
    for r in range(ROWS):
        to_row = (high[r : r + 1, :] == slot_row).astype(jnp.float32)
        to_lane = (low[r : r + 1, :] == slot_lane).astype(jnp.bfloat16)
        both = jnp.concatenate([to_row * own_lane, to_row * float(r)], axis=0)
        found = lax.dot_general(
            both.astype(jnp.bfloat16),
            to_lane,
            (((1,), (1,)), ((), ())),
            preferred_element_type=jnp.float32,
        )
        total = total + found[:ROWS] + found[ROWS:] * float(LANES)
    order[0:ROWS, :] = total.astype(jnp.int32)
    order[ROWS : ROWS + 8, :] = jnp.broadcast_to(end_row, (8, LANES)).astype(jnp.int32)


def compact(flat, count, is_kind, value, backwards, placed):
    found = jnp.zeros((ROWS, LANES), jnp.int32)
    for s in range(FANOUT):
        row = flat[s * ROWS : (s + 1) * ROWS, :]
        hit = jnp.logical_and(count > s, is_kind(row))
        at = jnp.where(hit, found, -1)
        for k in range(s + 1):
            place = FANOUT - 1 - k if backwards else k
            placed[place] = jnp.where(at == k, value(row), placed[place])
        found = found + hit.astype(jnp.int32)
    return found


def nothing_placed():
    return [jnp.zeros((ROWS, LANES), jnp.int32) for _ in range(FANOUT)]


def is_own(row):
    return jnp.logical_and(row >= OWN, row < UPPER)


def is_rim(row):
    return jnp.logical_or(row < OWN, jnp.logical_and(row >= UPPER, row < HUB_AT))


def all_plan_kernel(neighbors, counts, flat, order):
    for s in range(FANOUT):
        for r in range(ROWS):
            at = s * ROWS + r
            flat[at : at + 1, :] = neighbors[s : s + 1, r * LANES : (r + 1) * LANES]
    order_by(counts[...], order)


def hub_plan_kernel(flat, counts, slots, order):
    placed = nothing_placed()
    hubs = compact(
        flat, counts[...], lambda row: row >= HUB_AT, lambda row: row - HUB_AT, False, placed
    )
    for s in range(FANOUT):
        slots[s * ROWS : (s + 1) * ROWS, :] = placed[s]
    order_by(hubs, order)


def rim_plan_kernel(flat, counts, slots, order, own_order):
    placed = nothing_placed()
    owns = compact(flat, counts[...], is_own, lambda row: row - OWN, False, placed)
    rims = compact(
        flat, counts[...], is_rim, lambda row: jnp.where(row < OWN, row, row - NODES), True, placed
    )
    for s in range(FANOUT):
        slots[s * ROWS : (s + 1) * ROWS, :] = placed[s]
    order_by(rims, order)
    order_by(owns, own_order)


ORDER = NODES + 8 * LANES
ordered = jax.ShapeDtypeStruct((ROWS + 8, LANES), jnp.int32)
tiles = jax.ShapeDtypeStruct((FANOUT * ROWS, LANES), jnp.int32)


def plan(kernel, outs, us, *inputs):
    return pl.pallas_call(
        kernel,
        out_shape=outs,
        in_specs=[vmem] * len(inputs),
        out_specs=(vmem,) * len(outs),
        compiler_params=params,
        cost_estimate=cost(us),
        name=kernel.__name__,
    )(*inputs)


def lists(order, slots):
    return order.reshape(ORDER), slots.reshape(FANOUT * NODES)


list_specs = [hbm, hbm]
list_scratch = [pltpu.SMEM((ORDER,), jnp.int32)] + [pltpu.SMEM((NODES,), jnp.int32)] * FANOUT + [
    pltpu.SemaphoreType.DMA((1 + FANOUT,))
]


class Lists:
    def __init__(self, backwards, order, slots, order_at, *rest):
        slots_at, sems = rest[:FANOUT], rest[FANOUT]
        self.order, self.slots = order_at, slots_at
        self.copies = [pltpu.make_async_copy(order, order_at, sems.at[0])]
        for s in range(FANOUT):
            part = slots.at[pl.ds(s * NODES, NODES)]
            self.copies.append(pltpu.make_async_copy(part, slots_at[s], sems.at[1 + s]))
        if backwards:
            self.slots = self.slots[::-1]
            self.copies[1:] = self.copies[:0:-1]
        for copy in self.copies:
            copy.start()

    def visit(self, act, group_of):
        slots, copies = self.slots, self.copies[1:]
        self.copies[0].wait()
        for count in range(1, FANOUT + 1):
            copies[count - 1].wait()
            size = group_of(count)
            first = self.order[NODES + count - 1]
            last = self.order[NODES + count]
            groups = (last - first) // size
            rest = first + groups * size

            @pl.loop(0, groups)
            def _(g, count=count, size=size, first=first):
                at = first + g * size
                act([self.order[at + u] for u in range(size)], count, slots)

            @pl.loop(rest, last)
            def _(at, count=count):
                act([self.order[at]], count, slots)


def clear(ref, at, rows):
    step = 512

    @pl.loop(0, rows // step)
    def _(i):
        ref[pl.ds(at + i * step, step), :] = jnp.zeros((step, F), jnp.float32)


BLOCK = 2048
HUB_PIECES = (1, 1, 2, 4, 8, 8, 8)
PIECES = len(HUB_PIECES)


def forward_kernel(order, slots, features, rim_up, rim_down, *refs):
    pieces, refs = refs[:PIECES], refs[PIECES:]
    small, cotangent, (act, src, base, grads) = refs[:4], refs[4], refs[5:9]
    table, sums, features_at, rims_at, hubs_at, cot_at, act_at, src_at, base_at = refs[9:18]
    small_at, lists_at, (sem_in, sem_out) = refs[18:21], refs[21:-2], refs[-2:]
    counts, weights, bias = small_at
    copies = [
        pltpu.make_async_copy(features, features_at, sem_in.at[0]),
        pltpu.make_async_copy(rim_up, rims_at.at[pl.ds(0, HALO)], sem_in.at[1]),
        pltpu.make_async_copy(rim_down, rims_at.at[pl.ds(HALO, HALO)], sem_in.at[2]),
    ]
    at = 0
    for k, piece in enumerate(pieces):
        rows = HUB_PIECES[k] * HUB
        copies.append(
            pltpu.make_async_copy(piece, hubs_at.at[pl.ds(at, rows)], sem_in.at[3 + k])
        )
        at += rows
    for copy in copies:
        copy.start()
    todo = Lists(False, order, slots, *lists_at)
    cot_copy = pltpu.make_async_copy(cotangent, cot_at, sem_in.at[3 + PIECES])
    cot_copy.start()
    to = (counts, weights.at[pl.ds(0, F)], weights.at[pl.ds(F, F)], bias)
    late = [pltpu.make_async_copy(small[k], to[k], sem_in.at[4 + PIECES + k]) for k in range(4)]
    for copy in late:
        copy.start()
    late.append(cot_copy)
    grads[...] = jnp.zeros_like(grads)
    self_at = pl.multiple_of(lax.axis_index("core") * HALF, 8)
    neigh_at = pl.multiple_of((1 - lax.axis_index("core")) * HALF, 8)

    def widen(source, start, at, rows):
        step = 256

        @pl.loop(0, rows // step)
        def _(i):
            table[pl.ds(at + i * step, step), :] = source[
                pl.ds(start + i * step, step), :
            ].astype(jnp.float32)

    copies[0].wait()
    widen(features_at, 0, OWN, NODES)
    for half in range(2):
        copies[1 + half].wait()
        widen(rims_at, half * HALO, pl.multiple_of(faces_up(half) * UPPER, HALO), HALO)
    y, x, core = lax.axis_index("y"), lax.axis_index("x"), lax.axis_index("core")
    position = 0
    for k in range(PIECES):
        copies[3 + k].wait()
        for _ in range(HUB_PIECES[k]):
            b = [(position >> k) & 1 for k in range(5)]
            owner_y = y ^ (b[0] * 1) ^ (b[1] * 3)
            owner_x = x ^ (b[2] * 1) ^ (b[3] * 3)
            owner = owner_y * 8 + owner_x * 2 + (core ^ b[4])
            table[pl.ds(HUB_AT + owner * HUB, HUB), :] = hubs_at[
                position * HUB : (position + 1) * HUB, :
            ].astype(jnp.float32)
            position += 1

    def gather(nodes, count, slots):
        for n in nodes:
            total = table[pl.ds(slots[0][n], 1), :]
            for s in range(1, count):
                total = total + table[pl.ds(slots[s][n], 1), :]
            sums[pl.ds(n, 1), :] = total

    todo.visit(gather, wide_group_of)
    for copy in late:
        copy.wait()

    @pl.loop(0, NODES // BLOCK)
    def _(i):
        cut = pl.ds(i * BLOCK, BLOCK)
        parts = []
        for k in range(BLOCK // LANES):
            row = counts[pl.ds(i * (BLOCK // LANES) + k, 1), :].astype(jnp.float32)
            parts.append(jnp.broadcast_to(row, (LANES, LANES)).T)
        divisor = jnp.concatenate(parts, axis=0)
        agg = (sums[cut, :] / divisor).astype(jnp.bfloat16)
        both = jnp.concatenate([features_at[cut, :], agg], axis=1)
        z = jnp.dot(both, weights[...], preferred_element_type=jnp.float32) + bias[...]
        scale = 0.7978845608028654
        cubic = 0.044715 * scale
        squared = z * z
        t = jnp.tanh(z * (scale + cubic * squared))
        half = 0.5 * z
        rest = half * t
        act_at[cut, :] = (half + rest).astype(jnp.bfloat16)
        slope = (0.5 + 0.5 * t) + (half - rest * t) * (scale + 3 * cubic * squared)
        dz = (cot_at[cut, :].astype(jnp.float32) * slope).astype(jnp.bfloat16)
        products = lax.dot_general(
            both, dz, (((0,), (0,)), ((), ())), preferred_element_type=jnp.float32
        )
        grads[pl.ds(self_at, F), :] += products[:F]
        grads[pl.ds(neigh_at, F), :] += products[F:]
        grads[pl.ds(self_at + F, 8), :] += jnp.sum(
            dz.astype(jnp.float32).reshape(BLOCK // 8, 8, H), axis=0
        )
        back = lax.dot_general(
            dz, weights[...], (((1,), (1,)), ((), ())), preferred_element_type=jnp.float32
        )
        base_at[cut, :] = back[:, :F]
        src_at[cut, :] = back[:, F:] / divisor
        for k, (here, there) in enumerate(((act_at, act), (src_at, src), (base_at, base))):
            pltpu.make_async_copy(here.at[cut], there.at[cut], sem_out.at[k]).start()

    for k, (here, there) in enumerate(((act_at, act), (src_at, src), (base_at, base))):
        pltpu.make_async_copy(here, there, sem_out.at[k]).wait()


def forward(lists, features, rims, hubs, counts, w_self, w_neigh, bias, cot):
    return pl.pallas_call(
        forward_kernel,
        out_shape=(
            jax.ShapeDtypeStruct((NODES, H), jnp.bfloat16),
            jax.ShapeDtypeStruct((NODES, F), jnp.float32),
            jax.ShapeDtypeStruct((NODES, F), jnp.float32),
            jax.ShapeDtypeStruct((2 * HALF, H), jnp.float32),
        ),
        in_specs=list_specs + [hbm] * (3 + len(hubs)) + [hbm] * 5,
        out_specs=(hbm, hbm, hbm, vmem),
        scratch_shapes=[
            pltpu.VMEM((EXTENT, F), jnp.float32),
            pltpu.VMEM((NODES, F), jnp.float32),
            pltpu.VMEM((NODES, F), jnp.bfloat16),
            pltpu.VMEM((2 * HALO, F), jnp.bfloat16),
            pltpu.VMEM((HUBS, F), jnp.bfloat16),
            pltpu.VMEM((NODES, H), jnp.bfloat16),
            pltpu.VMEM((NODES, H), jnp.bfloat16),
            pltpu.VMEM((NODES, F), jnp.float32),
            pltpu.VMEM((NODES, F), jnp.float32),
            pltpu.VMEM((ROWS, LANES), jnp.int32),
            pltpu.VMEM((2 * F, H), jnp.bfloat16),
            pltpu.VMEM((1, H), jnp.float32),
        ]
        + list_scratch
        + [pltpu.SemaphoreType.DMA((8 + PIECES,)), pltpu.SemaphoreType.DMA((3,))],
        compiler_params=params,
        cost_estimate=cost(30),
        name="forward",
    )(*lists, features, *rims, *hubs, counts, w_self, w_neigh, bias, cot)


def chain_sum(chains, cut):
    out = chains[0][cut, :]
    for chain in chains[1:]:
        out = out + chain[cut, :]
    return out


def scatter_kernel(kind, order, slots, src, *refs):
    if kind == "own":
        base, refs = refs[0], refs[1:]
    parts = 1 if kind == "own" else 2
    outs, refs = refs[:parts], refs[parts:]
    lists_at, (src_at, out_at, sems), chains = refs[: FANOUT + 2], refs[FANOUT + 2 : FANOUT + 5], refs[
        FANOUT + 5 :
    ]
    todo = Lists(kind == "rim", order, slots, *lists_at)
    src_copy = pltpu.make_async_copy(src, src_at, sems.at[0])
    src_copy.start()
    rows = out_at.shape[0]
    if kind == "own":
        base_copy = pltpu.make_async_copy(base, chains[0], sems.at[1])
        base_copy.start()
    for chain in chains[1 if kind == "own" else 0 :]:
        clear(chain, 0, rows)
    if kind == "own":
        base_copy.wait()
    src_copy.wait()

    def scatter(nodes, count, slots):
        turn = 0
        for n in nodes:
            row = src_at[pl.ds(n, 1), :]
            for s in range(count):
                chain = chains[turn % len(chains)]
                turn += 1
                at = pl.ds(slots[s][n], 1)
                chain[at, :] = chain[at, :] + row

    todo.visit(scatter, group_of)

    part = rows // len(outs)
    for half, out in enumerate(outs):

        @pl.loop(0, part // HUB)
        def _(i, half=half, out=out):
            if kind == "hub":
                flip_x, flip_y = (i >> 2) ^ (i >> 3), (i & 3) ^ ((i >> 1) & 1)
                owner_y = lax.axis_index("y") ^ flip_y
                owner_x = lax.axis_index("x") ^ flip_x
                taken = owner_y * 8 + owner_x * 2 + (lax.axis_index("core") ^ half)
            elif kind == "rim":
                taken = i + faces_up(half) * (HALO // HUB)
            else:
                taken = i
            to = pl.ds(i * HUB, HUB)
            at = pl.ds(half * part + i * HUB, HUB)
            out_at[at, :] = chain_sum(chains, pl.ds(taken * HUB, HUB)).astype(out_at.dtype)
            pltpu.make_async_copy(out_at.at[at], out.at[to], sems.at[2 + half]).start()

    for half, out in enumerate(outs):
        at = pl.ds(half * part, part)
        pltpu.make_async_copy(out_at.at[at], out, sems.at[2 + half]).wait()


def scatter(kind, rows, dtype, us, chains, lists, *inputs):
    parts = 1 if kind == "own" else 2
    return pl.pallas_call(
        functools.partial(scatter_kernel, kind),
        out_shape=(jax.ShapeDtypeStruct((rows // parts, F), dtype),) * parts,
        in_specs=list_specs + [hbm] * len(inputs),
        out_specs=(hbm,) * parts,
        scratch_shapes=list_scratch
        + [
            pltpu.VMEM((NODES, F), jnp.float32),
            pltpu.VMEM((rows, F), dtype),
            pltpu.SemaphoreType.DMA((4,)),
        ]
        + [pltpu.VMEM((rows, F), jnp.float32)] * chains,
        compiler_params=params,
        cost_estimate=cost(us),
        name=kind + "_scatter",
    )(*lists, *inputs)


def finish_kernel(hub_rows, own, rim_0, rim_1, share, out, total, rims, share_at, out_at, rows, sems):
    to = (total, rims.at[pl.ds(0, HALO)], rims.at[pl.ds(HALO, HALO)], share_at, rows)
    copies = [
        pltpu.make_async_copy(source, to[k], sems.at[k])
        for k, source in enumerate((own, rim_0, rim_1, share, hub_rows))
    ]
    for copy in copies:
        copy.start()
    for copy in copies:
        copy.wait()
    step = 256
    for half in range(2):
        start = pl.multiple_of(faces_up(half) * (NODES - HALO), HALO)

        @pl.loop(0, HALO // step)
        def _(i, half=half, start=start):
            cut = pl.ds(start + i * step, step)
            rim = rims[pl.ds(half * HALO + i * step, step), :]
            total[cut, :] = total[cut, :] + rim.astype(jnp.float32)

    @pl.loop(0, HUB // 16)
    def _(i):
        for u in range(16):
            at = pl.ds(rows[i * 16 + u], 1)
            total[at, :] = total[at, :] + share_at[pl.ds(i * 16 + u, 1), :]

    @pl.loop(0, NODES // 512)
    def _(i):
        cut = pl.ds(i * 512, 512)
        out_at[cut, :] = total[cut, :].astype(jnp.bfloat16)
        pltpu.make_async_copy(out_at.at[cut], out.at[cut], sems.at[5]).start()

    pltpu.make_async_copy(out_at, out, sems.at[5]).wait()


def finish(hub_rows, own, rim_0, rim_1, share):
    return pl.pallas_call(
        finish_kernel,
        out_shape=jax.ShapeDtypeStruct((NODES, F), jnp.bfloat16),
        in_specs=[anywhere] * 5,
        out_specs=hbm,
        scratch_shapes=[
            pltpu.VMEM((NODES, F), jnp.float32),
            pltpu.VMEM((2 * HALO, F), jnp.bfloat16),
            pltpu.VMEM((HUB, F), jnp.float32),
            pltpu.VMEM((NODES, F), jnp.bfloat16),
            pltpu.SMEM((HUB,), jnp.int32),
            pltpu.SemaphoreType.DMA((6,)),
        ],
        compiler_params=pltpu.CompilerParams(vmem_limit_bytes=16 * 2**20),
        cost_estimate=cost(3),
        name="finish",
    )(hub_rows, own, rim_0, rim_1, share)


def hand_out_kernel(mine, other, grad_self, grad_neigh, grad_bias):
    first = lax.axis_index("core") == 0
    grad_self[...] = jnp.where(first, mine[0:F, :], other[0:F, :])
    grad_neigh[...] = jnp.where(first, other[0:F, :], mine[0:F, :])
    bias = jnp.where(first, mine[F:HALF, :], other[F:HALF, :])
    grad_bias[...] = jnp.sum(bias, axis=0, keepdims=True)


def hand_out(mine, other):
    return pl.pallas_call(
        hand_out_kernel,
        out_shape=(jax.ShapeDtypeStruct((F, H), jnp.float32),) * 2
        + (jax.ShapeDtypeStruct((1, H), jnp.float32),),
        in_specs=[vmem] * 2,
        out_specs=(vmem,) * 3,
        compiler_params=pltpu.CompilerParams(vmem_limit_bytes=8 * 2**20),
        cost_estimate=cost(1),
        name="hand_out",
    )(mine, other)


def swap(value, axis, flip):
    count = lax.axis_size(axis)
    return lax.ppermute(value, axis, [(i, i ^ flip) for i in range(count)])


def swap_rims(first, second):
    above = lax.ppermute(first, "z", [(0, 1), (1, 0), (2, 3), (3, 2)])
    return above, lax.ppermute(second, "z", [(1, 2), (2, 1)])


def halves(value):
    rows = value.shape[0] // 2
    return value[:rows], value[rows:]


def give_half(parts, axis, flip):
    rows = min(part.shape[0] for part in parts)
    return swap(add_up(parts, rows // 2, rows).astype(jnp.bfloat16), axis, flip)


def add_up(parts, start, stop):
    total = parts[0][start:stop].astype(jnp.float32)
    for part in parts[1:]:
        total = total + part[start:stop].astype(jnp.float32)
    return total


def tie(*values):
    return lax.optimization_barrier(values)


def on_device(features, neighbors, counts, hub_rows, w_self, w_neigh, out_bias, cotangent):
    counts = counts.reshape(ROWS, LANES)

    h0 = pick_hubs(hub_rows, features)
    h1 = swap(h0, "y", 1)
    flat, order = plan(all_plan_kernel, (tiles, ordered), 4, neighbors.T, counts)
    all_lists = lists(order, flat)
    h1, flat = tie(h1, flat)
    held = jnp.concatenate([h0, h1], axis=0)
    h2 = swap(held, "y", 3)
    slots, order = plan(hub_plan_kernel, (tiles, ordered), 4, flat, counts)
    hub_lists = lists(order, slots)
    h2, flat, edges, *hub_lists = tie(h2, flat, features, *hub_lists)
    held = jnp.concatenate([held, h2], axis=0)
    h3 = swap(held, "x", 1)
    rims = swap_rims(*(
        lax.dynamic_slice_in_dim(edges, faces_up(half) * (NODES - HALO), HALO, axis=0)
        for half in range(2)
    ))
    h3, flat = tie(h3, flat)
    held = jnp.concatenate([held, h3], axis=0)
    h4 = swap(held, "x", 3)
    slots, order, own_order = plan(rim_plan_kernel, (tiles, ordered, ordered), 5, flat, counts)
    rim_lists = lists(order, slots)
    own_lists = lists(own_order, slots)
    h5 = swap(held, "core", 1)
    h4, h5, rim_lists, own_lists, *rims = tie(h4, h5, rim_lists, own_lists, *rims)
    h6 = swap(h4, "core", 1)

    act, src, base, grads = forward(
        all_lists, features, rims, (h0, h1, h2, h3, h4, h5, h6), counts,
        w_self, w_neigh, out_bias.reshape(1, H), cotangent,
    )

    other = swap(grads, "z", 1)
    keep, give = scatter("hub", HUBS, jnp.bfloat16, 8, 6, hub_lists, src)
    keep, give, src, other = tie(keep, give, src, other)
    grads = grads + other
    parts = [keep, swap(give, "core", 1)]
    other = swap(grads, "z", 3)
    parts, src = tie(parts, src)
    got = give_half(parts, "x", 3)
    rims = scatter("rim", 2 * HALO, jnp.bfloat16, 8, 6, rim_lists, src)
    parts, src, other, rims = tie(parts + [got], src, other, rims)

    grads, give = halves(grads + other)
    other = swap(give, "core", 1)
    got = give_half(parts, "x", 1)
    other, src = tie(other, src)
    grads = grads + other
    others = [swap(grads, "x", flip) for flip in (1, 3, 2)]
    (own,) = scatter("own", NODES, jnp.float32, 20, 12, own_lists, src, base)
    parts, others, own, rims = tie(parts + [got], others, own, rims)

    grads = (grads + others[0]) + (others[1] + others[2])
    got = give_half(parts, "y", 3)
    other = swap(grads, "y", 1)
    rims = swap_rims(*rims)
    parts, other = tie(parts + [got], other)
    got = give_half(parts, "y", 1)
    grads = grads + other
    other = swap(grads, "y", 3)
    parts, other, rims = tie(parts + [got], other, rims)
    grads = grads + other
    other = swap(grads, "core", 1)
    grad_features = finish(hub_rows, own, *rims, add_up(parts, 0, HUB))
    other, grad_features = tie(other, grad_features)
    grad_self, grad_neigh, grad_bias = hand_out(grads, other)
    return act, grad_features, grad_self, grad_neigh, grad_bias.reshape(H)


def solution(mesh):
    mesh = Mesh(mesh.devices.reshape(4, 4, 4, 2), AXES)
    rows = P(AXES, None)
    placed = (rows, rows, P(AXES), P(AXES), P(), P(), P(), rows)
    return jax.shard_map(
        on_device,
        mesh=mesh,
        in_specs=placed,
        out_specs=(rows, rows, P(), P(), P()),
        check_vma=False,
    )
```

```python
import functools

import jax
import jax.numpy as jnp
from jax import lax
from jax.experimental import pallas as pl
from jax.experimental.pallas import tpu as pltpu
from jax.sharding import Mesh, PartitionSpec as P

F = 128
H = 256
NODES = 4096
HALO = 1024
HUB = 128
FANOUT = 10
COLS = 32
HUBS = HUB * COLS
OWN = HALO
UPPER = HALO + NODES
HUB_AT = 2 * HALO + NODES
EXTENT = HUB_AT + HUBS
LANES = 128
VMEM_BYTES = 60 * 2**20
HALF = F + 8
AXES = ("z", "y", "x", "core")

smem = pl.BlockSpec(memory_space=pltpu.SMEM)
vmem = pl.BlockSpec(memory_space=pltpu.VMEM)
hbm = pl.BlockSpec(memory_space=pltpu.HBM)
anywhere = pl.BlockSpec(memory_space=pl.ANY)
params = pltpu.CompilerParams(vmem_limit_bytes=VMEM_BYTES)


def group_of(count):
    return 16 if count <= 3 else 8


def wide_group_of(count):
    return 32 if count == 1 else 16


def cost(us):
    return pl.CostEstimate(flops=int(us * 1e9), bytes_accessed=0, transcendentals=0)


def faces_up(half):
    return (lax.axis_index("z") & 1) ^ (1 - half)


def faces_up(half):
    return (lax.axis_index("z") & 1) ^ (1 - half)


def hub_kernel(hub_rows, features, out, wide, rows):
    @pl.loop(0, NODES // 512)
    def _(i):
        cut = pl.ds(i * 512, 512)
        wide[cut, :] = features[cut, :].astype(jnp.float32)

    @pl.loop(0, HUB // 16)
    def _(i):
        for u in range(16):
            rows[pl.ds(i * 16 + u, 1), :] = wide[pl.ds(hub_rows[i * 16 + u], 1), :]

    out[...] = rows[...].astype(jnp.bfloat16)


def pick_hubs(hub_rows, features):
    return pl.pallas_call(
        hub_kernel,
        out_shape=jax.ShapeDtypeStruct((HUB, F), jnp.bfloat16),
        in_specs=[smem, vmem],
        out_specs=vmem,
        scratch_shapes=[pltpu.VMEM((NODES, F), jnp.float32), pltpu.VMEM((HUB, F), jnp.float32)],
        compiler_params=params,
        cost_estimate=cost(2),
        name="pick_hubs",
    )(hub_rows, features)


ROWS = NODES // LANES


def order_by(count, order):
    lane_r = lax.broadcasted_iota(jnp.int32, (LANES, LANES), 0)
    lane_c = lax.broadcasted_iota(jnp.int32, (LANES, LANES), 1)
    before = (lane_r < lane_c).astype(jnp.bfloat16)
    row_r = lax.broadcasted_iota(jnp.int32, (ROWS, ROWS), 0)
    row_c = lax.broadcasted_iota(jnp.int32, (ROWS, ROWS), 1)
    above = (row_c < row_r).astype(jnp.bfloat16)
    lane = lax.broadcasted_iota(jnp.int32, (1, LANES), 1)
    hits = [(count == c).astype(jnp.float32) for c in range(FANOUT + 1)]
    stacked = jnp.concatenate(hits, axis=0).astype(jnp.bfloat16)
    in_rows = jnp.dot(stacked, before, preferred_element_type=jnp.float32)
    place = jnp.zeros((ROWS, LANES), jnp.float32)
    start = jnp.zeros((1, 1), jnp.float32)
    end_row = jnp.zeros((1, LANES), jnp.float32)
    for c in range(FANOUT + 1):
        hit = hits[c]
        per_row = jnp.sum(hit, axis=1, keepdims=True)
        earlier = jnp.dot(
            above,
            jnp.broadcast_to(per_row, (ROWS, LANES)).astype(jnp.bfloat16),
            preferred_element_type=jnp.float32,
        )
        in_row = in_rows[c * ROWS : (c + 1) * ROWS]
        place = place + hit * (in_row + earlier + start)
        start = start + jnp.sum(per_row, axis=0, keepdims=True)
        end_row = end_row + jnp.where(lane == c, start, 0.0)
    place = place.astype(jnp.int32)
    high = place >> 7
    low = place & (LANES - 1)
    slot_row = lax.broadcasted_iota(jnp.int32, (ROWS, LANES), 0)
    slot_lane = lax.broadcasted_iota(jnp.int32, (LANES, LANES), 0)
    own_lane = lax.broadcasted_iota(jnp.int32, (ROWS, LANES), 1).astype(jnp.float32)
    total = jnp.zeros((ROWS, LANES), jnp.float32)
    for r in range(ROWS):
        to_row = (high[r : r + 1, :] == slot_row).astype(jnp.float32)
        to_lane = (low[r : r + 1, :] == slot_lane).astype(jnp.bfloat16)
        both = jnp.concatenate([to_row * own_lane, to_row * float(r)], axis=0)
        found = lax.dot_general(
            both.astype(jnp.bfloat16),
            to_lane,
            (((1,), (1,)), ((), ())),
            preferred_element_type=jnp.float32,
        )
        total = total + found[:ROWS] + found[ROWS:] * float(LANES)
    order[0:ROWS, :] = total.astype(jnp.int32)
    order[ROWS : ROWS + 8, :] = jnp.broadcast_to(end_row, (8, LANES)).astype(jnp.int32)


def compact(flat, count, is_kind, value, backwards, placed):
    found = jnp.zeros((ROWS, LANES), jnp.int32)
    for s in range(FANOUT):
        row = flat[s * ROWS : (s + 1) * ROWS, :]
        hit = jnp.logical_and(count > s, is_kind(row))
        at = jnp.where(hit, found, -1)
        for k in range(s + 1):
            place = FANOUT - 1 - k if backwards else k
            placed[place] = jnp.where(at == k, value(row), placed[place])
        found = found + hit.astype(jnp.int32)
    return found


def nothing_placed():
    return [jnp.zeros((ROWS, LANES), jnp.int32) for _ in range(FANOUT)]


def is_own(row):
    return jnp.logical_and(row >= OWN, row < UPPER)


def is_rim(row):
    return jnp.logical_or(row < OWN, jnp.logical_and(row >= UPPER, row < HUB_AT))


def all_plan_kernel(neighbors, counts, flat, order):
    for s in range(FANOUT):
        for r in range(ROWS):
            at = s * ROWS + r
            flat[at : at + 1, :] = neighbors[s : s + 1, r * LANES : (r + 1) * LANES]
    order_by(counts[...], order)


def hub_plan_kernel(flat, counts, slots, order):
    placed = nothing_placed()
    hubs = compact(
        flat, counts[...], lambda row: row >= HUB_AT, lambda row: row - HUB_AT, False, placed
    )
    for s in range(FANOUT):
        slots[s * ROWS : (s + 1) * ROWS, :] = placed[s]
    order_by(hubs, order)


def rim_plan_kernel(flat, counts, slots, order, own_order):
    placed = nothing_placed()
    owns = compact(flat, counts[...], is_own, lambda row: row - OWN, False, placed)
    rims = compact(
        flat, counts[...], is_rim, lambda row: jnp.where(row < OWN, row, row - NODES), True, placed
    )
    for s in range(FANOUT):
        slots[s * ROWS : (s + 1) * ROWS, :] = placed[s]
    order_by(rims, order)
    order_by(owns, own_order)


ORDER = NODES + 8 * LANES
ordered = jax.ShapeDtypeStruct((ROWS + 8, LANES), jnp.int32)
tiles = jax.ShapeDtypeStruct((FANOUT * ROWS, LANES), jnp.int32)


def plan(kernel, outs, us, *inputs):
    return pl.pallas_call(
        kernel,
        out_shape=outs,
        in_specs=[vmem] * len(inputs),
        out_specs=(vmem,) * len(outs),
        compiler_params=params,
        cost_estimate=cost(us),
        name=kernel.__name__,
    )(*inputs)


def lists(order, slots):
    return order.reshape(ORDER), slots.reshape(FANOUT * NODES)


list_specs = [hbm, hbm]
list_scratch = [pltpu.SMEM((ORDER,), jnp.int32)] + [pltpu.SMEM((NODES,), jnp.int32)] * FANOUT + [
    pltpu.SemaphoreType.DMA((1 + FANOUT,))
]


class Lists:
    def __init__(self, backwards, order, slots, order_at, *rest):
        slots_at, sems = rest[:FANOUT], rest[FANOUT]
        self.order, self.slots = order_at, slots_at
        self.copies = [pltpu.make_async_copy(order, order_at, sems.at[0])]
        for s in range(FANOUT):
            part = slots.at[pl.ds(s * NODES, NODES)]
            self.copies.append(pltpu.make_async_copy(part, slots_at[s], sems.at[1 + s]))
        if backwards:
            self.slots = self.slots[::-1]
            self.copies[1:] = self.copies[:0:-1]
        for copy in self.copies:
            copy.start()

    def visit(self, act, group_of):
        slots, copies = self.slots, self.copies[1:]
        self.copies[0].wait()
        for count in range(1, FANOUT + 1):
            copies[count - 1].wait()
            size = group_of(count)
            first = self.order[NODES + count - 1]
            last = self.order[NODES + count]
            groups = (last - first) // size
            rest = first + groups * size

            @pl.loop(0, groups)
            def _(g, count=count, size=size, first=first):
                at = first + g * size
                act([self.order[at + u] for u in range(size)], count, slots)

            @pl.loop(rest, last)
            def _(at, count=count):
                act([self.order[at]], count, slots)


def clear(ref, at, rows):
    step = 512

    @pl.loop(0, rows // step)
    def _(i):
        ref[pl.ds(at + i * step, step), :] = jnp.zeros((step, F), jnp.float32)


BLOCK = 2048
HUB_PIECES = (1, 1, 2, 4, 8, 8, 8)
PIECES = len(HUB_PIECES)


def forward_kernel(order, slots, features, rim_up, rim_down, *refs):
    pieces, refs = refs[:PIECES], refs[PIECES:]
    small, cotangent, (act, src, base, grads) = refs[:4], refs[4], refs[5:9]
    table, sums, features_at, rims_at, hubs_at, cot_at, act_at, src_at, base_at = refs[9:18]
    small_at, lists_at, (sem_in, sem_out) = refs[18:21], refs[21:-2], refs[-2:]
    counts, weights, bias = small_at
    copies = [
        pltpu.make_async_copy(features, features_at, sem_in.at[0]),
        pltpu.make_async_copy(rim_up, rims_at.at[pl.ds(0, HALO)], sem_in.at[1]),
        pltpu.make_async_copy(rim_down, rims_at.at[pl.ds(HALO, HALO)], sem_in.at[2]),
    ]
    at = 0
    for k, piece in enumerate(pieces):
        rows = HUB_PIECES[k] * HUB
        copies.append(
            pltpu.make_async_copy(piece, hubs_at.at[pl.ds(at, rows)], sem_in.at[3 + k])
        )
        at += rows
    for copy in copies:
        copy.start()
    todo = Lists(False, order, slots, *lists_at)
    cot_copy = pltpu.make_async_copy(cotangent, cot_at, sem_in.at[3 + PIECES])
    cot_copy.start()
    to = (counts, weights.at[pl.ds(0, F)], weights.at[pl.ds(F, F)], bias)
    late = [pltpu.make_async_copy(small[k], to[k], sem_in.at[4 + PIECES + k]) for k in range(4)]
    for copy in late:
        copy.start()
    late.append(cot_copy)
    grads[...] = jnp.zeros_like(grads)
    self_at = pl.multiple_of(lax.axis_index("core") * HALF, 8)
    neigh_at = pl.multiple_of((1 - lax.axis_index("core")) * HALF, 8)

    def widen(source, start, at, rows):
        step = 256

        @pl.loop(0, rows // step)
        def _(i):
            table[pl.ds(at + i * step, step), :] = source[
                pl.ds(start + i * step, step), :
            ].astype(jnp.float32)

    copies[0].wait()
    widen(features_at, 0, OWN, NODES)
    for half in range(2):
        copies[1 + half].wait()
        widen(rims_at, half * HALO, pl.multiple_of(faces_up(half) * UPPER, HALO), HALO)
    y, x, core = lax.axis_index("y"), lax.axis_index("x"), lax.axis_index("core")
    position = 0
    for k in range(PIECES):
        copies[3 + k].wait()
        for _ in range(HUB_PIECES[k]):
            b = [(position >> k) & 1 for k in range(5)]
            owner_y = y ^ (b[0] * 1) ^ (b[1] * 3)
            owner_x = x ^ (b[2] * 1) ^ (b[3] * 3)
            owner = owner_y * 8 + owner_x * 2 + (core ^ b[4])
            table[pl.ds(HUB_AT + owner * HUB, HUB), :] = hubs_at[
                position * HUB : (position + 1) * HUB, :
            ].astype(jnp.float32)
            position += 1

    def gather(nodes, count, slots):
        for n in nodes:
            total = table[pl.ds(slots[0][n], 1), :]
            for s in range(1, count):
                total = total + table[pl.ds(slots[s][n], 1), :]
            sums[pl.ds(n, 1), :] = total

    todo.visit(gather, wide_group_of)
    for copy in late:
        copy.wait()

    @pl.loop(0, NODES // BLOCK)
    def _(i):
        cut = pl.ds(i * BLOCK, BLOCK)
        parts = []
        for k in range(BLOCK // LANES):
            row = counts[pl.ds(i * (BLOCK // LANES) + k, 1), :].astype(jnp.float32)
            parts.append(jnp.broadcast_to(row, (LANES, LANES)).T)
        divisor = jnp.concatenate(parts, axis=0)
        agg = (sums[cut, :] / divisor).astype(jnp.bfloat16)
        both = jnp.concatenate([features_at[cut, :], agg], axis=1)
        z = jnp.dot(both, weights[...], preferred_element_type=jnp.float32) + bias[...]
        scale = 0.7978845608028654
        cubic = 0.044715 * scale
        squared = z * z
        t = jnp.tanh(z * (scale + cubic * squared))
        half = 0.5 * z
        rest = half * t
        act_at[cut, :] = (half + rest).astype(jnp.bfloat16)
        slope = (0.5 + 0.5 * t) + (half - rest * t) * (scale + 3 * cubic * squared)
        dz = (cot_at[cut, :].astype(jnp.float32) * slope).astype(jnp.bfloat16)
        products = lax.dot_general(
            both, dz, (((0,), (0,)), ((), ())), preferred_element_type=jnp.float32
        )
        grads[pl.ds(self_at, F), :] += products[:F]
        grads[pl.ds(neigh_at, F), :] += products[F:]
        grads[pl.ds(self_at + F, 8), :] += jnp.sum(
            dz.astype(jnp.float32).reshape(BLOCK // 8, 8, H), axis=0
        )
        back = lax.dot_general(
            dz, weights[...], (((1,), (1,)), ((), ())), preferred_element_type=jnp.float32
        )
        base_at[cut, :] = back[:, :F]
        src_at[cut, :] = back[:, F:] / divisor
        for k, (here, there) in enumerate(((act_at, act), (src_at, src), (base_at, base))):
            pltpu.make_async_copy(here.at[cut], there.at[cut], sem_out.at[k]).start()

    for k, (here, there) in enumerate(((act_at, act), (src_at, src), (base_at, base))):
        pltpu.make_async_copy(here, there, sem_out.at[k]).wait()


def forward(lists, features, rims, hubs, counts, w_self, w_neigh, bias, cot):
    return pl.pallas_call(
        forward_kernel,
        out_shape=(
            jax.ShapeDtypeStruct((NODES, H), jnp.bfloat16),
            jax.ShapeDtypeStruct((NODES, F), jnp.float32),
            jax.ShapeDtypeStruct((NODES, F), jnp.float32),
            jax.ShapeDtypeStruct((2 * HALF, H), jnp.float32),
        ),
        in_specs=list_specs + [hbm] * (3 + len(hubs)) + [hbm] * 5,
        out_specs=(hbm, hbm, hbm, vmem),
        scratch_shapes=[
            pltpu.VMEM((EXTENT, F), jnp.float32),
            pltpu.VMEM((NODES, F), jnp.float32),
            pltpu.VMEM((NODES, F), jnp.bfloat16),
            pltpu.VMEM((2 * HALO, F), jnp.bfloat16),
            pltpu.VMEM((HUBS, F), jnp.bfloat16),
            pltpu.VMEM((NODES, H), jnp.bfloat16),
            pltpu.VMEM((NODES, H), jnp.bfloat16),
            pltpu.VMEM((NODES, F), jnp.float32),
            pltpu.VMEM((NODES, F), jnp.float32),
            pltpu.VMEM((ROWS, LANES), jnp.int32),
            pltpu.VMEM((2 * F, H), jnp.bfloat16),
            pltpu.VMEM((1, H), jnp.float32),
        ]
        + list_scratch
        + [pltpu.SemaphoreType.DMA((8 + PIECES,)), pltpu.SemaphoreType.DMA((3,))],
        compiler_params=params,
        cost_estimate=cost(30),
        name="forward",
    )(*lists, features, *rims, *hubs, counts, w_self, w_neigh, bias, cot)


def chain_sum(chains, cut):
    out = chains[0][cut, :]
    for chain in chains[1:]:
        out = out + chain[cut, :]
    return out


def scatter_kernel(kind, order, slots, src, *refs):
    if kind == "own":
        base, refs = refs[0], refs[1:]
    parts = {"own": 1, "rim": 2, "hub": 4}[kind]
    outs, refs = refs[:parts], refs[parts:]
    lists_at, (src_at, out_at, sems), chains = refs[: FANOUT + 2], refs[FANOUT + 2 : FANOUT + 5], refs[
        FANOUT + 5 :
    ]
    todo = Lists(kind == "rim", order, slots, *lists_at)
    src_copy = pltpu.make_async_copy(src, src_at, sems.at[0])
    src_copy.start()
    rows = out_at.shape[0]
    if kind == "own":
        base_copy = pltpu.make_async_copy(base, chains[0], sems.at[1])
        base_copy.start()
    for chain in chains[1 if kind == "own" else 0 :]:
        clear(chain, 0, rows)
    if kind == "own":
        base_copy.wait()
    src_copy.wait()

    def scatter(nodes, count, slots):
        turn = 0
        for n in nodes:
            row = src_at[pl.ds(n, 1), :]
            for s in range(count):
                chain = chains[turn % len(chains)]
                turn += 1
                at = pl.ds(slots[s][n], 1)
                chain[at, :] = chain[at, :] + row

    todo.visit(scatter, group_of)

    part = rows // len(outs)
    for half, out in enumerate(outs):

        @pl.loop(0, part // HUB)
        def _(i, half=half, out=out):
            if kind == "hub":
                j = i + (half & 1) * (COLS // 4)
                flip_x, flip_y = (j >> 2) ^ (j >> 3), (j & 3) ^ ((j >> 1) & 1)
                owner_y = lax.axis_index("y") ^ flip_y
                owner_x = lax.axis_index("x") ^ flip_x
                taken = owner_y * 8 + owner_x * 2 + (lax.axis_index("core") ^ (half >> 1))
            elif kind == "rim":
                taken = i + faces_up(half) * (HALO // HUB)
            else:
                taken = i
            to = pl.ds(i * HUB, HUB)
            at = pl.ds(half * part + i * HUB, HUB)
            out_at[at, :] = chain_sum(chains, pl.ds(taken * HUB, HUB)).astype(out_at.dtype)
            pltpu.make_async_copy(out_at.at[at], out.at[to], sems.at[2 + half]).start()

    for half, out in enumerate(outs):
        at = pl.ds(half * part, part)
        pltpu.make_async_copy(out_at.at[at], out, sems.at[2 + half]).wait()


def scatter(kind, rows, dtype, us, chains, lists, *inputs):
    parts = {"own": 1, "rim": 2, "hub": 4}[kind]
    return pl.pallas_call(
        functools.partial(scatter_kernel, kind),
        out_shape=(jax.ShapeDtypeStruct((rows // parts, F), dtype),) * parts,
        in_specs=list_specs + [hbm] * len(inputs),
        out_specs=(hbm,) * parts,
        scratch_shapes=list_scratch
        + [
            pltpu.VMEM((NODES, F), jnp.float32),
            pltpu.VMEM((rows, F), dtype),
            pltpu.SemaphoreType.DMA((6,)),
        ]
        + [pltpu.VMEM((rows, F), jnp.float32)] * chains,
        compiler_params=params,
        cost_estimate=cost(us),
        name=kind + "_scatter",
    )(*lists, *inputs)


def finish_kernel(hub_rows, own, rim_0, rim_1, share, out, total, rims, share_at, out_at, rows, sems):
    to = (total, rims.at[pl.ds(0, HALO)], rims.at[pl.ds(HALO, HALO)], share_at, rows)
    copies = [
        pltpu.make_async_copy(source, to[k], sems.at[k])
        for k, source in enumerate((own, rim_0, rim_1, share, hub_rows))
    ]
    for copy in copies:
        copy.start()
    for copy in copies:
        copy.wait()
    step = 256
    for half in range(2):
        start = pl.multiple_of(faces_up(half) * (NODES - HALO), HALO)

        @pl.loop(0, HALO // step)
        def _(i, half=half, start=start):
            cut = pl.ds(start + i * step, step)
            rim = rims[pl.ds(half * HALO + i * step, step), :]
            total[cut, :] = total[cut, :] + rim.astype(jnp.float32)

    @pl.loop(0, HUB // 16)
    def _(i):
        for u in range(16):
            at = pl.ds(rows[i * 16 + u], 1)
            total[at, :] = total[at, :] + share_at[pl.ds(i * 16 + u, 1), :]

    @pl.loop(0, NODES // 512)
    def _(i):
        cut = pl.ds(i * 512, 512)
        out_at[cut, :] = total[cut, :].astype(jnp.bfloat16)
        pltpu.make_async_copy(out_at.at[cut], out.at[cut], sems.at[5]).start()

    pltpu.make_async_copy(out_at, out, sems.at[5]).wait()


def finish(hub_rows, own, rim_0, rim_1, share):
    return pl.pallas_call(
        finish_kernel,
        out_shape=jax.ShapeDtypeStruct((NODES, F), jnp.bfloat16),
        in_specs=[anywhere] * 5,
        out_specs=hbm,
        scratch_shapes=[
            pltpu.VMEM((NODES, F), jnp.float32),
            pltpu.VMEM((2 * HALO, F), jnp.bfloat16),
            pltpu.VMEM((HUB, F), jnp.float32),
            pltpu.VMEM((NODES, F), jnp.bfloat16),
            pltpu.SMEM((HUB,), jnp.int32),
            pltpu.SemaphoreType.DMA((6,)),
        ],
        compiler_params=pltpu.CompilerParams(vmem_limit_bytes=16 * 2**20),
        cost_estimate=cost(3),
        name="finish",
    )(hub_rows, own, rim_0, rim_1, share)


def hand_out_kernel(mine, other, grad_self, grad_neigh, grad_bias):
    first = lax.axis_index("core") == 0
    grad_self[...] = jnp.where(first, mine[0:F, :], other[0:F, :])
    grad_neigh[...] = jnp.where(first, other[0:F, :], mine[0:F, :])
    bias = jnp.where(first, mine[F:HALF, :], other[F:HALF, :])
    grad_bias[...] = jnp.sum(bias, axis=0, keepdims=True)


def hand_out(mine, other):
    return pl.pallas_call(
        hand_out_kernel,
        out_shape=(jax.ShapeDtypeStruct((F, H), jnp.float32),) * 2
        + (jax.ShapeDtypeStruct((1, H), jnp.float32),),
        in_specs=[vmem] * 2,
        out_specs=(vmem,) * 3,
        compiler_params=pltpu.CompilerParams(vmem_limit_bytes=8 * 2**20),
        cost_estimate=cost(1),
        name="hand_out",
    )(mine, other)


def swap(value, axis, flip):
    count = lax.axis_size(axis)
    return lax.ppermute(value, axis, [(i, i ^ flip) for i in range(count)])


def swap_rims(first, second):
    above = lax.ppermute(first, "z", [(0, 1), (1, 0), (2, 3), (3, 2)])
    return above, lax.ppermute(second, "z", [(1, 2), (2, 1)])


def halves(value):
    rows = value.shape[0] // 2
    return value[:rows], value[rows:]


def give_half(parts, axis, flip):
    rows = min(part.shape[0] for part in parts)
    return swap(add_up(parts, rows // 2, rows).astype(jnp.bfloat16), axis, flip)


def add_up(parts, start, stop):
    total = parts[0][start:stop].astype(jnp.float32)
    for part in parts[1:]:
        total = total + part[start:stop].astype(jnp.float32)
    return total


def tie(*values):
    return lax.optimization_barrier(values)


def on_device(features, neighbors, counts, hub_rows, w_self, w_neigh, out_bias, cotangent):
    counts = counts.reshape(ROWS, LANES)

    h0 = pick_hubs(hub_rows, features)
    h1 = swap(h0, "y", 1)
    flat, order = plan(all_plan_kernel, (tiles, ordered), 4, neighbors.T, counts)
    all_lists = lists(order, flat)
    h1, flat = tie(h1, flat)
    held = jnp.concatenate([h0, h1], axis=0)
    h2 = swap(held, "y", 3)
    slots, order = plan(hub_plan_kernel, (tiles, ordered), 4, flat, counts)
    hub_lists = lists(order, slots)
    h2, flat, edges, *hub_lists = tie(h2, flat, features, *hub_lists)
    held = jnp.concatenate([held, h2], axis=0)
    h3 = swap(held, "x", 1)
    rims = swap_rims(*(
        lax.dynamic_slice_in_dim(edges, faces_up(half) * (NODES - HALO), HALO, axis=0)
        for half in range(2)
    ))
    h3, flat = tie(h3, flat)
    held = jnp.concatenate([held, h3], axis=0)
    h4 = swap(held, "x", 3)
    slots, order, own_order = plan(rim_plan_kernel, (tiles, ordered, ordered), 5, flat, counts)
    rim_lists = lists(order, slots)
    own_lists = lists(own_order, slots)
    h5 = swap(held, "core", 1)
    h4, h5, rim_lists, own_lists, *rims = tie(h4, h5, rim_lists, own_lists, *rims)
    h6 = swap(h4, "core", 1)

    act, src, base, grads = forward(
        all_lists, features, rims, (h0, h1, h2, h3, h4, h5, h6), counts,
        w_self, w_neigh, out_bias.reshape(1, H), cotangent,
    )

    other = swap(grads, "z", 1)
    keep, keep_far, give, give_far = scatter("hub", HUBS, jnp.bfloat16, 8, 6, hub_lists, src)
    keep, keep_far, give, give_far, src, other = tie(keep, keep_far, give, give_far, src, other)
    grads = grads + other
    far = [keep_far, swap(give_far, "core", 1)]
    other = swap(grads, "z", 3)
    far, src, give = tie(far, src, give)
    got = swap(add_up(far, 0, far[0].shape[0]).astype(jnp.bfloat16), "x", 3)
    parts = [keep, swap(give, "core", 1)]
    rims = scatter("rim", 2 * HALO, jnp.bfloat16, 8, 6, rim_lists, src)
    parts, src, other, rims = tie(parts + [got], src, other, rims)

    grads, give = halves(grads + other)
    other = swap(give, "core", 1)
    got = give_half(parts, "x", 1)
    other, src = tie(other, src)
    grads = grads + other
    others = [swap(grads, "x", flip) for flip in (1, 3, 2)]
    (own,) = scatter("own", NODES, jnp.float32, 20, 12, own_lists, src, base)
    parts, others, own, rims = tie(parts + [got], others, own, rims)

    grads = (grads + others[0]) + (others[1] + others[2])
    got = give_half(parts, "y", 3)
    other = swap(grads, "y", 1)
    rims = swap_rims(*rims)
    parts, other = tie(parts + [got], other)
    got = give_half(parts, "y", 1)
    grads = grads + other
    other = swap(grads, "y", 3)
    parts, other, rims = tie(parts + [got], other, rims)
    grads = grads + other
    other = swap(grads, "core", 1)
    grad_features = finish(hub_rows, own, *rims, add_up(parts, 0, HUB))
    other, grad_features = tie(other, grad_features)
    grad_self, grad_neigh, grad_bias = hand_out(grads, other)
    return act, grad_features, grad_self, grad_neigh, grad_bias.reshape(H)


def solution(mesh):
    mesh = Mesh(mesh.devices.reshape(4, 4, 4, 2), AXES)
    rows = P(AXES, None)
    placed = (rows, rows, P(AXES), P(AXES), P(), P(), P(), rows)
    return jax.shard_map(
        on_device,
        mesh=mesh,
        in_specs=placed,
        out_specs=(rows, rows, P(), P(), P()),
        check_vma=False,
    )
```
